128 devices in a mesh: rep: 2 (over z_hi), section: 8 (over x, core), tp: 8 (over y, z_lo).
Axes of the slice: x: 4, y: 4, z: 4 (z_hi: 2, z_lo: 2; z = z_hi * 2 + z_lo), core: 2. Of those that a mesh axis runs over, the one named last changes fastest.
Arguments:
- section_map: int32 [2, 8], replicated, may hold values from 0 to 7, as said below
- checkpoint: bfloat16 [2, 8, 2, 64, 4096], P('rep', 'section'), may hold values from -6 to 6
- top_grad: bfloat16 [2, 2, 64, 4096], P('rep'), may hold values from -6 to 6
- value_weight: bfloat16 [2, 16, 4096, 4096], P('rep', 'section', None, 'tp'), may hold values from -0.09375 to 0.09375
- out_weight: bfloat16 [2, 16, 4096, 4096], P('rep', 'section', None, 'tp'), may hold values from -0.09375 to 0.09375
Outputs:
- value_grad: bfloat16 [8, 4096, 4096], P(None, ('rep', 'section'), 'tp')
- out_grad: bfloat16 [8, 4096, 4096], P(None, ('rep', 'section'), 'tp')
The draws below stay inside these ranges and needn't reach their ends.
Inputs may be any that keep to these rules, and one draw needn't show every extreme that they name: `section_map`: row r lists the section of each layer for replica r; entries never fall along a row; a section holds at most 2 layers and may hold none.
All inputs are finite; a program needn't handle non-finite values.
Results may differ from the reference program's by a relative error of at most 0.035.
Values may be sent and summed in bfloat16 or wider, within the bound.
No kernel may reach another device: no remote copies, remote signals or barrier semaphores. Data moves between devices by JAX's collectives and lax.ppermute only.
A program may use at most 192 MiB of HBM per device.

```python
import jax
import jax.numpy as jnp
from jax import lax

D = 4096
HW = 4096
TOK = 64
MB = 2
SLOTS = 2
LAYERS = 8
N_REP = 2
N_SECTION = 8
N_TP = 8


def draw_section_map(key, part):
    key = jax.random.fold_in(key, 7)
    table_rows = []
    for replica in range(N_REP):
        replica_key = jax.random.fold_in(key, replica)
        ordering = jax.random.permutation(replica_key, N_SECTION)
        position = jnp.argsort(ordering).astype(jnp.int32)
        spared = replica * N_SECTION // 4
        counts = jnp.where(position < spared, 0, jnp.where(position < 2 * spared, 2, 1)).astype(jnp.int32)
        boundary = jnp.cumsum(counts).astype(jnp.int32)
        layer_ids = jnp.arange(N_SECTION, dtype=jnp.int32)
        table_rows.append(jnp.sum((boundary[None, :] <= layer_ids[:, None]).astype(jnp.int32), axis=1))
    return jnp.stack(table_rows).astype(jnp.int32)


def block_scale(rng, shape, pieces, low, largest):
    def one(dim, parts):
        heights = jax.random.uniform(jax.random.fold_in(jax.random.fold_in(rng, 6), dim), (parts,), jnp.float32, low / len(pieces), largest / len(pieces))
        return jnp.repeat(jnp.exp(heights), shape[dim] // parts).reshape((-1,) + (1,) * (len(shape) - dim - 1))

    gain = one(*pieces[0])
    for cut in pieces[1:]:
        gain = gain * one(*cut)
    return gain


def bell_draw(stream_key, extent, width, reach, pieces=(), kind=jnp.bfloat16):
    values = jax.random.normal(stream_key, extent, jnp.float32) * width
    if len(pieces) > 0:
        values = block_scale(stream_key, extent, pieces, -0.22, 0.18) * values
    return jnp.clip(values, min=-reach, max=reach).astype(kind)


def setup_inputs(seed: int = 0) -> dict:
    arg_keys = jax.random.split(jax.random.key(seed), 6)
    return {
        "section_map": draw_section_map(jax.random.fold_in(arg_keys[5], 71), 0),
        "checkpoint": bell_draw(arg_keys[1], (N_REP, N_SECTION, MB, TOK, D), 1.0, 6.0, ((0, 2), (1, 8))),
        "top_grad": bell_draw(arg_keys[2], (N_REP, MB, TOK, D), 1.0, 6.0, ((0, 2),)),
        "value_weight": bell_draw(arg_keys[3], (N_REP, N_SECTION * SLOTS, D, HW), D ** -0.5, 0.09375, ((0, 2), (1, 8), (3, 8))),
        "out_weight": bell_draw(arg_keys[4], (N_REP, N_SECTION * SLOTS, D, HW), HW ** -0.5, 0.09375, ((0, 2), (1, 8), (3, 8))),
    }


def silu_slope(preact):
    sigma = jax.nn.sigmoid(preact)
    return sigma * (1.0 + preact * (1.0 - sigma))


def head_groups(left, right):
    row_count = left.shape[0]
    group_width = right.shape[1] // N_TP
    lhs = left.reshape(row_count, N_TP, group_width).astype(jnp.float32)
    rhs = right.reshape(right.shape[0], N_TP, group_width).astype(jnp.float32)
    partial_sums = jnp.einsum("rgh,dgh->grd", lhs, rhs, precision=lax.Precision.HIGHEST)
    rounded = lax.optimization_barrier(partial_sums.astype(jnp.bfloat16))
    return jnp.sum(rounded.astype(jnp.float32), axis=0)


def reference(section_map, checkpoint, top_grad, value_weight, out_weight):
    row_count = MB * TOK
    total_value = jnp.zeros((LAYERS, D, HW), jnp.float32)
    total_out = jnp.zeros((LAYERS, D, HW), jnp.float32)
    for replica in range(N_REP):
        own_map = section_map[replica]
        upstream = top_grad[replica].reshape(row_count, D)
        for section_index in reversed(range(N_SECTION)):
            section_count = jnp.sum((own_map == section_index).astype(jnp.int32))
            first_layer = jnp.sum((own_map < section_index).astype(jnp.int32))
            current = checkpoint[replica, section_index].reshape(row_count, D)
            saved_slots = []
            for slot_index in range(SLOTS):
                is_valid = slot_index < section_count
                w_value = value_weight[replica, section_index * SLOTS + slot_index]
                w_out = out_weight[replica, section_index * SLOTS + slot_index]
                preact = jnp.dot(current, w_value, preferred_element_type=jnp.float32)
                activated = jax.nn.silu(preact).astype(jnp.bfloat16)
                saved_slots.append((current, preact, activated, is_valid, w_value, w_out))
                advanced = (current.astype(jnp.float32) + head_groups(activated, w_out)).astype(jnp.bfloat16)
                current = jnp.where(is_valid, advanced, current)
            for slot_index in reversed(range(SLOTS)):
                slot_input, preact, activated, is_valid, w_value, w_out = saved_slots[slot_index]
                act_grad = jnp.dot(upstream, w_out, preferred_element_type=jnp.float32)
                head_grad = (act_grad * silu_slope(preact)).astype(jnp.bfloat16)
                slot_out = jnp.dot(upstream.T, activated, preferred_element_type=jnp.float32).astype(jnp.bfloat16)
                slot_value = jnp.dot(slot_input.T, head_grad, preferred_element_type=jnp.float32).astype(jnp.bfloat16)
                layer_slot = jnp.minimum(first_layer + slot_index, LAYERS - 1).astype(jnp.int32)
                keep_flag = is_valid.astype(jnp.float32)
                total_value = total_value.at[layer_slot].add(keep_flag * slot_value.astype(jnp.float32))
                total_out = total_out.at[layer_slot].add(keep_flag * slot_out.astype(jnp.float32))
                advanced = (upstream.astype(jnp.float32) + head_groups(head_grad, w_value)).astype(jnp.bfloat16)
                upstream = jnp.where(is_valid, advanced, upstream)
    return total_value.astype(jnp.bfloat16), total_out.astype(jnp.bfloat16)
```

```python
import functools

import jax
import jax.numpy as jnp
from jax import lax
from jax.experimental import pallas as pl
from jax.experimental.pallas import tpu as pltpu
from jax.sharding import PartitionSpec as P

BF16 = jnp.bfloat16
F32 = jnp.float32
VMEM_BYTES = 48 * 1024 * 1024
NT = (((1,), (1,)), ((), ()))
TN = (((0,), (0,)), ((), ()))


def silu_slope(preact):
    sigma = jax.nn.sigmoid(preact)
    return sigma * (1.0 + preact * (1.0 - sigma))


def weight_copies(pick_ref, own, sibling, buffer, sems, chunks):
    step = buffer.shape[0] // chunks
    slot = pick_ref[1]

    def begin(source):
        for i in range(chunks):
            rows = pl.ds(i * step, step)
            pltpu.make_async_copy(source.at[slot, rows], buffer.at[rows], sems.at[i]).start()

    if sibling is None:
        begin(own)
    else:
        pl.when(pick_ref[0] == 1)(lambda: begin(own))
        pl.when(pick_ref[0] == 0)(lambda: begin(sibling))

    def wait(i):
        rows = pl.ds(i * step, step)
        pltpu.make_async_copy(own.at[slot, rows], buffer.at[rows], sems.at[i]).wait()

    return wait


def first_product(rows_ref, buffer, wait, chunks):
    step = buffer.shape[0] // chunks
    total = None
    for i in range(chunks):
        wait(i)
        part = jnp.dot(rows_ref[i], buffer[i * step : (i + 1) * step, :], preferred_element_type=F32)
        total = part if total is None else total + part
    return total


def second_product(rows, buffer, wait, chunks, out_ref):
    step = buffer.shape[0] // chunks
    for i in range(chunks):
        wait(i)
        part = lax.dot_general(rows, buffer[i * step : (i + 1) * step, :], NT, preferred_element_type=F32)
        out_ref[i] = part.astype(BF16)


def forward_kernel(chunks, pick_ref, x_ref, v_ref, o_ref, part_ref, act_ref, slope_ref, vbuf, obuf, vsem, osem):
    wait_v = weight_copies(pick_ref, v_ref, None, vbuf, vsem, chunks)
    wait_o = weight_copies(pick_ref, o_ref, None, obuf, osem, chunks)
    pre = first_product(x_ref, vbuf, wait_v, chunks)
    act = jax.nn.silu(pre).astype(BF16)
    act_ref[...] = act
    slope_ref[...] = silu_slope(pre)
    second_product(act, obuf, wait_o, chunks, part_ref)


def last_slot_kernel(chunks, pick_ref, x_ref, v_ref, act_ref, slope_ref, vbuf, vsem):
    wait_v = weight_copies(pick_ref, v_ref, None, vbuf, vsem, chunks)
    pre = first_product(x_ref, vbuf, wait_v, chunks)
    act_ref[...] = jax.nn.silu(pre).astype(BF16)
    slope_ref[...] = silu_slope(pre)


def backward_kernel(
    chunks, pick_ref, g_ref, slope_ref, o_own, o_sib, v_own, v_sib, part_ref, head_ref, obuf, vbuf, osem, vsem
):
    wait_o = weight_copies(pick_ref, o_own, o_sib, obuf, osem, chunks)
    wait_v = weight_copies(pick_ref, v_own, v_sib, vbuf, vsem, chunks)
    act_grad = first_product(g_ref, obuf, wait_o, chunks)
    head = (act_grad * slope_ref[0]).astype(BF16)
    head_ref[...] = head
    second_product(head, vbuf, wait_v, chunks, part_ref)


def last_layer_kernel(chunks, pick_ref, g_ref, slope_ref, o_own, o_sib, head_ref, obuf, osem):
    wait_o = weight_copies(pick_ref, o_own, o_sib, obuf, osem, chunks)
    act_grad = first_product(g_ref, obuf, wait_o, chunks)
    head_ref[...] = (act_grad * slope_ref[0]).astype(BF16)


def call(kernel, pick, operands, specs, outs, weight_shape, weights):
    chunks = operands[0].shape[0]
    flops = 2 * operands[0].shape[1] * weight_shape[0] * weight_shape[1] * weights
    scratch = [pltpu.VMEM(weight_shape, BF16)] * weights + [pltpu.SemaphoreType.DMA((chunks,))] * weights
    return pl.pallas_call(
        functools.partial(kernel, chunks),
        out_shape=outs,
        grid_spec=pltpu.PrefetchScalarGridSpec(
            num_scalar_prefetch=1,
            grid=(1,),
            in_specs=specs,
            out_specs=jax.tree.map(lambda o: pl.BlockSpec(o.shape, lambda i, p, n=len(o.shape): (0,) * n), outs),
            scratch_shapes=scratch,
        ),
        compiler_params=pltpu.CompilerParams(vmem_limit_bytes=VMEM_BYTES),
        cost_estimate=pl.CostEstimate(
            flops=flops, bytes_accessed=weights * weight_shape[0] * weight_shape[1] * 2, transcendentals=0
        ),
    )(pick, *operands)


def whole(array):
    return pl.BlockSpec(array.shape, lambda i, p, n=array.ndim: (0,) * n)


ANY = pl.BlockSpec(memory_space=pl.ANY)


def gradient_kernel(tab_ref, x0, x1, h0, h1, g0, g1, a0, a1, value_ref, out_ref):
    def rows(ref):
        return ref[...].reshape(-1, ref.shape[-1])

    def both(left0, right0, left1, right1):
        left = jnp.concatenate([rows(left0), rows(left1)], axis=0)
        right = jnp.concatenate([rows(right0), rows(right1)], axis=0)
        return lax.dot_general(left, right, TN, preferred_element_type=F32).astype(BF16)

    value_ref[0] = both(x0, h0, x1, h1)
    out_ref[0] = both(g0, a0, g1, a1)


def gradients(section_map, position, slot_of, x_all, head_all, g_all, act_all):
    layers = section_map.shape[1]
    table = jnp.stack([section_map, slot_of, position]).astype(jnp.int32)

    def by_slot(r, array):
        return pl.BlockSpec((1, 1, 1) + array.shape[3:], lambda l, t: (r, t[0, r, l], t[1, r, l], 0, 0))

    def by_window(r, array):
        shape = array.shape
        return pl.BlockSpec(
            (1, 1, shape[2], 1) + shape[4:], lambda l, t: (r, t[0, r, l] // 2, 0, t[2, r, l], 0, 0)
        )

    piece, width = x_all.shape[-1], act_all.shape[-1]
    out = jax.ShapeDtypeStruct((layers, piece, width), BF16)
    out_spec = pl.BlockSpec((1, piece, width), lambda l, t: (l, 0, 0))
    return pl.pallas_call(
        gradient_kernel,
        out_shape=(out, out),
        grid_spec=pltpu.PrefetchScalarGridSpec(
            num_scalar_prefetch=1,
            grid=(layers,),
            in_specs=[by_slot(0, x_all), by_slot(1, x_all), by_window(0, head_all), by_window(1, head_all)]
            + [by_window(0, g_all), by_window(1, g_all), by_slot(0, act_all), by_slot(1, act_all)],
            out_specs=(out_spec, out_spec),
        ),
        compiler_params=pltpu.CompilerParams(vmem_limit_bytes=VMEM_BYTES),
    )(table, x_all, x_all, head_all, head_all, g_all, g_all, act_all, act_all)


def per_device(section_map, checkpoint, top_grad, value_weight, out_weight):
    tp_total = lax.axis_size("tp")
    section_total = lax.axis_size("section")
    replica_total = lax.axis_size("rep")
    owners = replica_total * section_total
    rep, section, tp = (lax.axis_index(name) for name in ("rep", "section", "tp"))
    chip, core = section // 2, section % 2
    layers = section_map.shape[1]
    _, _, micro, tokens, model = checkpoint.shape
    slots, width = value_weight.shape[1], value_weight.shape[3]
    rows = micro * tokens
    cut = model // tp_total
    piece = model // owners
    v_own, o_own = value_weight[0], out_weight[0]
    weight_shape = (model, width)

    layer_ids = jnp.arange(layers, dtype=jnp.int32)
    first_of = jnp.sum(section_map[:, None, :] < section_map[:, :, None], axis=2).astype(jnp.int32)
    slot_of = layer_ids[None] - first_of
    chip_of = section_map // 2
    window = 2 * slots
    chip_first = jnp.sum(chip_of[:, None, :] < jnp.arange(section_total // 2)[None, :, None], axis=2)
    window_first = jnp.minimum(chip_first, layers - window).astype(jnp.int32)
    position = layer_ids[None] - jnp.take_along_axis(window_first, chip_of, axis=1)
    my_map = lax.dynamic_index_in_dim(section_map, rep, 0, keepdims=False)
    my_slot = lax.dynamic_index_in_dim(slot_of, rep, 0, keepdims=False)
    my_window = lax.dynamic_index_in_dim(window_first, rep, 0, keepdims=False)[chip]

    swap = [(i, i ^ 1) for i in range(section_total)]
    o_sib = lax.ppermute(o_own, "section", swap)
    v_sib = lax.ppermute(v_own, "section", swap)

    def by_cut(array):
        return array.reshape(-1, tp_total, cut).transpose(1, 0, 2)

    def reduce_slices(parts, base):
        got = lax.all_to_all(parts, "tp", 0, 0, tiled=True)
        mine = lax.dynamic_index_in_dim(base, tp, 0, keepdims=False)
        return (mine.astype(F32) + jnp.sum(got.astype(F32), axis=0)).astype(BF16)

    def gather_slices(mine):
        spread = jnp.broadcast_to(mine[None], (tp_total,) + mine.shape)
        return lax.all_to_all(spread, "tp", 0, 0, tiled=True)

    x_first = by_cut(checkpoint[0, 0].reshape(rows, model))
    wide = jax.ShapeDtypeStruct((rows, width), F32)
    narrow = jax.ShapeDtypeStruct((rows, width), BF16)
    parts, act_first, slope_first = call(
        forward_kernel,
        jnp.array([1, 0], jnp.int32),
        (x_first, v_own, o_own),
        [whole(x_first), ANY, ANY],
        (jax.ShapeDtypeStruct(x_first.shape, BF16), narrow, wide),
        weight_shape,
        2,
    )
    x_second = gather_slices(reduce_slices(parts, x_first))
    act_second, slope_second = call(
        last_slot_kernel,
        jnp.array([1, 1], jnp.int32),
        (x_second, v_own),
        [whole(x_second), ANY],
        (narrow, wide),
        weight_shape,
        1,
    )
    acts = jnp.stack([act_first, act_second])
    act_all = lax.all_gather(acts, ("rep", "section"), axis=0, tiled=False)
    act_all = act_all.reshape(replica_total, section_total, slots, rows, width)
    xs = jnp.stack([x_first, x_second]).reshape(slots, tp_total, rows, 2, piece)
    x_all = lax.all_to_all(
        xs.transpose(1, 3, 0, 2, 4).reshape(owners, slots, rows, piece), ("rep", "section"), 0, 0, tiled=True
    ).reshape(replica_total, section_total, slots, rows, piece)

    slopes = jnp.stack([slope_first, slope_second]).reshape(slots, 2, tokens, width)
    slopes_own = lax.dynamic_index_in_dim(slopes, core, 1, keepdims=False)
    slopes_sib = lax.ppermute(lax.dynamic_index_in_dim(slopes, 1 - core, 1, keepdims=False), "section", swap)
    slope_all = jnp.concatenate([slopes_own, slopes_sib])

    g = by_cut(lax.dynamic_index_in_dim(top_grad[0], core, 0, keepdims=False))
    down = [(i, i - 2) for i in range(2, section_total)]
    g_at, head_at = [None] * layers, [None] * layers
    for layer in reversed(range(layers)):
        own = (my_map[layer] % 2 == core).astype(jnp.int32)
        pick = jnp.stack([own, my_slot[layer]])
        slope_spec = pl.BlockSpec((1, tokens, width), lambda i, p: ((1 - p[0]) * slots + p[1], 0, 0))
        g_at[layer] = g
        head_shape = jax.ShapeDtypeStruct((tokens, width), BF16)
        if layer == 0:
            (head_at[layer],) = call(
                last_layer_kernel,
                pick,
                (g, slope_all, o_own, o_sib),
                [whole(g), slope_spec, ANY, ANY],
                (head_shape,),
                weight_shape,
                1,
            )
            break
        parts, head_at[layer] = call(
            backward_kernel,
            pick,
            (g, slope_all, o_own, o_sib, v_own, v_sib),
            [whole(g), slope_spec, ANY, ANY, ANY, ANY],
            (jax.ShapeDtypeStruct(g.shape, BF16), head_shape),
            weight_shape,
            2,
        )
        mine = reduce_slices(parts, g)
        distance = chip_of[:, layer] - chip_of[:, layer - 1]
        my_distance = lax.dynamic_index_in_dim(distance, rep, 0, keepdims=False)

        def hop(i, value, my_distance=my_distance):
            came = lax.ppermute(value, "section", down)
            return jnp.where(i < my_distance, came, value)

        mine = lax.fori_loop(0, jnp.max(distance), hop, mine)
        g = gather_slices(mine)

    g_window = lax.dynamic_slice_in_dim(jnp.stack(g_at), my_window, window, 0)
    head_window = lax.dynamic_slice_in_dim(jnp.stack(head_at), my_window, window, 0)
    g_send = g_window.reshape(window, tp_total, tokens, 2, piece).transpose(1, 3, 0, 2, 4)
    g_all = lax.all_to_all(g_send.reshape(owners, window, tokens, piece), ("rep", "section"), 0, 0, tiled=True)
    head_send = jnp.broadcast_to(head_window[None], (owners,) + head_window.shape)
    head_all = lax.all_to_all(head_send, ("rep", "section"), 0, 0, tiled=True)
    by_chip = (replica_total, section_total // 2, 2, window, tokens)
    return gradients(
        section_map,
        position,
        slot_of,
        x_all,
        head_all.reshape(by_chip + (width,)),
        g_all.reshape(by_chip + (piece,)),
        act_all,
    )


def solution(mesh):
    placed = (
        P(),
        P("rep", "section", None, None, None),
        P("rep", None, None, None),
        P("rep", "section", None, "tp"),
        P("rep", "section", None, "tp"),
    )
    return jax.shard_map(
        per_device,
        mesh=mesh,
        in_specs=placed,
        out_specs=(P(None, ("rep", "section"), "tp"), P(None, ("rep", "section"), "tp")),
        check_vma=False,
    )
```

```python
import functools

import jax
import jax.numpy as jnp
from jax import lax
from jax.experimental import pallas as pl
from jax.experimental.pallas import tpu as pltpu
from jax.sharding import PartitionSpec as P

BF16 = jnp.bfloat16
F32 = jnp.float32
VMEM_BYTES = 48 * 1024 * 1024
NT = (((1,), (1,)), ((), ()))
TN = (((0,), (0,)), ((), ()))
ANY = pl.BlockSpec(memory_space=pl.ANY)
HBM = pl.BlockSpec(memory_space=pltpu.HBM)
SMEM = pl.BlockSpec(memory_space=pltpu.SMEM)
VMEM = pl.BlockSpec(memory_space=pltpu.VMEM)


def silu_slope(preact):
    sigma = jax.nn.sigmoid(preact)
    return sigma * (1.0 + preact * (1.0 - sigma))


def run(kernel, operands, specs, outs, out_specs, scratch, bytes_moved, flops=0):
    return pl.pallas_call(
        kernel,
        out_shape=outs,
        in_specs=specs,
        out_specs=out_specs,
        scratch_shapes=scratch,
        compiler_params=pltpu.CompilerParams(vmem_limit_bytes=VMEM_BYTES),
        cost_estimate=pl.CostEstimate(flops=flops, bytes_accessed=bytes_moved, transcendentals=0),
    )(*operands)


class Feed:
    def __init__(self, sources, buffer, sems, chunks):
        self.last = sources[-1][1]
        self.buffer, self.sems = buffer, sems
        for condition, place in sources:

            def begin(place=place):
                for i in range(chunks):
                    pltpu.make_async_copy(place(i), buffer.at[i], sems.at[i]).start()

            if condition is None:
                begin()
            else:
                pl.when(condition)(begin)

    def take(self, i):
        pltpu.make_async_copy(self.last(i), self.buffer.at[i], self.sems.at[i]).wait()
        return self.buffer[i]


def weight_places(scalars, refs, cut):
    slot = scalars[1]

    def place(ref):
        return lambda i: ref.at[slot, pl.ds(i * cut, cut)]

    if len(refs) == 1:
        return [(None, place(refs[0]))]
    return [(scalars[0] == 1, place(refs[0])), (scalars[0] == 0, place(refs[1]))]


def rows_place(ref, core, cut):
    if ref.shape[-1] == cut:
        return lambda i: ref.at[i]
    if len(ref.shape) == 2:
        return lambda i: ref.at[:, pl.ds(i * cut, cut)]
    return lambda i: ref.at[core, :, pl.ds(i * cut, cut)]


def dot_in(rows, weight, chunks):
    total = None
    for i in range(chunks):
        part = jnp.dot(rows.take(i), weight.take(i), preferred_element_type=F32)
        total = part if total is None else total + part
    return total


def dot_out(rows, weight, chunks, stage, part_ref, sems):
    copies = []
    for i in range(chunks):
        stage[i] = lax.dot_general(rows, weight.take(i), NT, preferred_element_type=F32).astype(BF16)
        copies.append(pltpu.make_async_copy(stage.at[i], part_ref.at[i], sems.at[i]))
        copies[-1].start()
    return copies


def recompute(chunks, with_parts, scalars, x_ref, v_ref, *refs):
    o_ref, refs = (refs[0], refs[1:]) if with_parts else (None, refs)
    part_ref, refs = (refs[0], refs[1:]) if with_parts else (None, refs)
    act_mine, act_other, slope_mine, slope_other, xbuf, vbuf, act_rows, slope_rows, xsem, vsem = refs[:10]
    cut = vbuf.shape[1]
    core = scalars[2]
    x = Feed([(None, rows_place(x_ref, core, cut))], xbuf, xsem, chunks)
    v = Feed(weight_places(scalars, [v_ref], cut), vbuf, vsem, chunks)
    if with_parts:
        obuf, stage, osem, psem = refs[10:]
        o = Feed(weight_places(scalars, [o_ref], cut), obuf, osem, chunks)
    pre = dot_in(x, v, chunks)
    act = jax.nn.silu(pre).astype(BF16)
    copies = dot_out(act, o, chunks, stage, part_ref, psem) if with_parts else []
    act_rows[...] = act
    slope_rows[...] = silu_slope(pre)
    half = act_mine.shape[0]
    mine = pl.ds(pl.multiple_of(core * half, half), half)
    other = pl.ds(pl.multiple_of((1 - core) * half, half), half)
    act_mine[...] = act_rows[mine, :]
    act_other[...] = act_rows[other, :]
    slope_mine[...] = slope_rows[mine, :]
    slope_other[...] = slope_rows[other, :]
    for copy in copies:
        copy.wait()


def step(chunks, with_parts, deps, scalars, g_ref, *refs):
    slopes, refs = refs[:4], refs[4:]
    o_refs, refs = refs[:2], refs[2:]
    if with_parts:
        v_refs, refs = refs[:2], refs[2:]
    refs = refs[deps:]
    if with_parts:
        part_ref, refs = refs[0], refs[1:]
    head_ref, gbuf, sbuf, obuf, head_rows, gsem, ssem, osem, hsem = refs[:9]
    cut = obuf.shape[1]
    g = Feed([(None, rows_place(g_ref, scalars[2], cut))], gbuf, gsem, chunks)
    o = Feed(weight_places(scalars, o_refs, cut), obuf, osem, chunks)
    which = (1 - scalars[0]) * 2 + scalars[1]
    slope = Feed([(which == j, lambda i, ref=slopes[j]: ref) for j in range(4)], sbuf, ssem, 1)
    if with_parts:
        vbuf, stage, vsem, psem = refs[9:]
        v = Feed(weight_places(scalars, v_refs, cut), vbuf, vsem, chunks)
    act_grad = dot_in(g, o, chunks)
    head = (act_grad * slope.take(0)).astype(BF16)
    head_rows[...] = head
    out = pltpu.make_async_copy(head_rows, head_ref, hsem.at[0])
    out.start()
    copies = dot_out(head, v, chunks, stage, part_ref, psem) if with_parts else []
    for copy in copies + [out]:
        copy.wait()


def reduce_kernel(scalars, got_ref, base_ref, mine_ref, base, sem):
    cut = base.shape[1]
    place = rows_place(base_ref, scalars[2], cut)(scalars[3])
    copy = pltpu.make_async_copy(place, base, sem.at[0])
    copy.start()
    total = got_ref[0].astype(F32)
    for i in range(1, got_ref.shape[0]):
        total += got_ref[i].astype(F32)
    copy.wait()
    mine_ref[...] = (base[...].astype(F32) + total).astype(BF16)


def carve_kernel(count, scalars, *refs):
    heads, grads, outs, sems = refs[:count], refs[count : 2 * count], refs[2 * count : -1], refs[-1]
    chip, core = scalars[0], scalars[1]
    chips = len(outs)
    copies = []

    def copy(source, target):
        copies.append(pltpu.make_async_copy(source, target, sems.at[len(copies)]))
        copies[-1].start()

    for far, out in enumerate(outs):
        width = out.shape[-1] // 3
        to = lax.rem(chip + far, chips)
        for n in range(count):
            at = scalars[2 + n]
            copy(heads[n], out.at[at, :, pl.ds(0, width)])
            ref = grads[n]
            for replica in range(2):
                cut = replica * chips + to
                if ref.shape[-1] != width:
                    columns = pl.ds(pl.multiple_of(cut * width, width), width)
                    source = ref.at[:, columns] if len(ref.shape) == 2 else ref.at[core, :, columns]
                elif ref.shape[1] == out.shape[1]:
                    source = ref.at[cut]
                else:
                    source = ref.at[cut, pl.ds(pl.multiple_of(core * out.shape[1], out.shape[1]), out.shape[1])]
                copy(source, out.at[at, :, pl.ds((1 + replica) * width, width)])
    for one in copies:
        one.wait()


def pick_kernel(count, scalars, *refs):
    chips = 4
    sources, (own_out, own_here, sib_out, sib_here), sems = refs[:chips], refs[chips : chips + 4], refs[-1]
    core, rep = scalars[0], scalars[1]
    width = sources[0].shape[-1] // 3
    half = width // 2

    def columns(replica, side):
        return pl.ds(pl.multiple_of((1 + replica) * width + side * half, half), half)

    def moves(n, source, at):
        block = source.at[at]
        return [
            (block.at[:, pl.ds(0, width)], own_out.at[n, :, pl.ds(0, width)]),
            (block.at[:, columns(1 - rep, core)], own_out.at[n, :, pl.ds(width, half)]),
            (block.at[:, columns(rep, core)], own_here.at[n]),
            (block.at[:, pl.ds(0, width)], sib_out.at[n, :, pl.ds(0, width)]),
            (block.at[:, columns(1 - rep, 1 - core)], sib_out.at[n, :, pl.ds(width, half)]),
            (block.at[:, columns(rep, 1 - core)], sib_here.at[n]),
        ]

    for n in range(count):
        at = scalars[2 + 2 * n + 1]
        for far in range(chips):

            def begin(n=n, far=far, at=at):
                for k, (a, b) in enumerate(moves(n, sources[far], at)):
                    pltpu.make_async_copy(a, b, sems.at[n, k]).start()

            pl.when(scalars[2 + 2 * n] == far)(begin)
    for n in range(count):
        for k, (a, b) in enumerate(moves(n, sources[0], 0)):
            pltpu.make_async_copy(a, b, sems.at[n, k]).wait()


def gradient_kernel(first, *refs):
    (x0, xa1, x1, xa2, xa3, xa4), (g0, gh1, g1, gh2, gh3, gh4) = refs[:6], refs[6:12]
    value_ref, out_ref = refs[-2:]
    width = value_ref.shape[-1]

    def rows(alone0, with0, alone1, with1, with2, with3):
        narrow = [alone0[0], alone1[0], with2[0][:, width:], with3[0][:, width:]]
        wide = [with0[0][:, :width], with1[0][:, :width], with2[0][:, :width], with3[0][:, :width]]
        return jnp.concatenate(narrow, axis=0), jnp.concatenate(wide, axis=0)

    x, act = rows(x0, xa1, x1, xa2, xa3, xa4)
    g, head = rows(g0, gh1, g1, gh2, gh3, gh4)
    value_ref[0] = lax.dot_general(x, head, TN, preferred_element_type=F32).astype(BF16)
    out_ref[0] = lax.dot_general(g, act, TN, preferred_element_type=F32).astype(BF16)


def gradients(layers, first, count, forward, backward, before):
    piece = forward[0].shape[-1]
    width = forward[1].shape[-1] - piece
    out = jax.ShapeDtypeStruct((layers, piece, width), BF16)
    out_spec = pl.BlockSpec((1, piece, width), lambda l: (first + l, 0, 0))

    def block(array, start):
        return pl.BlockSpec((1,) + array.shape[1:], lambda l: (start + l, 0, 0))

    specs = [block(a, first) for a in forward] + [block(a, 0) for a in backward]
    operands = list(forward) + list(backward)
    aliases = {}
    if before is not None:
        aliases = {len(operands): 0, len(operands) + 1: 1}
        operands, specs = operands + list(before), specs + [ANY, ANY]
    return pl.pallas_call(
        functools.partial(gradient_kernel, first),
        out_shape=(out, out),
        grid=(count,),
        in_specs=specs,
        out_specs=(out_spec, out_spec),
        input_output_aliases=aliases,
        compiler_params=pltpu.CompilerParams(vmem_limit_bytes=VMEM_BYTES),
        cost_estimate=pl.CostEstimate(
            flops=count * 4 * piece * width * 256, bytes_accessed=count * 2400000, transcendentals=0
        ),
    )(*operands)


def per_device(section_map, checkpoint, top_grad, value_weight, out_weight):
    tp_total = lax.axis_size("tp")
    section_total = lax.axis_size("section")
    replica_total = lax.axis_size("rep")
    chips = section_total // 2
    rep, section, tp = (lax.axis_index(name) for name in ("rep", "section", "tp"))
    chip, core = section // 2, section % 2
    layers = section_map.shape[1]
    _, _, micro, tokens, model = checkpoint.shape
    slots, width = value_weight.shape[1], value_weight.shape[3]
    rows = micro * tokens
    cut = model // tp_total
    piece = model // (replica_total * section_total)
    v_own, o_own = value_weight[0], out_weight[0]
    x_pair, top_pair = checkpoint[0, 0], top_grad[0]

    first_of = jnp.sum(section_map[:, None, :] < section_map[:, :, None], axis=2).astype(jnp.int32)
    slot_of = jnp.arange(layers, dtype=jnp.int32)[None] - first_of
    my_map = lax.dynamic_index_in_dim(section_map, rep, 0, keepdims=False)
    my_slot = lax.dynamic_index_in_dim(slot_of, rep, 0, keepdims=False)
    my_chip = my_map // 2
    far_of = lax.rem(my_chip - chip + chips, chips)

    swap = [(i, i ^ 1) for i in range(section_total)]

    def to_sibling(array):
        return lax.ppermute(array, "section", swap)

    def to_replica(array):
        return lax.ppermute(array, "rep", [(0, 1), (1, 0)])

    o_sib, v_sib = to_sibling(o_own), to_sibling(v_own)

    def scalars(own, slot):
        return jnp.stack([jnp.asarray(v, jnp.int32) for v in (own, slot, core, tp)])

    def shape(*dims, dtype=BF16):
        return jax.ShapeDtypeStruct(dims, dtype)

    def dma(*dims):
        return pltpu.SemaphoreType.DMA(dims)

    weight_bytes = model * width * 2
    weight_buffer = pltpu.VMEM((tp_total, cut, width), BF16)

    def reduce_slices(parts, base):
        got = lax.all_to_all(parts, "tp", 0, 0, tiled=True)
        count = parts.shape[1]
        return run(
            reduce_kernel,
            (scalars(1, 0), got, base),
            [SMEM, VMEM, ANY],
            shape(count, cut),
            VMEM,
            [pltpu.VMEM((count, cut), BF16), dma(1)],
            got.size * 2,
        )

    def gather_slices(mine):
        spread = jnp.broadcast_to(mine[None], (tp_total,) + mine.shape)
        return lax.all_to_all(spread, "tp", 0, 0, tiled=True)

    def recompute_slot(slot, x, with_parts):
        halves = (shape(tokens, width),) * 2 + (shape(tokens, width, dtype=F32),) * 2
        outs = ((shape(tp_total, rows, cut),) if with_parts else ()) + halves
        out_specs = ((HBM,) if with_parts else ()) + (VMEM,) * 4
        scratch = [pltpu.VMEM((tp_total, rows, cut), BF16), weight_buffer]
        scratch += [pltpu.VMEM((rows, width), BF16), pltpu.VMEM((rows, width), F32), dma(tp_total), dma(tp_total)]
        if with_parts:
            scratch += [weight_buffer, pltpu.VMEM((tp_total, rows, cut), BF16), dma(tp_total), dma(tp_total)]
        operands = (scalars(1, slot), x, v_own) + ((o_own,) if with_parts else ())
        specs = [SMEM, ANY, ANY] + ([ANY] if with_parts else [])
        count = 2 if with_parts else 1
        return run(
            functools.partial(recompute, tp_total, with_parts),
            operands,
            specs,
            outs,
            out_specs,
            scratch,
            count * weight_bytes,
            count * 2 * rows * model * width,
        )

    x_rows = x_pair.reshape(rows, model)
    parts, act_mine_0, act_other_0, slope_mine_0, slope_other_0 = recompute_slot(0, x_rows, True)
    x_other_0 = lax.dynamic_index_in_dim(x_pair, 1 - core, 0, keepdims=False)
    act_sib_0, slope_sib_0, x_sib_0 = to_sibling(act_other_0), to_sibling(slope_other_0), to_sibling(x_other_0)
    x_second = gather_slices(reduce_slices(parts, x_rows))
    act_mine_1, act_other_1, slope_mine_1, slope_other_1 = recompute_slot(1, x_second, False)
    slope_sib_1 = to_sibling(slope_other_1)
    act_sib_1 = to_sibling(act_other_1)
    x_other_1 = lax.dynamic_slice_in_dim(x_second, (1 - core) * tokens, tokens, 1)
    x_sib_1 = to_sibling(x_other_1)
    slopes = (slope_mine_0, slope_mine_1, slope_sib_0, slope_sib_1)

    def along_chips(heads, grads, places):
        count = len(heads)
        table = jnp.stack([jnp.asarray(v, jnp.int32) for v in [chip, core] + places])
        block = shape(count, tokens, width + 2 * cut)
        cuts = run(
            functools.partial(carve_kernel, count),
            (table, *heads, *grads),
            [SMEM] + [ANY] * (2 * count),
            (block,) * chips,
            (HBM,) * chips,
            [dma(chips * count * 3)],
            chips * count * tokens * (width + 2 * cut) * 4,
        )
        got = [cuts[0]]
        for far in range(1, chips):
            back = chips - far
            got.append(
                lax.ppermute(
                    cuts[back], "section", [(i, (i + 2 * back) % section_total) for i in range(section_total)]
                )
            )
        return got

    def to_owners(got, wanted, place_of):
        count = len(wanted)
        entries = [core, rep]
        for n, layer in enumerate(wanted):
            entries += [far_of[layer], place_of(n, layer)]
        table = jnp.stack([jnp.asarray(v, jnp.int32) for v in entries])
        both, alone = shape(count, tokens, width + piece), shape(count, tokens, piece)
        own_out, own_here, sib_out, sib_here = run(
            functools.partial(pick_kernel, count),
            (table, *got),
            [SMEM] + [ANY] * chips,
            (both, alone, both, alone),
            (HBM,) * 4,
            [dma(count, 6)],
            count * tokens * (width + piece) * 12,
        )
        from_sib, here_sib = to_sibling(sib_out), to_sibling(sib_here)
        return (own_here, own_out, here_sib, from_sib, to_replica(own_out), to_replica(from_sib))

    forward_got = along_chips(
        (act_mine_0, act_mine_1, act_sib_0, act_sib_1),
        (x_pair, x_second, x_sib_0, x_sib_1),
        [2 * core, 2 * core + 1, 2 - 2 * core, 3 - 2 * core],
    )

    down = [(i, i - 2) for i in range(2, section_total)]

    def one_layer(layer, g, deps):
        last = layer == 0
        own = my_map[layer] % 2 == core
        operands = (scalars(own, my_slot[layer]), g, *slopes, o_own, o_sib) + (() if last else (v_own, v_sib))
        outs = (() if last else (shape(tp_total, tokens, cut),)) + (shape(tokens, width),)
        scratch = [pltpu.VMEM((tp_total, tokens, cut), BF16), pltpu.VMEM((1, tokens, width), F32), weight_buffer]
        scratch += [pltpu.VMEM((tokens, width), BF16), dma(tp_total), dma(1), dma(tp_total), dma(1)]
        if not last:
            scratch += [weight_buffer, pltpu.VMEM((tp_total, tokens, cut), BF16), dma(tp_total), dma(tp_total)]
        count = 1 if last else 2
        return run(
            functools.partial(step, tp_total, not last, len(deps)),
            operands + tuple(deps),
            [SMEM] + [ANY] * (len(operands) + len(deps) - 1),
            outs,
            (HBM,) * len(outs),
            scratch,
            count * weight_bytes,
            count * 2 * tokens * model * width,
        )

    g = top_pair
    g_at, head_at = [None] * layers, [None] * layers
    deps = {layer: () for layer in range(layers)}
    upper, middle = list(range(layers - 1, 2, -1)), [2, 1]
    for layer in reversed(range(layers)):
        g_at[layer] = g
        if layer == 5:
            deps[5] = forward_got
            forward = to_owners(
                forward_got, list(range(layers)), lambda n, layer: 2 * (my_map[layer] % 2) + my_slot[layer]
            )
            deps[3] = forward
        if layer == 1:
            deps[1] = upper_got
            upper_all = to_owners(upper_got, upper[::-1], lambda n, layer: n)
            deps[0] = upper_all
        if layer == 0:
            deps[0] = tuple(deps[0]) + tuple(middle_got)
            (head_at[0],) = one_layer(0, g, deps[0])
            break
        parts, head_at[layer] = one_layer(layer, g, deps[layer])
        if layer == upper[-1]:
            order = upper[::-1]
            upper_got = along_chips([head_at[l] for l in order], [g_at[l] for l in order], list(range(len(order))))
        if layer == middle[-1]:
            order = middle[::-1]
            middle_got = along_chips([head_at[l] for l in order], [g_at[l] for l in order], list(range(len(order))))
        mine = reduce_slices(parts, g)
        distance = (section_map[:, layer] // 2) - (section_map[:, layer - 1] // 2)
        my_distance = my_chip[layer] - my_chip[layer - 1]

        def hop(i, value, my_distance=my_distance):
            came = lax.ppermute(value, "section", down)
            return jnp.where(i < my_distance, came, value)

        mine = lax.fori_loop(0, jnp.max(distance), hop, mine)
        g = gather_slices(mine)

    last_got = along_chips([head_at[0]], [g_at[0]], [0])
    middle_all = to_owners(middle_got, middle[::-1], lambda n, layer: n)
    last_all = to_owners(last_got, [0], lambda n, layer: n)
    result = gradients(layers, upper[-1], len(upper), forward, upper_all, None)
    result = gradients(layers, middle[-1], len(middle), forward, middle_all, result)
    return gradients(layers, 0, 1, forward, last_all, result)


def solution(mesh):
    placed = (
        P(),
        P("rep", "section", None, None, None),
        P("rep", None, None, None),
        P("rep", "section", None, "tp"),
        P("rep", "section", None, "tp"),
    )
    return jax.shard_map(
        per_device,
        mesh=mesh,
        in_specs=placed,
        out_specs=(P(None, ("rep", "section"), "tp"), P(None, ("rep", "section"), "tp")),
        check_vma=False,
    )
```

```python
import functools

import jax
import jax.numpy as jnp
from jax import lax
from jax.experimental import pallas as pl
from jax.experimental.pallas import tpu as pltpu
from jax.sharding import PartitionSpec as P

BF16 = jnp.bfloat16
F32 = jnp.float32
VMEM_BYTES = 16 * 1024 * 1024
NT = (((1,), (1,)), ((), ()))
TN = (((0,), (0,)), ((), ()))
ANY = pl.BlockSpec(memory_space=pl.ANY)
HBM = pl.BlockSpec(memory_space=pltpu.HBM)
SMEM = pl.BlockSpec(memory_space=pltpu.SMEM)
VMEM = pl.BlockSpec(memory_space=pltpu.VMEM)


def silu_slope(preact):
    sigma = jax.nn.sigmoid(preact)
    return sigma * (1.0 + preact * (1.0 - sigma))


def run(kernel, operands, specs, outs, out_specs, scratch, bytes_moved, flops=0):
    return pl.pallas_call(
        kernel,
        out_shape=outs,
        in_specs=specs,
        out_specs=out_specs,
        scratch_shapes=scratch,
        compiler_params=pltpu.CompilerParams(vmem_limit_bytes=VMEM_BYTES),
        cost_estimate=pl.CostEstimate(flops=flops, bytes_accessed=bytes_moved, transcendentals=0),
    )(*operands)


class Feed:
    def __init__(self, place, buffer, sems, chunks):
        self.copies = [pltpu.make_async_copy(place(i), buffer.at[i], sems.at[i]) for i in range(chunks)]
        self.buffer = buffer
        for copy in self.copies:
            copy.start()

    def take(self, i):
        self.copies[i].wait()
        return self.buffer[i]


def rows_place(ref, cut):
    if len(ref.shape) == 3:
        return lambda i: ref.at[i]
    return lambda i: ref.at[:, pl.ds(pl.multiple_of(i * cut, cut), cut)]


def recompute(chunks, with_parts, slot, deps, scalars, x_ref, v_ref, *refs):
    o_ref, refs = (refs[0], refs[1:]) if with_parts else (None, refs)
    refs = refs[deps:]
    part_ref, refs = (refs[0], refs[1:]) if with_parts else (None, refs)
    act_mine, act_other, slope_mine, slope_other, xbuf, vbuf, act_rows, slope_rows, xsem, vsem = refs[:10]
    cut = vbuf.shape[1]
    core = scalars[0]
    x = Feed(rows_place(x_ref, cut), xbuf, xsem, chunks)
    if with_parts:
        v = Feed(lambda i: v_ref.at[slot, pl.ds(i * cut, cut)], vbuf, vsem, chunks)
        obuf, stage, osem, psem = refs[10:]
        o = Feed(lambda i: o_ref.at[slot, pl.ds(i * cut, cut)], obuf, osem, chunks)
    pre = None
    for i in range(chunks):
        weight = v.take(i) if with_parts else v_ref[slot, i * cut : (i + 1) * cut, :]
        part = jnp.dot(x.take(i), weight, preferred_element_type=F32)
        pre = part if pre is None else pre + part
    act = jax.nn.silu(pre).astype(BF16)
    copies = []
    if with_parts:
        for i in range(chunks):
            stage[i] = lax.dot_general(act, o.take(i), NT, preferred_element_type=F32).astype(BF16)
            copies.append(pltpu.make_async_copy(stage.at[i], part_ref.at[i], psem.at[i]))
            copies[-1].start()
    act_rows[...] = act
    slope_rows[...] = silu_slope(pre)
    half = act_mine.shape[0]
    mine = pl.ds(pl.multiple_of(core * half, half), half)
    other = pl.ds(pl.multiple_of((1 - core) * half, half), half)
    act_mine[...] = act_rows[mine, :]
    act_other[...] = act_rows[other, :]
    slope_mine[...] = slope_rows[mine, :]
    slope_other[...] = slope_rows[other, :]
    for copy in copies:
        copy.wait()


def send_out(sources, outs, sems):
    copies = []
    for far, out in enumerate(outs):
        for k, source in sources(far):
            width = source.shape[-1]
            copies.append(pltpu.make_async_copy(source, out.at[:, pl.ds(k * width, width)], sems.at[len(copies)]))
            copies[-1].start()
    return copies


def step(chunks, chips, with_parts, deps, scalars, g_ref, *refs):
    slopes, refs = refs[:4], refs[4:]
    o_refs, refs = refs[:2], refs[2:]
    if with_parts:
        v_refs, refs = refs[:2], refs[2:]
    refs = refs[deps:]
    if with_parts:
        part_ref, refs = refs[0], refs[1:]
    outs, refs = refs[:chips], refs[chips:]
    head_rows, sems, g_sems = refs[:3]
    cut = g_ref.shape[-1]
    own, slot, chip = scalars[0], scalars[1], scalars[2]
    copies = send_out(
        lambda far: [(1 + r, g_ref.at[r * chips + lax.rem(chip + far, chips)]) for r in range(2)], outs, g_sems
    )

    def layer(o_ref, slope_pair, v_ref):
        total = None
        for i in range(chunks):
            part = jnp.dot(g_ref[i], o_ref[slot, i * cut : (i + 1) * cut, :], preferred_element_type=F32)
            total = part if total is None else total + part
        slope = jnp.where(slot == 0, slope_pair[0][...], slope_pair[1][...])
        head = (total * slope).astype(BF16)
        head_rows[...] = head
        send_out(lambda far: [(0, head_rows)], outs, sems)
        if with_parts:
            stage, psem = refs[3:]
            for i in range(chunks):
                part = lax.dot_general(
                    head, v_ref[slot, i * cut : (i + 1) * cut, :], NT, preferred_element_type=F32
                )
                stage[i] = part.astype(BF16)
                pltpu.make_async_copy(stage.at[i], part_ref.at[i], psem.at[i]).start()

    pl.when(own == 1)(lambda: layer(o_refs[0], slopes[:2], v_refs[0] if with_parts else None))
    pl.when(own == 0)(lambda: layer(o_refs[1], slopes[2:], v_refs[1] if with_parts else None))
    width = head_rows.shape[-1]
    for far, out in enumerate(outs):
        copies.append(pltpu.make_async_copy(head_rows, out.at[:, pl.ds(0, width)], sems.at[far]))
    if with_parts:
        stage, psem = refs[3:]
        copies += [pltpu.make_async_copy(stage.at[i], part_ref.at[i], psem.at[i]) for i in range(chunks)]
    for copy in copies:
        copy.wait()


def reduce_kernel(deps, scalars, got_ref, base_ref, *refs):
    mine_ref, base, sem = refs[deps:]
    copy = pltpu.make_async_copy(rows_place(base_ref, base.shape[1])(scalars[0]), base, sem.at[0])
    copy.start()
    total = got_ref[0].astype(F32)
    for i in range(1, got_ref.shape[0]):
        total += got_ref[i].astype(F32)
    copy.wait()
    mine_ref[...] = (base[...].astype(F32) + total).astype(BF16)


def load_kernel(first, second, after, first_near, second_near, sems):
    del after
    copies = []
    for source, target in ((first, first_near), (second, second_near)):
        for slot in range(source.shape[0]):
            copies.append(pltpu.make_async_copy(source.at[slot], target.at[slot], sems.at[len(copies)]))
            copies[-1].start()
    for copy in copies:
        copy.wait()


def carve_kernel(chips, scalars, act_mine, act_sib, x_mine, x_sib, *refs):
    outs, sems = refs[:chips], refs[chips]
    chip, core = scalars[0], scalars[1]
    width = act_mine.shape[-1]
    copies = []
    for k, (act, x) in enumerate(((act_mine, x_mine), (act_sib, x_sib))):
        at = core if k == 0 else 1 - core
        copies += send_out(
            lambda far: [(0, act)]
            + [(1 + r, rows_place(x, width)(r * chips + lax.rem(chip + far, chips))) for r in range(2)],
            [out.at[at] for out in outs],
            sems.at[k],
        )
    for copy in copies:
        copy.wait()


def pick_kernel(candidates, scalars, *refs):
    count = len(candidates)
    total = 1 + max(max(c) for c in candidates)
    sources, (own_out, own_here, sib_out, sib_here) = refs[:total], refs[total : total + 4]
    block, in_sems, sems = refs[total + 4 :]
    core, rep = scalars[0], scalars[1]
    width = block.shape[-1] // 3
    half = width // 2

    def columns(replica, side):
        return pl.ds(pl.multiple_of((1 + replica) * width + side * half, half), half)

    for n in range(count):
        for j in candidates[n]:

            def begin(n=n, j=j):
                source = sources[j].at[scalars[2 + 2 * n + 1]] if len(sources[j].shape) == 3 else sources[j]
                pltpu.make_async_copy(source, block.at[n], in_sems.at[n]).start()

            pl.when(scalars[2 + 2 * n] == j)(begin)
    copies = []
    for n in range(count):
        pltpu.make_async_copy(block.at[n], block.at[n], in_sems.at[n]).wait()
        moves = [
            (pl.ds(0, width), own_out.at[n, :, pl.ds(0, width)]),
            (columns(1 - rep, core), own_out.at[n, :, pl.ds(width, half)]),
            (columns(rep, core), own_here.at[n]),
            (pl.ds(0, width), sib_out.at[n, :, pl.ds(0, width)]),
            (columns(1 - rep, 1 - core), sib_out.at[n, :, pl.ds(width, half)]),
            (columns(rep, 1 - core), sib_here.at[n]),
        ]
        for k, (a, b) in enumerate(moves):
            copies.append(pltpu.make_async_copy(block.at[n, :, a], b, sems.at[n, k]))
            copies[-1].start()
    for copy in copies:
        copy.wait()


def gradient_kernel(first, *refs):
    (x0, xa1, x1, xa2, xa3, xa4), (g0, gh1, g1, gh2, gh3, gh4) = refs[:6], refs[6:12]
    value_ref, out_ref = refs[-2:]
    width = value_ref.shape[-1]

    def rows(alone0, with0, alone1, with1, with2, with3):
        narrow = [alone0[0], alone1[0], with2[0][:, width:], with3[0][:, width:]]
        wide = [with0[0][:, :width], with1[0][:, :width], with2[0][:, :width], with3[0][:, :width]]
        return jnp.concatenate(narrow, axis=0), jnp.concatenate(wide, axis=0)

    x, act = rows(x0, xa1, x1, xa2, xa3, xa4)
    g, head = rows(g0, gh1, g1, gh2, gh3, gh4)
    value_ref[0] = lax.dot_general(x, head, TN, preferred_element_type=F32).astype(BF16)
    out_ref[0] = lax.dot_general(g, act, TN, preferred_element_type=F32).astype(BF16)


def gradients(layers, first, count, forward, backward, before):
    piece = forward[0].shape[-1]
    width = forward[1].shape[-1] - piece
    out = jax.ShapeDtypeStruct((layers, piece, width), BF16)
    out_spec = pl.BlockSpec((1, piece, width), lambda l: (first + l, 0, 0))

    def block(array, start):
        return pl.BlockSpec((1,) + array.shape[1:], lambda l: (start + l, 0, 0))

    specs = [block(a, first) for a in forward] + [block(a, 0) for a in backward]
    operands = list(forward) + list(backward)
    aliases = {}
    if before is not None:
        aliases = {len(operands): 0, len(operands) + 1: 1}
        operands, specs = operands + list(before), specs + [ANY, ANY]
    return pl.pallas_call(
        functools.partial(gradient_kernel, first),
        out_shape=(out, out),
        grid=(count,),
        in_specs=specs,
        out_specs=(out_spec, out_spec),
        input_output_aliases=aliases,
        compiler_params=pltpu.CompilerParams(vmem_limit_bytes=VMEM_BYTES),
        cost_estimate=pl.CostEstimate(
            flops=count * 4 * piece * width * 256, bytes_accessed=count * 2400000, transcendentals=0
        ),
    )(*operands)


def per_device(section_map, checkpoint, top_grad, value_weight, out_weight):
    tp_total = lax.axis_size("tp")
    section_total = lax.axis_size("section")
    replica_total = lax.axis_size("rep")
    chips = section_total // 2
    rep, section, tp = (lax.axis_index(name) for name in ("rep", "section", "tp"))
    chip, core = section // 2, section % 2
    layers = section_map.shape[1]
    _, _, micro, tokens, model = checkpoint.shape
    slots, width = value_weight.shape[1], value_weight.shape[3]
    rows = micro * tokens
    cut = model // tp_total
    piece = model // (replica_total * section_total)
    v_own, o_own = value_weight[0], out_weight[0]
    x_pair, top_pair = checkpoint[0, 0], top_grad[0]

    first_of = jnp.sum(section_map[:, None, :] < section_map[:, :, None], axis=2).astype(jnp.int32)
    slot_of = jnp.arange(layers, dtype=jnp.int32)[None] - first_of
    my_map = lax.dynamic_index_in_dim(section_map, rep, 0, keepdims=False)
    my_slot = lax.dynamic_index_in_dim(slot_of, rep, 0, keepdims=False)
    my_chip = my_map // 2
    far_of = lax.rem(my_chip - chip + chips, chips)

    swap = [(i, i ^ 1) for i in range(section_total)]

    def to_sibling(array):
        return lax.ppermute(array, "section", swap)

    def to_replica(array):
        return lax.ppermute(array, "rep", [(0, 1), (1, 0)])

    o_sib, v_sib = to_sibling(o_own), to_sibling(v_own)

    def table(*values):
        return jnp.stack([jnp.asarray(v, jnp.int32) for v in values])

    def shape(*dims, dtype=BF16):
        return jax.ShapeDtypeStruct(dims, dtype)

    def in_hbm(*dims):
        return pltpu.HBM(dims, BF16)

    def dma(*dims):
        return pltpu.SemaphoreType.DMA(dims)

    weight_bytes = model * width * 2
    weight_buffer = pltpu.VMEM((tp_total, cut, width), BF16)

    def reduce_slices(parts, base, deps=()):
        got = lax.all_to_all(parts, "tp", 0, 0, tiled=True)
        count = parts.shape[1]
        return run(
            functools.partial(reduce_kernel, len(deps)),
            (table(tp), got, base, *deps),
            [SMEM, VMEM, ANY] + [ANY] * len(deps),
            shape(count, cut),
            VMEM,
            [pltpu.VMEM((count, cut), BF16), dma(1)],
            got.size * 2,
        )

    def gather_slices(mine):
        spread = jnp.broadcast_to(mine[None], (tp_total,) + mine.shape)
        return lax.all_to_all(spread, "tp", 0, 0, tiled=True)

    def load(first, second, deps):
        weight = pltpu.VMEM((slots, model, width), BF16)
        near = run(
            load_kernel,
            (first, second, deps),
            [ANY] * 3,
            (weight, weight),
            (VMEM, VMEM),
            [dma(2 * slots)],
            4 * slots * weight_bytes,
        )
        return tuple(pltpu.with_memory_space_constraint(a, pltpu.VMEM) for a in near)

    def recompute_slot(slot, x, with_parts, deps=()):
        halves = (shape(tokens, width),) * 2 + (shape(tokens, width, dtype=F32),) * 2
        outs = ((in_hbm(tp_total, rows, cut),) if with_parts else ()) + halves
        out_specs = ((HBM,) if with_parts else ()) + (VMEM,) * 4
        scratch = [pltpu.VMEM((tp_total, rows, cut), BF16), weight_buffer]
        scratch += [pltpu.VMEM((rows, width), BF16), pltpu.VMEM((rows, width), F32), dma(tp_total), dma(tp_total)]
        if with_parts:
            scratch += [weight_buffer, pltpu.VMEM((tp_total, rows, cut), BF16), dma(tp_total), dma(tp_total)]
        operands = (table(core), x) + ((v_own, o_own) if with_parts else (v_near,)) + tuple(deps)
        count = 2 if with_parts else 1
        return run(
            functools.partial(recompute, tp_total, with_parts, slot, len(deps)),
            operands,
            [SMEM, ANY] + ([ANY, ANY] if with_parts else [VMEM]) + [ANY] * len(deps),
            outs,
            out_specs,
            scratch,
            count * weight_bytes,
            count * 2 * rows * model * width,
        )

    def along_chips(cuts):
        got = [cuts[0]]
        for far in range(1, chips):
            back = chips - far
            route = [(i, (i + 2 * back) % section_total) for i in range(section_total)]
            got.append(lax.ppermute(cuts[back], "section", route))
        return got

    def carve(act_mine, act_sib, x_mine, x_sib):
        block = in_hbm(2, tokens, width + 2 * cut)
        return along_chips(
            run(
                functools.partial(carve_kernel, chips),
                (table(chip, core), act_mine, act_sib, x_mine, x_sib),
                [SMEM] + [VMEM] * 4,
                (block,) * chips,
                (HBM,) * chips,
                [dma(2, chips * 3)],
                2 * chips * tokens * (width + 2 * cut) * 4,
            )
        )

    def to_owners(sources, candidates, entries):
        count = len(candidates)
        both, alone = in_hbm(count, tokens, width + piece), in_hbm(count, tokens, piece)
        own_out, own_here, sib_out, sib_here = run(
            functools.partial(pick_kernel, candidates),
            (table(core, rep, *entries), *sources),
            [SMEM] + [ANY] * len(sources),
            (both, alone, both, alone),
            (HBM,) * 4,
            [pltpu.VMEM((count, tokens, width + 2 * cut), BF16), dma(count), dma(count, 6)],
            count * tokens * (width + piece) * 12,
        )
        from_sib, here_sib = to_sibling(sib_out), to_sibling(sib_here)
        return (own_here, own_out, here_sib, from_sib, to_replica(own_out), to_replica(from_sib))

    x_rows = x_pair.reshape(rows, model)
    parts, act_mine_0, act_other_0, slope_mine_0, slope_other_0 = recompute_slot(0, x_rows, True)
    x_mine_0 = lax.dynamic_index_in_dim(x_pair, core, 0, keepdims=False)
    x_sib_0 = to_sibling(lax.dynamic_index_in_dim(x_pair, 1 - core, 0, keepdims=False))
    act_sib_0, slope_sib_0 = to_sibling(act_other_0), to_sibling(slope_other_0)
    first_got = carve(act_mine_0, act_sib_0, x_mine_0, x_sib_0)
    o_near, v_near = load(o_own, v_own, parts)
    x_slice = reduce_slices(parts, x_rows, (o_near, v_near))
    o_far, v_far = load(o_sib, v_sib, x_slice)
    x_second = gather_slices(x_slice)
    act_mine_1, act_other_1, slope_mine_1, slope_other_1 = recompute_slot(
        1, x_second, False, (*first_got, o_far, v_far)
    )
    slope_sib_1, act_sib_1 = to_sibling(slope_other_1), to_sibling(act_other_1)
    x_mine_1 = lax.dynamic_slice_in_dim(x_second, core * tokens, tokens, 1)
    x_sib_1 = to_sibling(lax.dynamic_slice_in_dim(x_second, (1 - core) * tokens, tokens, 1))
    second_got = carve(act_mine_1, act_sib_1, x_mine_1, x_sib_1)
    slopes = (slope_mine_0, slope_mine_1, slope_sib_0, slope_sib_1)

    down = [(i, i - 2) for i in range(2, section_total)]

    def one_layer(layer, g, deps):
        last = layer == 0
        own = my_map[layer] % 2 == core
        operands = (table(own, my_slot[layer], chip), g, *slopes, o_near, o_far)
        operands += () if last else (v_near, v_far)
        block = in_hbm(tokens, width + 2 * cut)
        outs = (() if last else (in_hbm(tp_total, tokens, cut),)) + (block,) * chips
        scratch = [pltpu.VMEM((tokens, width), BF16), dma(chips), dma(2 * chips)]
        if not last:
            scratch += [pltpu.VMEM((tp_total, tokens, cut), BF16), dma(tp_total)]
        count = 1 if last else 2
        result = run(
            functools.partial(step, tp_total, chips, not last, len(deps)),
            operands + tuple(deps),
            [SMEM] + [VMEM] * (len(operands) - 1) + [ANY] * len(deps),
            outs,
            (HBM,) * len(outs),
            scratch,
            count * weight_bytes // 8,
            count * 2 * tokens * model * width,
        )
        cuts = result[-chips:]
        return (None if last else result[0]), along_chips(cuts)

    g = lax.dynamic_index_in_dim(top_pair, core, 0, keepdims=False)
    g = g.reshape(tokens, tp_total, cut).transpose(1, 0, 2)
    got_at = [None] * layers
    deps = {layer: () for layer in range(layers)}
    upper, middle = [3, 4, 5, 6, 7], [1, 2]

    def collect(wanted):
        sources = [array for layer in wanted for array in got_at[layer]]
        candidates = [[n * chips + far for far in range(chips)] for n in range(len(wanted))]
        entries = []
        for n, layer in enumerate(wanted):
            entries += [n * chips + far_of[layer], 0]
        return to_owners(sources, candidates, entries)

    for layer in reversed(range(layers)):
        if layer == 6:
            deps[6] = second_got
            sources = first_got + second_got
            entries = []
            for wanted in range(layers):
                entries += [my_slot[wanted] * chips + far_of[wanted], my_map[wanted] % 2]
            forward = to_owners(sources, [list(range(2 * chips))] * layers, entries)
            deps[3] = forward
        if layer == 2:
            upper_all = collect(upper)
            deps[0] = upper_all
        parts, got_at[layer] = one_layer(layer, g, deps[layer])
        if layer == 0:
            break
        mine = reduce_slices(parts, g, got_at[layer])
        distance = (section_map[:, layer] // 2) - (section_map[:, layer - 1] // 2)
        my_distance = my_chip[layer] - my_chip[layer - 1]

        def hop(i, value, my_distance=my_distance):
            came = lax.ppermute(value, "section", down)
            return jnp.where(i < my_distance, came, value)

        mine = lax.fori_loop(0, jnp.max(distance), hop, mine)
        g = gather_slices(mine)

    middle_all, last_all = collect(middle), collect([0])
    result = gradients(layers, upper[0], len(upper), forward, upper_all, None)
    result = gradients(layers, middle[0], len(middle), forward, middle_all, result)
    return gradients(layers, 0, 1, forward, last_all, result)


def solution(mesh):
    placed = (
        P(),
        P("rep", "section", None, None, None),
        P("rep", None, None, None),
        P("rep", "section", None, "tp"),
        P("rep", "section", None, "tp"),
    )
    return jax.shard_map(
        per_device,
        mesh=mesh,
        in_specs=placed,
        out_specs=(P(None, ("rep", "section"), "tp"), P(None, ("rep", "section"), "tp")),
        check_vma=False,
    )
```

```python
import functools

import jax
import jax.numpy as jnp
from jax import lax
from jax.experimental import pallas as pl
from jax.experimental.pallas import tpu as pltpu
from jax.sharding import PartitionSpec as P

BF16 = jnp.bfloat16
F32 = jnp.float32
VMEM_BYTES = 64 * 1024 * 1024
NT = (((1,), (1,)), ((), ()))
TN = (((0,), (0,)), ((), ()))
ANY = pl.BlockSpec(memory_space=pl.ANY)
HBM = pl.BlockSpec(memory_space=pltpu.HBM)
SMEM = pl.BlockSpec(memory_space=pltpu.SMEM)
VMEM = pl.BlockSpec(memory_space=pltpu.VMEM)


def silu_slope(preact):
    sigma = jax.nn.sigmoid(preact)
    return sigma * (1.0 + preact * (1.0 - sigma))


def run(kernel, operands, specs, outs, out_specs, scratch, bytes_moved, flops=0):
    return pl.pallas_call(
        kernel,
        out_shape=outs,
        in_specs=specs,
        out_specs=out_specs,
        scratch_shapes=scratch,
        compiler_params=pltpu.CompilerParams(vmem_limit_bytes=VMEM_BYTES),
        cost_estimate=pl.CostEstimate(flops=flops, bytes_accessed=bytes_moved, transcendentals=0),
    )(*operands)


def rows_place(ref, cut):
    if len(ref.shape) == 3:
        return lambda i: ref.at[i]
    return lambda i: ref.at[:, pl.ds(pl.multiple_of(i * cut, cut), cut)]


class Copies:
    def __init__(self, sems):
        self.sems, self.all = sems, []

    def start(self, source, target, condition=None):
        copy = pltpu.make_async_copy(source, target, self.sems.at[len(self.all)])
        if condition is None:
            copy.start()
        else:
            pl.when(condition)(copy.start)
        self.all.append(copy)
        return copy

    def either(self, condition, first, second, target):
        sem = self.sems.at[len(self.all)]
        pl.when(condition)(lambda: pltpu.make_async_copy(first, target, sem).start())
        pl.when(jnp.logical_not(condition))(lambda: pltpu.make_async_copy(second, target, sem).start())
        self.all.append(pltpu.make_async_copy(first, target, sem))
        return self.all[-1]

    def wait(self):
        for copy in self.all:
            copy.wait()


def halves(ref):
    step = ref.shape[0] // 2
    return [pl.ds(i * step, step) for i in range(2)]


def product_in(rows, weight, waits):
    cuts, cut = rows.shape[0], rows.shape[-1]
    total = None
    for i in range(cuts):
        if i % (cuts // len(waits)) == 0:
            waits[i // (cuts // len(waits))].wait()
        part = jnp.dot(rows[i], weight[i * cut : (i + 1) * cut, :], preferred_element_type=F32)
        total = part if total is None else total + part
    return total


def product_out(rows, weight, waits, stage, part_ref, out):
    cuts, cut = stage.shape[0], stage.shape[-1]
    group = cuts // len(waits)
    for i in range(cuts):
        if i % group == 0:
            waits[i // group].wait()
        part = lax.dot_general(rows, weight[i * cut : (i + 1) * cut, :], NT, preferred_element_type=F32)
        stage[i] = part.astype(BF16)
        if i % group == group - 1:
            cuts_done = pl.ds(i - group + 1, group)
            out.start(stage.at[cuts_done], part_ref.at[cuts_done])


def recompute(chips, with_parts, slot, deps, scalars, x_ref, v_ref, *refs):
    o_ref, refs = (refs[0], refs[1:]) if with_parts else (None, refs)
    refs = refs[deps:]
    part_ref, refs = (refs[0], refs[1:]) if with_parts else (None, refs)
    outs, (xbuf, vbuf, act_rows, slope_rows, in_sems, out_sems) = refs[:6], refs[6:12]
    cuts, cut = xbuf.shape[0], xbuf.shape[-1]
    core, side = scalars[0], scalars[1]
    arriving, leaving = Copies(in_sems), Copies(out_sems)
    x = [arriving.start(rows_place(x_ref, cut)(i), xbuf.at[i]) for i in range(cuts)]
    v = [arriving.start(v_ref.at[slot, rows], vbuf.at[rows]) for rows in halves(vbuf)]
    if with_parts:
        obuf, stage = refs[12:]
        o = [arriving.start(o_ref.at[slot, rows], obuf.at[rows]) for rows in halves(obuf)]
    for copy in x:
        copy.wait()
    pre = product_in(xbuf, vbuf, v)
    act = jax.nn.silu(pre).astype(BF16)
    if with_parts:
        product_out(act, obuf, o, stage, part_ref, leaving)
    act_rows[...] = act
    slope_rows[...] = silu_slope(pre)
    half = outs[0].shape[0]
    quarter = cut // 4
    for k, which in enumerate((core, 1 - core)):
        rows = pl.ds(pl.multiple_of(which * half, half), half)
        act_out, slope_out, x_out = outs[k], outs[2 + k], outs[4 + k]
        act_out[...] = act_rows[rows, :]
        slope_out[...] = slope_rows[rows, :]
        for to in range(chips):
            for j in range(4):
                columns = pl.ds(pl.multiple_of((j % 2) * 2 * quarter + side * quarter, quarter), quarter)
                x_out[to, :, j * quarter : (j + 1) * quarter] = xbuf[(j // 2) * chips + to, rows, columns]
    leaving.wait()


def step(chips, with_parts, deps, scalars, g_ref, *refs):
    slopes, refs = refs[:4], refs[4:]
    o_refs, refs = refs[:2], refs[2:]
    v_refs, refs = (refs[:2], refs[2:]) if with_parts else (None, refs)
    refs = refs[deps:]
    part_ref, refs = (refs[0], refs[1:]) if with_parts else (None, refs)
    outs, (gbuf, sbuf, obuf, head_rows, in_sems, out_sems) = refs[:chips], refs[chips : chips + 6]
    cut, width = gbuf.shape[-1], head_rows.shape[-1]
    quarter = cut // 4
    own, slot, chip, side = scalars[0] == 1, scalars[1], scalars[2], scalars[3]
    arriving, leaving = Copies(in_sems), Copies(out_sems)
    g = arriving.start(g_ref, gbuf)
    o = [arriving.either(own, o_refs[0].at[slot, r], o_refs[1].at[slot, r], obuf.at[r]) for r in halves(obuf)]
    which = jnp.where(own, 0, 2) + slot
    for j in range(4):
        pl.when(which == j)(pltpu.make_async_copy(slopes[j], sbuf, in_sems.at[5]).start)
    slope = pltpu.make_async_copy(slopes[0], sbuf, in_sems.at[5])
    if with_parts:
        vbuf, stage = refs[chips + 6 :]
        v = [arriving.either(own, v_refs[0].at[slot, r], v_refs[1].at[slot, r], vbuf.at[r]) for r in halves(vbuf)]
    g.wait()
    total = product_in(gbuf, obuf, o)
    slope.wait()
    head = (total * sbuf[...]).astype(BF16)
    head_rows[...] = head
    for far, out in enumerate(outs):
        to = lax.rem(chip + far, chips)
        for j in range(4):
            columns = pl.ds(pl.multiple_of((j % 2) * 2 * quarter + side * quarter, quarter), quarter)
            source = gbuf.at[(j // 2) * chips + to, :, columns]
            leaving.start(source, out.at[:, pl.ds(width + j * quarter, quarter)])
        leaving.start(head_rows, out.at[:, pl.ds(0, width)])
    if with_parts:
        product_out(head, vbuf, v, stage, part_ref, leaving)
    leaving.wait()


def reduce_kernel(deps, scalars, got_ref, base_ref, *refs):
    mine_ref, base, sem = refs[deps:]
    copy = pltpu.make_async_copy(rows_place(base_ref, base.shape[1])(scalars[0]), base, sem.at[0])
    copy.start()
    total = got_ref[0].astype(F32)
    for i in range(1, got_ref.shape[0]):
        total += got_ref[i].astype(F32)
    copy.wait()
    mine_ref[...] = (base[...].astype(F32) + total).astype(BF16)


def carve_kernel(chips, scalars, act_mine, act_sib, x_mine, x_sib, *refs):
    outs, sems = refs[:chips], refs[chips]
    chip, core = scalars[0], scalars[1]
    width = act_mine.shape[-1]
    copies = []
    for k, (act, x) in enumerate(((act_mine, x_mine), (act_sib, x_sib))):
        at = core if k == 0 else 1 - core
        for far, out in enumerate(outs):
            to = lax.rem(chip + far, chips)
            for j, source in enumerate((act, x.at[to])):
                target = out.at[at, :, pl.ds(j * width, width)]
                copies.append(pltpu.make_async_copy(source, target, sems.at[k, far, j]))
                copies[-1].start()
    for copy in copies:
        copy.wait()


def pick_kernel(candidates, scalars, *refs):
    count = len(candidates)
    total = 1 + max(max(c) for c in candidates)
    sources, (own_out, sib_out, block, in_sems, sems) = refs[:total], refs[total:]
    core, rep = scalars[0], scalars[1]
    width = block.shape[-1] // 2
    quarter = width // 4
    for n in range(count):
        for j in candidates[n]:

            def begin(n=n, j=j):
                source = sources[j].at[scalars[2 + 2 * n + 1]] if len(sources[j].shape) == 3 else sources[j]
                pltpu.make_async_copy(source, block.at[n], in_sems.at[n]).start()

            pl.when(scalars[2 + 2 * n] == j)(begin)
    copies = []
    for n in range(count):
        pltpu.make_async_copy(block.at[n], block.at[n], in_sems.at[n]).wait()
        for k, (out, side) in enumerate(((own_out, core), (sib_out, 1 - core))):
            for j, replica in enumerate((None, 1 - rep, rep)):
                if replica is None:
                    source, target = block.at[n, :, pl.ds(0, width)], out.at[n, :, pl.ds(0, width)]
                else:
                    columns = pl.ds(pl.multiple_of(width + (replica * 2 + side) * quarter, quarter), quarter)
                    source = block.at[n, :, columns]
                    target = out.at[n, :, pl.ds(width + (j - 1) * quarter, quarter)]
                copies.append(pltpu.make_async_copy(source, target, sems.at[n, k, j]))
                copies[-1].start()
    for copy in copies:
        copy.wait()


def gradient_kernel(scalars, *refs):
    value_ref, out_ref = refs[-2:]
    width = value_ref.shape[-1]
    first_side = scalars[0] == 0

    def factors(parts, mine, theirs):
        wide = jnp.concatenate([part[0][:, :width] for part in parts], axis=0)
        mine, theirs = (jnp.concatenate([ref[k, 0] for k in range(4)], axis=0) for ref in (mine, theirs))
        left = jnp.where(first_side, mine, theirs)
        right = jnp.where(first_side, theirs, mine)
        return jnp.concatenate([left, right], axis=1), wide

    x, act = factors(refs[0:4], refs[4], refs[5])
    g, head = factors(refs[6:10], refs[10], refs[11])
    value_ref[0] = lax.dot_general(x, head, TN, preferred_element_type=F32).astype(BF16)
    out_ref[0] = lax.dot_general(g, act, TN, preferred_element_type=F32).astype(BF16)


def gradients(side, layers, first, count, forward, backward, before):
    quarter = forward[4].shape[-1]
    piece, width = 2 * quarter, forward[0].shape[-1] - 2 * quarter
    out = jax.ShapeDtypeStruct((layers, piece, width), BF16)
    out_spec = pl.BlockSpec((1, piece, width), lambda l: (first + l, 0, 0))

    def block(array, start):
        if array.ndim == 3:
            return pl.BlockSpec((1,) + array.shape[1:], lambda l: (start + l, 0, 0))
        return pl.BlockSpec((array.shape[0], 1) + array.shape[2:], lambda l: (0, start + l, 0, 0))

    specs = [SMEM] + [block(a, first) for a in forward] + [block(a, 0) for a in backward]
    operands = [side] + list(forward) + list(backward)
    aliases = {}
    if before is not None:
        aliases = {len(operands): 0, len(operands) + 1: 1}
        operands, specs = operands + list(before), specs + [ANY, ANY]
    return pl.pallas_call(
        gradient_kernel,
        out_shape=(out, out),
        grid=(count,),
        in_specs=specs,
        out_specs=(out_spec, out_spec),
        input_output_aliases=aliases,
        compiler_params=pltpu.CompilerParams(vmem_limit_bytes=VMEM_BYTES),
        cost_estimate=pl.CostEstimate(
            flops=count * 4 * piece * width * 256, bytes_accessed=count * 2400000, transcendentals=0
        ),
    )(*operands)


def per_device(section_map, checkpoint, top_grad, value_weight, out_weight):
    tp_total = lax.axis_size("tp")
    section_total = lax.axis_size("section")
    replica_total = lax.axis_size("rep")
    chips = section_total // 2
    rep, section, tp = (lax.axis_index(name) for name in ("rep", "section", "tp"))
    chip, core, side = section // 2, section % 2, tp % 2
    layers = section_map.shape[1]
    _, _, micro, tokens, model = checkpoint.shape
    slots, width = value_weight.shape[1], value_weight.shape[3]
    rows = micro * tokens
    cut = model // tp_total
    piece = model // (replica_total * section_total)
    v_own, o_own = value_weight[0], out_weight[0]
    x_pair, top_pair = checkpoint[0, 0], top_grad[0]

    first_of = jnp.sum(section_map[:, None, :] < section_map[:, :, None], axis=2).astype(jnp.int32)
    slot_of = jnp.arange(layers, dtype=jnp.int32)[None] - first_of
    my_map = lax.dynamic_index_in_dim(section_map, rep, 0, keepdims=False)
    my_slot = lax.dynamic_index_in_dim(slot_of, rep, 0, keepdims=False)
    my_chip = my_map // 2
    far_of = lax.rem(my_chip - chip + chips, chips)

    swap = [(i, i ^ 1) for i in range(section_total)]

    def to_sibling(array):
        return lax.ppermute(array, "section", swap)

    def to_replica(array):
        return lax.ppermute(array, "rep", [(0, 1), (1, 0)])

    o_sib, v_sib = to_sibling(o_own), to_sibling(v_own)

    def table(*values):
        return jnp.stack([jnp.asarray(v, jnp.int32) for v in values])

    def shape(*dims, dtype=BF16):
        return jax.ShapeDtypeStruct(dims, dtype)

    def in_hbm(*dims):
        return pltpu.HBM(dims, BF16)

    def dma(*dims):
        return pltpu.SemaphoreType.DMA(dims)

    weight_bytes = model * width * 2
    weight_buffer = pltpu.VMEM((model, width), BF16)

    def reduce_slices(parts, base, deps=()):
        got = lax.all_to_all(parts, "tp", 0, 0, tiled=True)
        count = parts.shape[1]
        return run(
            functools.partial(reduce_kernel, len(deps)),
            (table(tp), got, base, *deps),
            [SMEM, VMEM, ANY] + [ANY] * len(deps),
            shape(count, cut),
            VMEM,
            [pltpu.VMEM((count, cut), BF16), dma(1)],
            got.size * 2,
        )

    def gather_slices(mine):
        spread = jnp.broadcast_to(mine[None], (tp_total,) + mine.shape)
        return lax.all_to_all(spread, "tp", 0, 0, tiled=True)

    def recompute_slot(slot, x, with_parts, deps=()):
        halves = (shape(tokens, width),) * 2 + (shape(tokens, width, dtype=F32),) * 2
        halves += (shape(chips, tokens, cut),) * 2
        outs = ((in_hbm(tp_total, rows, cut),) if with_parts else ()) + halves
        out_specs = ((HBM,) if with_parts else ()) + (VMEM,) * 6
        scratch = [pltpu.VMEM((tp_total, rows, cut), BF16), weight_buffer]
        scratch += [pltpu.VMEM((rows, width), BF16), pltpu.VMEM((rows, width), F32), dma(tp_total + 4), dma(2)]
        if with_parts:
            scratch += [weight_buffer, pltpu.VMEM((tp_total, rows, cut), BF16)]
        operands = (table(core, side), x, v_own) + ((o_own,) if with_parts else ()) + tuple(deps)
        count = 2 if with_parts else 1
        return run(
            functools.partial(recompute, chips, with_parts, slot, len(deps)),
            operands,
            [SMEM] + [ANY] * (len(operands) - 1),
            outs,
            out_specs,
            scratch,
            count * weight_bytes,
            count * 2 * rows * model * width,
        )

    def along_chips(cuts):
        got = [cuts[0]]
        for far in range(1, chips):
            back = chips - far
            route = [(i, (i + 2 * back) % section_total) for i in range(section_total)]
            got.append(lax.ppermute(cuts[back], "section", route))
        return got

    def carve(act_mine, act_sib, x_mine, x_sib):
        block = in_hbm(2, tokens, width + cut)
        return along_chips(
            run(
                functools.partial(carve_kernel, chips),
                (table(chip, core), act_mine, act_sib, x_mine, x_sib),
                [SMEM] + [VMEM] * 4,
                (block,) * chips,
                (HBM,) * chips,
                [dma(2, chips, 2)],
                2 * chips * tokens * (width + cut) * 4,
            )
        )

    def to_owners(sources, candidates, entries):
        count = len(candidates)
        out = in_hbm(count, tokens, width + piece)
        own_out, sib_out = run(
            functools.partial(pick_kernel, candidates),
            (table(core, rep, *entries), *sources),
            [SMEM] + [ANY] * len(sources),
            (out, out),
            (HBM,) * 2,
            [pltpu.VMEM((count, tokens, width + cut), BF16), dma(count), dma(count, 2, 3)],
            count * tokens * (width + piece) * 12,
        )
        from_sib = to_sibling(sib_out)
        parts = (own_out, from_sib, to_replica(own_out), to_replica(from_sib))
        half = piece // 2
        mine = jnp.stack([p[:, :, -half:] for p in parts[:2]] + [p[:, :, -2 * half : -half] for p in parts[2:]])
        theirs = lax.ppermute(mine, "tp", [(i, i ^ 1) for i in range(tp_total)])
        return parts + (mine, theirs)

    x_rows = x_pair.reshape(rows, model)
    parts, act_mine_0, act_other_0, slope_mine_0, slope_other_0, x_mine_0, x_other_0 = recompute_slot(0, x_rows, True)
    act_sib_0, slope_sib_0, x_sib_0 = to_sibling(act_other_0), to_sibling(slope_other_0), to_sibling(x_other_0)
    first_got = carve(act_mine_0, act_sib_0, x_mine_0, x_sib_0)
    x_slice = reduce_slices(parts, x_rows)
    x_second = gather_slices(x_slice)
    act_mine_1, act_other_1, slope_mine_1, slope_other_1, x_mine_1, x_other_1 = recompute_slot(
        1, x_second, False, first_got
    )
    slope_sib_1, act_sib_1, x_sib_1 = to_sibling(slope_other_1), to_sibling(act_other_1), to_sibling(x_other_1)
    second_got = carve(act_mine_1, act_sib_1, x_mine_1, x_sib_1)
    slopes = (slope_mine_0, slope_mine_1, slope_sib_0, slope_sib_1)

    down = [(i, i - 2) for i in range(2, section_total)]

    def one_layer(layer, g, deps):
        last = layer == 0
        own = my_map[layer] % 2 == core
        operands = (table(own, my_slot[layer], chip, side), g, *slopes, o_own, o_sib)
        operands += (() if last else (v_own, v_sib)) + tuple(deps)
        block = in_hbm(tokens, width + cut)
        outs = (() if last else (in_hbm(tp_total, tokens, cut),)) + (block,) * chips
        scratch = [pltpu.VMEM((tp_total, tokens, cut), BF16), pltpu.VMEM((tokens, width), F32), weight_buffer]
        scratch += [pltpu.VMEM((tokens, width), BF16), dma(6), dma(5 * chips + 2)]
        if not last:
            scratch += [weight_buffer, pltpu.VMEM((tp_total, tokens, cut), BF16)]
        count = 1 if last else 2
        result = run(
            functools.partial(step, chips, not last, len(deps)),
            operands,
            [SMEM] + [ANY] * (len(operands) - 1),
            outs,
            (HBM,) * len(outs),
            scratch,
            count * weight_bytes,
            count * 2 * tokens * model * width,
        )
        return (None if last else result[0]), along_chips(result[-chips:])

    g = lax.dynamic_index_in_dim(top_pair, core, 0, keepdims=False)
    g = g.reshape(tokens, tp_total, cut).transpose(1, 0, 2)
    got_at = [None] * layers
    deps = {layer: [] for layer in range(layers)}
    upper, middle = [3, 4, 5, 6, 7], [1, 2]

    def collect(wanted):
        sources = [array for layer in wanted for array in got_at[layer]]
        candidates = [[n * chips + far for far in range(chips)] for n in range(len(wanted))]
        entries = []
        for n, layer in enumerate(wanted):
            entries += [n * chips + far_of[layer], 0]
        return to_owners(sources, candidates, entries)

    for layer in reversed(range(layers)):
        if layer < layers - 1:
            deps[layer] += got_at[layer + 1]
        if layer == 6:
            deps[6] += second_got
        if layer == 5:
            sources = first_got + second_got
            entries = []
            for wanted in range(layers):
                entries += [my_slot[wanted] * chips + far_of[wanted], my_map[wanted] % 2]
            forward = to_owners(sources, [list(range(2 * chips))] * layers, entries)
            deps[3] += forward
        if layer == 2:
            upper_all = collect(upper)
            deps[0] += upper_all
        parts, got_at[layer] = one_layer(layer, g, deps[layer])
        if layer == 0:
            break
        mine = reduce_slices(parts, g)
        distance = (section_map[:, layer] // 2) - (section_map[:, layer - 1] // 2)
        my_distance = my_chip[layer] - my_chip[layer - 1]

        def hop(i, value, my_distance=my_distance):
            came = lax.ppermute(value, "section", down)
            return jnp.where(i < my_distance, came, value)

        mine = lax.fori_loop(0, jnp.max(distance), hop, mine)
        g = gather_slices(mine)

    middle_all, last_all = collect(middle), collect([0])
    result = gradients(table(side), layers, upper[0], len(upper), forward, upper_all, None)
    result = gradients(table(side), layers, middle[0], len(middle), forward, middle_all, result)
    return gradients(table(side), layers, 0, 1, forward, last_all, result)


def solution(mesh):
    placed = (
        P(),
        P("rep", "section", None, None, None),
        P("rep", None, None, None),
        P("rep", "section", None, "tp"),
        P("rep", "section", None, "tp"),
    )
    return jax.shard_map(
        per_device,
        mesh=mesh,
        in_specs=placed,
        out_specs=(P(None, ("rep", "section"), "tp"), P(None, ("rep", "section"), "tp")),
        check_vma=False,
    )
```

```python
import functools

import jax
import jax.numpy as jnp
from jax import lax
from jax.experimental import pallas as pl
from jax.experimental.pallas import tpu as pltpu
from jax.sharding import PartitionSpec as P

BF16 = jnp.bfloat16
F32 = jnp.float32
VMEM_BYTES = 64 * 1024 * 1024
NT = (((1,), (1,)), ((), ()))
TN = (((0,), (0,)), ((), ()))
ANY = pl.BlockSpec(memory_space=pl.ANY)
HBM = pl.BlockSpec(memory_space=pltpu.HBM)
SMEM = pl.BlockSpec(memory_space=pltpu.SMEM)
VMEM = pl.BlockSpec(memory_space=pltpu.VMEM)


REP, CHIP, CORE, SIDE, TP = range(5)


def held_at(ids, section_map, layer):
    section = section_map[ids[REP], layer]
    slot = jnp.int32(0)
    if layer > 0:
        slot = (section_map[ids[REP], layer - 1] == section).astype(jnp.int32)
    chips = 4
    return lax.rem(section, 2), slot, lax.rem(section // 2 - ids[CHIP] + chips, chips)


def silu_slope(preact):
    sigma = jax.nn.sigmoid(preact)
    return sigma * (1.0 + preact * (1.0 - sigma))


def run(kernel, operands, specs, outs, out_specs, scratch, bytes_moved, flops=0):
    return pl.pallas_call(
        kernel,
        out_shape=outs,
        in_specs=specs,
        out_specs=out_specs,
        scratch_shapes=scratch,
        compiler_params=pltpu.CompilerParams(vmem_limit_bytes=VMEM_BYTES),
        cost_estimate=pl.CostEstimate(flops=flops, bytes_accessed=bytes_moved, transcendentals=0),
    )(*operands)


def rows_place(ref, cut, core):
    if len(ref.shape) == 3 and ref.shape[-1] == cut:
        return lambda i: ref.at[i]
    columns = lambda i: pl.ds(pl.multiple_of(i * cut, cut), cut)
    if len(ref.shape) == 2:
        return lambda i: ref.at[:, columns(i)]
    return lambda i: ref.at[core, :, columns(i)]


class Copies:
    def __init__(self, sems):
        self.sems, self.all = sems, []

    def start(self, source, target, condition=None):
        copy = pltpu.make_async_copy(source, target, self.sems.at[len(self.all)])
        if condition is None:
            copy.start()
        else:
            pl.when(condition)(copy.start)
        self.all.append(copy)
        return copy

    def either(self, condition, first, second, target):
        sem = self.sems.at[len(self.all)]
        pl.when(condition)(lambda: pltpu.make_async_copy(first, target, sem).start())
        pl.when(jnp.logical_not(condition))(lambda: pltpu.make_async_copy(second, target, sem).start())
        self.all.append(pltpu.make_async_copy(first, target, sem))
        return self.all[-1]

    def wait(self):
        for copy in self.all:
            copy.wait()


def halves(ref):
    step = ref.shape[0] // 2
    return [pl.ds(i * step, step) for i in range(2)]


def product_in(rows, weight, waits):
    cuts, cut = rows.shape[0], rows.shape[-1]
    total = None
    for i in range(cuts):
        if i % (cuts // len(waits)) == 0:
            waits[i // (cuts // len(waits))].wait()
        part = jnp.dot(rows[i], weight[i * cut : (i + 1) * cut, :], preferred_element_type=F32)
        total = part if total is None else total + part
    return total


def product_out(rows, weight, waits, stage, part_ref, out):
    cuts, cut = stage.shape[0], stage.shape[-1]
    group = cuts // len(waits)
    for i in range(cuts):
        if i % group == 0:
            waits[i // group].wait()
        part = lax.dot_general(rows, weight[i * cut : (i + 1) * cut, :], NT, preferred_element_type=F32)
        stage[i] = part.astype(BF16)
        if i % group == group - 1:
            cuts_done = pl.ds(i - group + 1, group)
            out.start(stage.at[cuts_done], part_ref.at[cuts_done])


def recompute(chips, with_parts, slot, ids, x_ref, v_ref, *refs):
    o_ref, refs = (refs[0], refs[1:]) if with_parts else (None, refs)
    part_ref, refs = (refs[0], refs[1:]) if with_parts else (None, refs)
    outs, (xbuf, vbuf, act_rows, slope_rows, in_sems, out_sems) = refs[:6], refs[6:12]
    cuts, cut = xbuf.shape[0], xbuf.shape[-1]
    core, side = ids[CORE], ids[SIDE]
    arriving, leaving = Copies(in_sems), Copies(out_sems)
    x = [arriving.start(rows_place(x_ref, cut, core)(i), xbuf.at[i]) for i in range(cuts)]
    v = [arriving.start(v_ref.at[slot, rows], vbuf.at[rows]) for rows in halves(vbuf)]
    if with_parts:
        obuf, stage = refs[12:]
        o = [arriving.start(o_ref.at[slot, rows], obuf.at[rows]) for rows in halves(obuf)]
    for copy in x:
        copy.wait()
    pre = product_in(xbuf, vbuf, v)
    act = jax.nn.silu(pre).astype(BF16)
    if with_parts:
        product_out(act, obuf, o, stage, part_ref, leaving)
    act_rows[...] = act
    slope_rows[...] = silu_slope(pre)
    half = outs[0].shape[0]
    quarter = cut // 4
    for k, which in enumerate((core, 1 - core)):
        rows = pl.ds(pl.multiple_of(which * half, half), half)
        act_out, slope_out, x_out = outs[k], outs[2 + k], outs[4 + k]
        act_out[...] = act_rows[rows, :]
        slope_out[...] = slope_rows[rows, :]
        for to in range(chips):
            for j in range(4):
                columns = pl.ds(pl.multiple_of((j % 2) * 2 * quarter + side * quarter, quarter), quarter)
                x_out[to, :, j * quarter : (j + 1) * quarter] = xbuf[(j // 2) * chips + to, rows, columns]
    leaving.wait()


def step(chips, layer, deps, ids, section_map, g_ref, *refs):
    with_parts = layer > 0
    slopes, refs = refs[:4], refs[4:]
    o_refs, refs = refs[:2], refs[2:]
    v_refs, refs = (refs[:2], refs[2:]) if with_parts else (None, refs)
    refs = refs[deps:]
    part_ref, refs = (refs[0], refs[1:]) if with_parts else (None, refs)
    outs, (gbuf, sbuf, obuf, head_rows, in_sems, out_sems) = refs[:chips], refs[chips : chips + 6]
    cut, width = gbuf.shape[-1], head_rows.shape[-1]
    quarter = cut // 4
    chip, core, side = ids[CHIP], ids[CORE], ids[SIDE]
    section_core, slot, _ = held_at(ids, section_map, layer)
    own = section_core == core
    arriving, leaving = Copies(in_sems), Copies(out_sems)
    if g_ref.shape == gbuf.shape:
        g = [arriving.start(g_ref, gbuf)]
    else:
        g = [arriving.start(rows_place(g_ref, cut, core)(i), gbuf.at[i]) for i in range(gbuf.shape[0])]
    o = [arriving.either(own, o_refs[0].at[slot, r], o_refs[1].at[slot, r], obuf.at[r]) for r in halves(obuf)]
    which = jnp.where(own, 0, 2) + slot
    for j in range(4):
        pl.when(which == j)(pltpu.make_async_copy(slopes[j], sbuf, in_sems.at[-1 + in_sems.shape[0]]).start)
    slope = pltpu.make_async_copy(slopes[0], sbuf, in_sems.at[-1 + in_sems.shape[0]])
    if with_parts:
        vbuf, stage = refs[chips + 6 :]
        v = [arriving.either(own, v_refs[0].at[slot, r], v_refs[1].at[slot, r], vbuf.at[r]) for r in halves(vbuf)]
    for copy in g:
        copy.wait()
    total = product_in(gbuf, obuf, o)
    slope.wait()
    head = (total * sbuf[...]).astype(BF16)
    head_rows[...] = head
    for far, out in enumerate(outs):
        to = lax.rem(chip + far, chips)
        for j in range(4):
            columns = pl.ds(pl.multiple_of((j % 2) * 2 * quarter + side * quarter, quarter), quarter)
            source = gbuf.at[(j // 2) * chips + to, :, columns]
            leaving.start(source, out.at[:, pl.ds(width + j * quarter, quarter)])
        leaving.start(head_rows, out.at[:, pl.ds(0, width)])
    if with_parts:
        product_out(head, vbuf, v, stage, part_ref, leaving)
    leaving.wait()


def reduce_kernel(spread, ids, got_ref, base_ref, out_ref, got, base, stage, sems, out_sems):
    cuts, cut = got.shape[0], got.shape[-1]
    arriving, leaving = Copies(sems), Copies(out_sems)
    arriving.start(rows_place(base_ref, cut, ids[CORE])(ids[TP]), base)
    for i in range(4):
        some = pl.ds(i * (cuts // 4), cuts // 4)
        arriving.start(got_ref.at[some], got.at[some])
    arriving.wait()
    total = got[0].astype(F32)
    for i in range(1, cuts):
        total += got[i].astype(F32)
    stage[...] = (base[...].astype(F32) + total).astype(BF16)
    for i in range(cuts if spread else 1):
        leaving.start(stage, out_ref.at[i] if spread else out_ref)
    leaving.wait()


def carve_kernel(chips, ids, act_mine, act_sib, x_mine, x_sib, *refs):
    outs, sems = refs[:chips], refs[chips]
    chip, core = ids[CHIP], ids[CORE]
    width = act_mine.shape[-1]
    copies = []
    for k, (act, x) in enumerate(((act_mine, x_mine), (act_sib, x_sib))):
        at = core if k == 0 else 1 - core
        for far, out in enumerate(outs):
            to = lax.rem(chip + far, chips)
            for j, source in enumerate((act, x.at[to])):
                target = out.at[at, :, pl.ds(j * width, width)]
                copies.append(pltpu.make_async_copy(source, target, sems.at[k, far, j]))
                copies[-1].start()
    for copy in copies:
        copy.wait()


def pick_kernel(wanted, of_slots, ids, section_map, *refs):
    chips = 4
    count = len(wanted)
    total = (2 if of_slots else count) * chips
    sources, (own_out, sib_out, block, in_sems, sems) = refs[:total], refs[total:]
    core, rep = ids[CORE], ids[REP]
    width = block.shape[-1] // 2
    quarter = width // 4
    for n, layer in enumerate(wanted):
        section_core, slot, far = held_at(ids, section_map, layer)
        at = slot * chips + far if of_slots else n * chips + far
        for j in range(total) if of_slots else range(n * chips, (n + 1) * chips):

            def begin(n=n, j=j, section_core=section_core):
                source = sources[j].at[section_core] if of_slots else sources[j]
                pltpu.make_async_copy(source, block.at[n], in_sems.at[n]).start()

            pl.when(at == j)(begin)
    copies = []
    for n in range(count):
        pltpu.make_async_copy(block.at[n], block.at[n], in_sems.at[n]).wait()
        for k, (out, side) in enumerate(((own_out, core), (sib_out, 1 - core))):
            for j, replica in enumerate((None, 1 - rep, rep)):
                if replica is None:
                    source, target = block.at[n, :, pl.ds(0, width)], out.at[n, :, pl.ds(0, width)]
                else:
                    columns = pl.ds(pl.multiple_of(width + (replica * 2 + side) * quarter, quarter), quarter)
                    source = block.at[n, :, columns]
                    target = out.at[n, :, pl.ds(width + (j - 1) * quarter, quarter)]
                copies.append(pltpu.make_async_copy(source, target, sems.at[n, k, j]))
                copies[-1].start()
    for copy in copies:
        copy.wait()


def gradient_kernel(ids, *refs):
    value_ref, out_ref = refs[-2:]
    width = value_ref.shape[-1]
    first_side = ids[SIDE] == 0

    def factors(parts, mine, theirs):
        wide = jnp.concatenate([part[0][:, :width] for part in parts], axis=0)
        mine, theirs = (jnp.concatenate([ref[k, 0] for k in range(4)], axis=0) for ref in (mine, theirs))
        left = jnp.where(first_side, mine, theirs)
        right = jnp.where(first_side, theirs, mine)
        return jnp.concatenate([left, right], axis=1), wide

    x, act = factors(refs[0:4], refs[4], refs[5])
    g, head = factors(refs[6:10], refs[10], refs[11])
    value_ref[0] = lax.dot_general(x, head, TN, preferred_element_type=F32).astype(BF16)
    out_ref[0] = lax.dot_general(g, act, TN, preferred_element_type=F32).astype(BF16)


def gradients(ids, layers, first, count, forward, backward, before):
    quarter = forward[4].shape[-1]
    piece, width = 2 * quarter, forward[0].shape[-1] - 2 * quarter
    out = jax.ShapeDtypeStruct((layers, piece, width), BF16)
    out_spec = pl.BlockSpec((1, piece, width), lambda l: (first + l, 0, 0))

    def block(array, start):
        if array.ndim == 3:
            return pl.BlockSpec((1,) + array.shape[1:], lambda l: (start + l, 0, 0))
        return pl.BlockSpec((array.shape[0], 1) + array.shape[2:], lambda l: (0, start + l, 0, 0))

    specs = [SMEM] + [block(a, first) for a in forward] + [block(a, 0) for a in backward]
    operands = [ids] + list(forward) + list(backward)
    aliases = {}
    if before is not None:
        aliases = {len(operands): 0, len(operands) + 1: 1}
        operands, specs = operands + list(before), specs + [ANY, ANY]
    return pl.pallas_call(
        gradient_kernel,
        out_shape=(out, out),
        grid=(count,),
        in_specs=specs,
        out_specs=(out_spec, out_spec),
        input_output_aliases=aliases,
        compiler_params=pltpu.CompilerParams(vmem_limit_bytes=VMEM_BYTES),
        cost_estimate=pl.CostEstimate(
            flops=count * 4 * piece * width * 256, bytes_accessed=count * 2400000, transcendentals=0
        ),
    )(*operands)


def per_device(section_map, checkpoint, top_grad, value_weight, out_weight):
    tp_total = lax.axis_size("tp")
    section_total = lax.axis_size("section")
    replica_total = lax.axis_size("rep")
    chips = section_total // 2
    rep, section, tp = (lax.axis_index(name) for name in ("rep", "section", "tp"))
    chip, core, side = section // 2, section % 2, tp % 2
    layers = section_map.shape[1]
    _, _, micro, tokens, model = checkpoint.shape
    slots, width = value_weight.shape[1], value_weight.shape[3]
    rows = micro * tokens
    cut = model // tp_total
    piece = model // (replica_total * section_total)
    v_own, o_own = value_weight[0], out_weight[0]
    x_pair, top_pair = checkpoint[0, 0], top_grad[0]

    ids = jnp.stack([rep, chip, core, side, tp]).astype(jnp.int32)

    chip_of = section_map // 2
    moves = chip_of[:, 1:] - chip_of[:, :-1]
    my_moves = lax.dynamic_index_in_dim(moves, rep, 0, keepdims=False)
    most_moves = jnp.max(moves, axis=0)

    swap = [(i, i ^ 1) for i in range(section_total)]

    def to_sibling(array):
        return lax.ppermute(array, "section", swap)

    def to_replica(array):
        return lax.ppermute(array, "rep", [(0, 1), (1, 0)])

    o_sib, v_sib = to_sibling(o_own), to_sibling(v_own)

    def shape(*dims, dtype=BF16):
        return jax.ShapeDtypeStruct(dims, dtype)

    def in_hbm(*dims):
        return pltpu.HBM(dims, BF16)

    def dma(*dims):
        return pltpu.SemaphoreType.DMA(dims)

    weight_bytes = model * width * 2
    weight_buffer = pltpu.VMEM((model, width), BF16)

    def reduce_slices(got, base, spread):
        count = got.shape[1]
        buffer = pltpu.VMEM((count, cut), BF16)
        return run(
            functools.partial(reduce_kernel, spread),
            (ids, got, base),
            [SMEM, ANY, ANY],
            in_hbm(*got.shape) if spread else in_hbm(count, cut),
            HBM,
            [pltpu.VMEM(got.shape, BF16), buffer, buffer, dma(5), dma(tp_total if spread else 1)],
            got.size * 2,
        )

    def over_tp(parts):
        return lax.all_to_all(parts, "tp", 0, 0, tiled=True)

    def recompute_slot(slot, x, with_parts):
        halves = (shape(tokens, width),) * 2 + (shape(tokens, width, dtype=F32),) * 2
        halves += (shape(chips, tokens, cut),) * 2
        outs = ((in_hbm(tp_total, rows, cut),) if with_parts else ()) + halves
        out_specs = ((HBM,) if with_parts else ()) + (VMEM,) * 6
        scratch = [pltpu.VMEM((tp_total, rows, cut), BF16), weight_buffer]
        scratch += [pltpu.VMEM((rows, width), BF16), pltpu.VMEM((rows, width), F32), dma(tp_total + 4), dma(2)]
        if with_parts:
            scratch += [weight_buffer, pltpu.VMEM((tp_total, rows, cut), BF16)]
        operands = (ids, x, v_own) + ((o_own,) if with_parts else ())
        count = 2 if with_parts else 1
        return run(
            functools.partial(recompute, chips, with_parts, slot),
            operands,
            [SMEM] + [ANY] * (len(operands) - 1),
            outs,
            out_specs,
            scratch,
            count * weight_bytes,
            count * 2 * rows * model * width,
        )

    def along_chips(cuts):
        got = [cuts[0]]
        for far in range(1, chips):
            back = chips - far
            route = [(i, (i + 2 * back) % section_total) for i in range(section_total)]
            got.append(lax.ppermute(cuts[back], "section", route))
        return got

    def carve(act_mine, act_sib, x_mine, x_sib):
        block = in_hbm(2, tokens, width + cut)
        return along_chips(
            run(
                functools.partial(carve_kernel, chips),
                (ids, act_mine, act_sib, x_mine, x_sib),
                [SMEM] + [VMEM] * 4,
                (block,) * chips,
                (HBM,) * chips,
                [dma(2, chips, 2)],
                2 * chips * tokens * (width + cut) * 4,
            )
        )

    def to_owners(sources, wanted, of_slots):
        count = len(wanted)
        out = in_hbm(count, tokens, width + piece)
        own_out, sib_out = run(
            functools.partial(pick_kernel, wanted, of_slots),
            (ids, section_map, *sources),
            [SMEM, SMEM] + [ANY] * len(sources),
            (out, out),
            (HBM,) * 2,
            [pltpu.VMEM((count, tokens, width + cut), BF16), dma(count), dma(count, 2, 3)],
            count * tokens * (width + piece) * 12,
        )
        from_sib = to_sibling(sib_out)
        parts = (own_out, from_sib, to_replica(own_out), to_replica(from_sib))
        half = piece // 2
        mine = jnp.stack([p[:, :, -half:] for p in parts[:2]] + [p[:, :, -2 * half : -half] for p in parts[2:]])
        theirs = lax.ppermute(mine, "tp", [(i, i ^ 1) for i in range(tp_total)])
        return parts + (mine, theirs)

    x_rows = x_pair.reshape(rows, model)
    parts, act_mine_0, act_other_0, slope_mine_0, slope_other_0, x_mine_0, x_other_0 = recompute_slot(0, x_rows, True)
    act_sib_0, slope_sib_0, x_sib_0 = to_sibling(act_other_0), to_sibling(slope_other_0), to_sibling(x_other_0)
    first_got = carve(act_mine_0, act_sib_0, x_mine_0, x_sib_0)
    x_second = over_tp(reduce_slices(over_tp(parts), x_rows, True))
    act_mine_1, act_other_1, slope_mine_1, slope_other_1, x_mine_1, x_other_1 = recompute_slot(
        1, x_second, False
    )
    slope_sib_1, act_sib_1, x_sib_1 = to_sibling(slope_other_1), to_sibling(act_other_1), to_sibling(x_other_1)
    second_got = carve(act_mine_1, act_sib_1, x_mine_1, x_sib_1)
    slopes = (slope_mine_0, slope_mine_1, slope_sib_0, slope_sib_1)

    down = [(i, i - 2) for i in range(2, section_total)]

    def one_layer(layer, g, deps):
        last = layer == 0
        operands = (ids, section_map, g, *slopes, o_own, o_sib)
        operands += (() if last else (v_own, v_sib)) + tuple(deps)
        block = in_hbm(tokens, width + cut)
        outs = (() if last else (in_hbm(tp_total, tokens, cut),)) + (block,) * chips
        scratch = [pltpu.VMEM((tp_total, tokens, cut), BF16), pltpu.VMEM((tokens, width), F32), weight_buffer]
        scratch += [pltpu.VMEM((tokens, width), BF16), dma(tp_total + 5), dma(5 * chips + 2)]
        if not last:
            scratch += [weight_buffer, pltpu.VMEM((tp_total, tokens, cut), BF16)]
        count = 1 if last else 2
        result = run(
            functools.partial(step, chips, layer, len(deps)),
            operands,
            [SMEM, SMEM] + [ANY] * (len(operands) - 2),
            outs,
            (HBM,) * len(outs),
            scratch,
            count * weight_bytes,
            count * 2 * tokens * model * width,
        )
        return (None if last else result[0]), along_chips(result[-chips:])

    g = top_pair
    got_at = [None] * layers
    deps = {layer: [] for layer in range(layers)}
    upper, middle = [3, 4, 5, 6, 7], [1, 2]

    def collect(wanted):
        return to_owners([array for layer in wanted for array in got_at[layer]], wanted, False)

    for layer in reversed(range(layers)):
        if layer < layers - 1:
            deps[layer] += got_at[layer + 1]
        if layer == 6:
            deps[6] += first_got + second_got
        if layer == 5:
            forward = to_owners(first_got + second_got, list(range(layers)), True)
            deps[3] += forward
        if layer == 2:
            upper_all = collect(upper)
            deps[0] += upper_all
        parts, got_at[layer] = one_layer(layer, g, deps[layer])
        if layer == 0:
            break
        got = over_tp(parts)
        my_move, most = my_moves[layer - 1], most_moves[layer - 1]

        def stay(got, base):
            return reduce_slices(got, base, True)

        def go_down(got, base, my_move=my_move, most=most):
            def hop(i, value):
                came = lax.ppermute(value, "section", down)
                return jnp.where(i < my_move, came, value)

            mine = lax.fori_loop(0, most, hop, reduce_slices(got, base, False))
            return jnp.broadcast_to(mine[None], got.shape)

        g = over_tp(lax.cond(most > 0, go_down, stay, got, g))

    middle_all, last_all = collect(middle), collect([0])
    result = gradients(ids, layers, upper[0], len(upper), forward, upper_all, None)
    result = gradients(ids, layers, middle[0], len(middle), forward, middle_all, result)
    return gradients(ids, layers, 0, 1, forward, last_all, result)


def solution(mesh):
    placed = (
        P(),
        P("rep", "section", None, None, None),
        P("rep", None, None, None),
        P("rep", "section", None, "tp"),
        P("rep", "section", None, "tp"),
    )
    return jax.shard_map(
        per_device,
        mesh=mesh,
        in_specs=placed,
        out_specs=(P(None, ("rep", "section"), "tp"), P(None, ("rep", "section"), "tp")),
        check_vma=False,
    )
```

```python
import functools

import jax
import jax.numpy as jnp
from jax import lax
from jax.experimental import pallas as pl
from jax.experimental.pallas import tpu as pltpu
from jax.sharding import PartitionSpec as P

BF16 = jnp.bfloat16
F32 = jnp.float32
VMEM_BYTES = 64 * 1024 * 1024
NT = (((1,), (1,)), ((), ()))
TN = (((0,), (0,)), ((), ()))
ANY = pl.BlockSpec(memory_space=pl.ANY)
HBM = pl.BlockSpec(memory_space=pltpu.HBM)
SMEM = pl.BlockSpec(memory_space=pltpu.SMEM)
VMEM = pl.BlockSpec(memory_space=pltpu.VMEM)


REP, CHIP, CORE, SIDE, TP = range(5)


def held_at(ids, section_map, layer):
    section = section_map[ids[REP], layer]
    slot = jnp.int32(0)
    if layer > 0:
        slot = (section_map[ids[REP], layer - 1] == section).astype(jnp.int32)
    chips = 4
    return lax.rem(section, 2), slot, lax.rem(section // 2 - ids[CHIP] + chips, chips)


def silu_slope(preact):
    sigma = jax.nn.sigmoid(preact)
    return sigma * (1.0 + preact * (1.0 - sigma))


def run(kernel, operands, specs, outs, out_specs, scratch, bytes_moved, flops=0):
    return pl.pallas_call(
        kernel,
        out_shape=outs,
        in_specs=specs,
        out_specs=out_specs,
        scratch_shapes=scratch,
        compiler_params=pltpu.CompilerParams(vmem_limit_bytes=VMEM_BYTES),
        cost_estimate=pl.CostEstimate(flops=flops, bytes_accessed=bytes_moved, transcendentals=0),
    )(*operands)


def rows_place(ref, cut, core):
    if len(ref.shape) == 3 and ref.shape[-1] == cut:
        return lambda i: ref.at[i]
    columns = lambda i: pl.ds(pl.multiple_of(i * cut, cut), cut)
    if len(ref.shape) == 2:
        return lambda i: ref.at[:, columns(i)]
    return lambda i: ref.at[core, :, columns(i)]


class Copies:
    def __init__(self, sems):
        self.sems, self.all = sems, []

    def start(self, source, target, condition=None):
        copy = pltpu.make_async_copy(source, target, self.sems.at[len(self.all)])
        if condition is None:
            copy.start()
        else:
            pl.when(condition)(copy.start)
        self.all.append(copy)
        return copy

    def either(self, condition, first, second, target):
        sem = self.sems.at[len(self.all)]
        pl.when(condition)(lambda: pltpu.make_async_copy(first, target, sem).start())
        pl.when(jnp.logical_not(condition))(lambda: pltpu.make_async_copy(second, target, sem).start())
        self.all.append(pltpu.make_async_copy(first, target, sem))
        return self.all[-1]

    def wait(self):
        for copy in self.all:
            copy.wait()


def halves(ref):
    step = ref.shape[0] // 2
    return [pl.ds(i * step, step) for i in range(2)]


def product_in(rows, weight, waits):
    cuts, cut = rows.shape[0], rows.shape[-1]
    total = None
    for i in range(cuts):
        if i % (cuts // len(waits)) == 0:
            waits[i // (cuts // len(waits))].wait()
        part = jnp.dot(rows[i], weight[i * cut : (i + 1) * cut, :], preferred_element_type=F32)
        total = part if total is None else total + part
    return total


def product_out(rows, weight, waits, stage, part_ref, out):
    cuts, cut = stage.shape[0], stage.shape[-1]
    group = cuts // len(waits)
    for i in range(cuts):
        if i % group == 0:
            waits[i // group].wait()
        part = lax.dot_general(rows, weight[i * cut : (i + 1) * cut, :], NT, preferred_element_type=F32)
        stage[i] = part.astype(BF16)
        if i % group == group - 1:
            cuts_done = pl.ds(i - group + 1, group)
            out.start(stage.at[cuts_done], part_ref.at[cuts_done])


def recompute(chips, with_parts, slot, deps, ids, x_ref, v_ref, *refs):
    o_ref, refs = (refs[0], refs[1:]) if with_parts else (None, refs)
    refs = refs[deps:]
    part_ref, refs = (refs[0], refs[1:]) if with_parts else (None, refs)
    outs, (xbuf, vbuf, act_rows, slope_rows, in_sems, out_sems) = refs[:6], refs[6:12]
    cuts, cut = xbuf.shape[0], xbuf.shape[-1]
    core, side = ids[CORE], ids[SIDE]
    arriving, leaving = Copies(in_sems), Copies(out_sems)
    x = [arriving.start(rows_place(x_ref, cut, core)(i), xbuf.at[i]) for i in range(cuts)]
    v = [arriving.start(v_ref.at[slot, rows], vbuf.at[rows]) for rows in halves(vbuf)]
    if with_parts:
        obuf, stage = refs[12:]
        o = [arriving.start(o_ref.at[slot, rows], obuf.at[rows]) for rows in halves(obuf)]
    for copy in x:
        copy.wait()
    pre = product_in(xbuf, vbuf, v)
    act = jax.nn.silu(pre).astype(BF16)
    if with_parts:
        product_out(act, obuf, o, stage, part_ref, leaving)
    act_rows[...] = act
    slope_rows[...] = silu_slope(pre)
    half = outs[0].shape[0]
    quarter = cut // 4
    for k, which in enumerate((core, 1 - core)):
        rows = pl.ds(pl.multiple_of(which * half, half), half)
        act_out, slope_out, x_out = outs[k], outs[2 + k], outs[4 + k]
        act_out[...] = act_rows[rows, :]
        slope_out[...] = slope_rows[rows, :]
        for to in range(chips):
            for j in range(4):
                columns = pl.ds(pl.multiple_of((j % 2) * 2 * quarter + side * quarter, quarter), quarter)
                x_out[to, :, j * quarter : (j + 1) * quarter] = xbuf[(j // 2) * chips + to, rows, columns]
    leaving.wait()


def step(chips, layer, deps, ids, section_map, g_ref, *refs):
    with_parts = layer > 0
    slopes, refs = refs[:4], refs[4:]
    o_refs, refs = refs[:2], refs[2:]
    v_refs, refs = (refs[:2], refs[2:]) if with_parts else (None, refs)
    refs = refs[deps:]
    part_ref, refs = (refs[0], refs[1:]) if with_parts else (None, refs)
    outs, (gbuf, sbuf, obuf, head_rows, in_sems, out_sems) = refs[:chips], refs[chips : chips + 6]
    cut, width = gbuf.shape[-1], head_rows.shape[-1]
    quarter = cut // 4
    chip, core, side = ids[CHIP], ids[CORE], ids[SIDE]
    section_core, slot, _ = held_at(ids, section_map, layer)
    own = section_core == core
    arriving, leaving = Copies(in_sems), Copies(out_sems)
    if g_ref.shape == gbuf.shape:
        g = [arriving.start(g_ref, gbuf)]
    else:
        g = [arriving.start(rows_place(g_ref, cut, core)(i), gbuf.at[i]) for i in range(gbuf.shape[0])]
    o = [arriving.either(own, o_refs[0].at[slot, r], o_refs[1].at[slot, r], obuf.at[r]) for r in halves(obuf)]
    which = jnp.where(own, 0, 2) + slot
    for j in range(4):
        pl.when(which == j)(pltpu.make_async_copy(slopes[j], sbuf, in_sems.at[-1 + in_sems.shape[0]]).start)
    slope = pltpu.make_async_copy(slopes[0], sbuf, in_sems.at[-1 + in_sems.shape[0]])
    if with_parts:
        vbuf, stage = refs[chips + 6 :]
        v = [arriving.either(own, v_refs[0].at[slot, r], v_refs[1].at[slot, r], vbuf.at[r]) for r in halves(vbuf)]
    for copy in g:
        copy.wait()
    total = product_in(gbuf, obuf, o)
    slope.wait()
    head = (total * sbuf[...]).astype(BF16)
    head_rows[...] = head
    for far, out in enumerate(outs):
        to = lax.rem(chip + far, chips)
        for j in range(4):
            columns = pl.ds(pl.multiple_of((j % 2) * 2 * quarter + side * quarter, quarter), quarter)
            source = gbuf.at[(j // 2) * chips + to, :, columns]
            leaving.start(source, out.at[:, pl.ds(width + j * quarter, quarter)])
        leaving.start(head_rows, out.at[:, pl.ds(0, width)])
    if with_parts:
        product_out(head, vbuf, v, stage, part_ref, leaving)
    leaving.wait()


def reduce_kernel(spread, ids, got_ref, base_ref, out_ref, got, base, stage, sems, out_sems):
    cuts, cut = got.shape[0], got.shape[-1]
    arriving, leaving = Copies(sems), Copies(out_sems)
    arriving.start(rows_place(base_ref, cut, ids[CORE])(ids[TP]), base)
    for i in range(4):
        some = pl.ds(i * (cuts // 4), cuts // 4)
        arriving.start(got_ref.at[some], got.at[some])
    arriving.wait()
    total = got[0].astype(F32)
    for i in range(1, cuts):
        total += got[i].astype(F32)
    stage[...] = (base[...].astype(F32) + total).astype(BF16)
    for i in range(cuts if spread else 1):
        leaving.start(stage, out_ref.at[i] if spread else out_ref)
    leaving.wait()


def settle_kernel(layer, ids, section_map, kept_ref, came_ref, out_ref, stage, sems, out_sems):
    rep = ids[REP]
    moved = section_map[rep, layer] // 2 > section_map[rep, layer - 1] // 2
    arriving, leaving = Copies(sems), Copies(out_sems)
    arriving.either(moved, came_ref, kept_ref, stage)
    arriving.wait()
    for i in range(out_ref.shape[0]):
        leaving.start(stage, out_ref.at[i])
    leaving.wait()


def carve_kernel(chips, ids, act_mine, act_sib, x_mine, x_sib, *refs):
    outs, sems = refs[:chips], refs[chips]
    chip, core = ids[CHIP], ids[CORE]
    width = act_mine.shape[-1]
    copies = []
    for k, (act, x) in enumerate(((act_mine, x_mine), (act_sib, x_sib))):
        at = core if k == 0 else 1 - core
        for far, out in enumerate(outs):
            to = lax.rem(chip + far, chips)
            for j, source in enumerate((act, x.at[to])):
                target = out.at[at, :, pl.ds(j * width, width)]
                copies.append(pltpu.make_async_copy(source, target, sems.at[k, far, j]))
                copies[-1].start()
    for copy in copies:
        copy.wait()


def pick_kernel(wanted, of_slots, deps, ids, section_map, *refs):
    chips = 4
    count = len(wanted)
    total = (2 if of_slots else count) * chips
    sources, (own_out, sib_out, rep_out, block, in_sems, sems) = refs[:total], refs[total + deps :]
    core, rep = ids[CORE], ids[REP]
    width = block.shape[-1] // 2
    quarter = width // 4
    for n, layer in enumerate(wanted):
        section_core, slot, far = held_at(ids, section_map, layer)
        at = slot * chips + far if of_slots else n * chips + far
        for j in range(total) if of_slots else range(n * chips, (n + 1) * chips):

            def begin(n=n, j=j, section_core=section_core):
                source = sources[j].at[section_core] if of_slots else sources[j]
                pltpu.make_async_copy(source, block.at[n], in_sems.at[n]).start()

            pl.when(at == j)(begin)
    plan = ((own_out, [(rep, core)]), (sib_out, [(rep, 1 - core)]), (rep_out, [(1 - rep, core), (1 - rep, 1 - core)]))
    leaving = Copies(sems)
    for n in range(count):
        pltpu.make_async_copy(block.at[n], block.at[n], in_sems.at[n]).wait()
        for out, pieces in plan:
            leaving.start(block.at[n, :, pl.ds(0, width)], out.at[n, :, pl.ds(0, width)])
            for j, (replica, side) in enumerate(pieces):
                columns = pl.ds(pl.multiple_of(width + (replica * 2 + side) * quarter, quarter), quarter)
                leaving.start(block.at[n, :, columns], out.at[n, :, pl.ds(width + j * quarter, quarter)])
    leaving.wait()


def gradient_kernel(ids, *refs):
    value_ref, out_ref = refs[-2:]
    width = value_ref.shape[-1]
    first_side = ids[SIDE] == 0

    def factors(parts, mine, theirs):
        wide = jnp.concatenate([part[0][:, :width] for part in parts], axis=0)
        mine, theirs = (jnp.concatenate([ref[k, 0] for k in range(4)], axis=0) for ref in (mine, theirs))
        left = jnp.where(first_side, mine, theirs)
        right = jnp.where(first_side, theirs, mine)
        return jnp.concatenate([left, right], axis=1), wide

    x, act = factors(refs[0:4], refs[4], refs[5])
    g, head = factors(refs[6:10], refs[10], refs[11])
    value_ref[0] = lax.dot_general(x, head, TN, preferred_element_type=F32).astype(BF16)
    out_ref[0] = lax.dot_general(g, act, TN, preferred_element_type=F32).astype(BF16)


def gradients(ids, layers, first, count, forward, backward, before):
    quarter = forward[4].shape[-1]
    piece, width = 2 * quarter, forward[0].shape[-1] - quarter
    out = jax.ShapeDtypeStruct((layers, piece, width), BF16)
    out_spec = pl.BlockSpec((1, piece, width), lambda l: (first + l, 0, 0))

    def block(array, start):
        if array.ndim == 3:
            return pl.BlockSpec((1,) + array.shape[1:], lambda l: (start + l, 0, 0))
        return pl.BlockSpec((array.shape[0], 1) + array.shape[2:], lambda l: (0, start + l, 0, 0))

    specs = [SMEM] + [block(a, first) for a in forward] + [block(a, 0) for a in backward]
    operands = [ids] + list(forward) + list(backward)
    aliases = {}
    if before is not None:
        aliases = {len(operands): 0, len(operands) + 1: 1}
        operands, specs = operands + list(before), specs + [ANY, ANY]
    return pl.pallas_call(
        gradient_kernel,
        out_shape=(out, out),
        grid=(count,),
        in_specs=specs,
        out_specs=(out_spec, out_spec),
        input_output_aliases=aliases,
        compiler_params=pltpu.CompilerParams(vmem_limit_bytes=VMEM_BYTES),
        cost_estimate=pl.CostEstimate(
            flops=count * 4 * piece * width * 256, bytes_accessed=count * 2400000, transcendentals=0
        ),
    )(*operands)


def per_device(section_map, checkpoint, top_grad, value_weight, out_weight):
    tp_total = lax.axis_size("tp")
    section_total = lax.axis_size("section")
    replica_total = lax.axis_size("rep")
    chips = section_total // 2
    rep, section, tp = (lax.axis_index(name) for name in ("rep", "section", "tp"))
    chip, core, side = section // 2, section % 2, tp % 2
    layers = section_map.shape[1]
    _, _, micro, tokens, model = checkpoint.shape
    slots, width = value_weight.shape[1], value_weight.shape[3]
    rows = micro * tokens
    cut = model // tp_total
    piece = model // (replica_total * section_total)
    v_own, o_own = value_weight[0], out_weight[0]
    x_pair, top_pair = checkpoint[0, 0], top_grad[0]

    ids = jnp.stack([rep, chip, core, side, tp]).astype(jnp.int32)

    chip_of = section_map // 2
    moves = chip_of[:, 1:] - chip_of[:, :-1]
    most_moves = jnp.max(moves, axis=0)

    swap = [(i, i ^ 1) for i in range(section_total)]

    def to_sibling(array):
        return lax.ppermute(array, "section", swap)

    def to_replica(array):
        return lax.ppermute(array, "rep", [(0, 1), (1, 0)])

    o_sib, v_sib = to_sibling(o_own), to_sibling(v_own)

    def shape(*dims, dtype=BF16):
        return jax.ShapeDtypeStruct(dims, dtype)

    def in_hbm(*dims):
        return pltpu.HBM(dims, BF16)

    def dma(*dims):
        return pltpu.SemaphoreType.DMA(dims)

    weight_bytes = model * width * 2
    weight_buffer = pltpu.VMEM((model, width), BF16)

    def reduce_slices(got, base, spread):
        count = got.shape[1]
        buffer = pltpu.VMEM((count, cut), BF16)
        return run(
            functools.partial(reduce_kernel, spread),
            (ids, got, base),
            [SMEM, ANY, ANY],
            in_hbm(*got.shape) if spread else in_hbm(count, cut),
            HBM,
            [pltpu.VMEM(got.shape, BF16), buffer, buffer, dma(5), dma(tp_total if spread else 1)],
            got.size * 2,
        )

    def over_tp(parts):
        return lax.all_to_all(parts, "tp", 0, 0, tiled=True)

    def recompute_slot(slot, x, with_parts, deps=()):
        halves = (shape(tokens, width),) * 2 + (shape(tokens, width, dtype=F32),) * 2
        halves += (shape(chips, tokens, cut),) * 2
        outs = ((in_hbm(tp_total, rows, cut),) if with_parts else ()) + halves
        out_specs = ((HBM,) if with_parts else ()) + (VMEM,) * 6
        scratch = [pltpu.VMEM((tp_total, rows, cut), BF16), weight_buffer]
        scratch += [pltpu.VMEM((rows, width), BF16), pltpu.VMEM((rows, width), F32), dma(tp_total + 4), dma(2)]
        if with_parts:
            scratch += [weight_buffer, pltpu.VMEM((tp_total, rows, cut), BF16)]
        operands = (ids, x, v_own) + ((o_own,) if with_parts else ()) + tuple(deps)
        count = 2 if with_parts else 1
        return run(
            functools.partial(recompute, chips, with_parts, slot, len(deps)),
            operands,
            [SMEM] + [ANY] * (len(operands) - 1),
            outs,
            out_specs,
            scratch,
            count * weight_bytes,
            count * 2 * rows * model * width,
        )

    def along_chips(cuts):
        got = [cuts[0]]
        for far in range(1, chips):
            back = chips - far
            route = [(i, (i + 2 * back) % section_total) for i in range(section_total)]
            got.append(lax.ppermute(cuts[back], "section", route))
        return got

    def carve(act_mine, act_sib, x_mine, x_sib):
        block = in_hbm(2, tokens, width + cut)
        return run(
            functools.partial(carve_kernel, chips),
            (ids, act_mine, act_sib, x_mine, x_sib),
            [SMEM] + [VMEM] * 4,
            (block,) * chips,
            (HBM,) * chips,
            [dma(2, chips, 2)],
            2 * chips * tokens * (width + cut) * 4,
        )

    def to_owners(sources, wanted, of_slots, deps=()):
        count = len(wanted)
        quarter = piece // 2
        alone, both = in_hbm(count, tokens, width + quarter), in_hbm(count, tokens, width + 2 * quarter)
        own_out, sib_out, rep_out = run(
            functools.partial(pick_kernel, wanted, of_slots, len(deps)),
            (ids, section_map, *sources, *deps),
            [SMEM, SMEM] + [ANY] * (len(sources) + len(deps)),
            (alone, alone, both),
            (HBM,) * 3,
            [pltpu.VMEM((count, tokens, width + cut), BF16), dma(count), dma(7 * count)],
            count * tokens * (width + piece) * 12,
        )
        from_rep = to_replica(rep_out)
        parts = (own_out, to_sibling(sib_out), from_rep, to_sibling(from_rep))
        starts = (width, width, width, width + quarter)
        mine = jnp.stack([p[:, :, i : i + quarter] for p, i in zip(parts, starts)])
        theirs = lax.ppermute(mine, "tp", [(i, i ^ 1) for i in range(tp_total)])
        return parts + (mine, theirs)

    x_rows = x_pair.reshape(rows, model)
    parts, act_mine_0, act_other_0, slope_mine_0, slope_other_0, x_mine_0, x_other_0 = recompute_slot(0, x_rows, True)
    act_sib_0, slope_sib_0, x_sib_0 = to_sibling(act_other_0), to_sibling(slope_other_0), to_sibling(x_other_0)
    first_cuts = carve(act_mine_0, act_sib_0, x_mine_0, x_sib_0)
    first_got = along_chips(first_cuts)
    x_second = over_tp(reduce_slices(over_tp(parts), x_rows, True))
    act_mine_1, act_other_1, slope_mine_1, slope_other_1, x_mine_1, x_other_1 = recompute_slot(
        1, x_second, False, first_cuts
    )
    slope_sib_1, act_sib_1, x_sib_1 = to_sibling(slope_other_1), to_sibling(act_other_1), to_sibling(x_other_1)
    second_got = along_chips(carve(act_mine_1, act_sib_1, x_mine_1, x_sib_1))
    slopes = (slope_mine_0, slope_mine_1, slope_sib_0, slope_sib_1)

    down = [(i, i - 2) for i in range(2, section_total)]

    def one_layer(layer, g, deps):
        last = layer == 0
        operands = (ids, section_map, g, *slopes, o_own, o_sib)
        operands += (() if last else (v_own, v_sib)) + tuple(deps)
        block = in_hbm(tokens, width + cut)
        outs = (() if last else (in_hbm(tp_total, tokens, cut),)) + (block,) * chips
        scratch = [pltpu.VMEM((tp_total, tokens, cut), BF16), pltpu.VMEM((tokens, width), F32), weight_buffer]
        scratch += [pltpu.VMEM((tokens, width), BF16), dma(tp_total + 5), dma(5 * chips + 2)]
        if not last:
            scratch += [weight_buffer, pltpu.VMEM((tp_total, tokens, cut), BF16)]
        count = 1 if last else 2
        result = run(
            functools.partial(step, chips, layer, len(deps)),
            operands,
            [SMEM, SMEM] + [ANY] * (len(operands) - 2),
            outs,
            (HBM,) * len(outs),
            scratch,
            count * weight_bytes,
            count * 2 * tokens * model * width,
        )
        return (None if last else result[0]), along_chips(result[-chips:])

    g = top_pair
    got_at = [None] * layers
    deps = {layer: [] for layer in range(layers)}
    upper, middle = [3, 4, 5, 6, 7], [1, 2]

    def collect(wanted, deps=()):
        return to_owners([array for layer in wanted for array in got_at[layer]], wanted, False, deps)

    for layer in reversed(range(layers)):
        if layer < layers - 1:
            deps[layer] += got_at[layer + 1]
        if layer == 7:
            deps[7] += first_got
        if layer == 5:
            deps[5] += second_got
        if layer == 4:
            forward = to_owners(first_got + second_got, list(range(layers)), True)
            deps[3] += forward[:4]
        if layer == 2:
            upper_all = collect(upper)
            deps[0] += upper_all[:4]
        parts, got_at[layer] = one_layer(layer, g, deps[layer])
        if layer == 0:
            break
        got = over_tp(parts)
        most = most_moves[layer - 1]

        def stay(got, base):
            return reduce_slices(got, base, True)

        def settle(kept, came, layer=layer):
            return run(
                functools.partial(settle_kernel, layer),
                (ids, section_map, kept, came),
                [SMEM, SMEM, ANY, ANY],
                in_hbm(tp_total, tokens, cut),
                HBM,
                [pltpu.VMEM((tokens, cut), BF16), dma(1), dma(tp_total)],
                tp_total * tokens * cut * 2,
            )

        def go_one(got, base):
            mine = reduce_slices(got, base, False)
            return settle(mine, lax.ppermute(mine, "section", down))

        def go_far(got, base, layer=layer, most=most):
            mine = reduce_slices(got, base, False)
            my_move = lax.dynamic_index_in_dim(moves, rep, 0, keepdims=False)[layer - 1]

            def hop(i, value):
                came = lax.ppermute(value, "section", down)
                return jnp.where(i < my_move, came, value)

            mine = lax.fori_loop(0, most, hop, mine)
            return settle(mine, mine)

        g = over_tp(lax.switch(jnp.minimum(most, 2), (stay, go_one, go_far), got, g))

    middle_all = collect(middle)
    result = gradients(ids, layers, upper[0], len(upper), forward, upper_all, None)
    result = gradients(ids, layers, middle[0], len(middle), forward, middle_all, result)
    last_all = collect([0], result)
    return gradients(ids, layers, 0, 1, forward, last_all, result)


def solution(mesh):
    placed = (
        P(),
        P("rep", "section", None, None, None),
        P("rep", None, None, None),
        P("rep", "section", None, "tp"),
        P("rep", "section", None, "tp"),
    )
    return jax.shard_map(
        per_device,
        mesh=mesh,
        in_specs=placed,
        out_specs=(P(None, ("rep", "section"), "tp"), P(None, ("rep", "section"), "tp")),
        check_vma=False,
    )
```

```python
import functools

import jax
import jax.numpy as jnp
from jax import lax
from jax.experimental import pallas as pl
from jax.experimental.pallas import tpu as pltpu
from jax.sharding import PartitionSpec as P

BF16 = jnp.bfloat16
F32 = jnp.float32
VMEM_BYTES = 64 * 1024 * 1024
NT = (((1,), (1,)), ((), ()))
TN = (((0,), (0,)), ((), ()))
ANY = pl.BlockSpec(memory_space=pl.ANY)
HBM = pl.BlockSpec(memory_space=pltpu.HBM)
SMEM = pl.BlockSpec(memory_space=pltpu.SMEM)
VMEM = pl.BlockSpec(memory_space=pltpu.VMEM)


REP, CHIP, CORE, SIDE, TP = range(5)


def held_at(ids, section_map, layer):
    section = section_map[ids[REP], layer]
    slot = jnp.int32(0)
    if layer > 0:
        slot = (section_map[ids[REP], layer - 1] == section).astype(jnp.int32)
    chips = 4
    return lax.rem(section, 2), slot, lax.rem(section // 2 - ids[CHIP] + chips, chips)


def silu_slope(preact):
    sigma = jax.nn.sigmoid(preact)
    return sigma * (1.0 + preact * (1.0 - sigma))


def run(kernel, operands, specs, outs, out_specs, scratch, bytes_moved, flops=0):
    return pl.pallas_call(
        kernel,
        out_shape=outs,
        in_specs=specs,
        out_specs=out_specs,
        scratch_shapes=scratch,
        compiler_params=pltpu.CompilerParams(vmem_limit_bytes=VMEM_BYTES),
        cost_estimate=pl.CostEstimate(flops=flops, bytes_accessed=bytes_moved, transcendentals=0),
    )(*operands)


def rows_place(ref, cut, core):
    if len(ref.shape) == 3 and ref.shape[-1] == cut:
        return lambda i: ref.at[i]
    columns = lambda i: pl.ds(pl.multiple_of(i * cut, cut), cut)
    if len(ref.shape) == 2:
        return lambda i: ref.at[:, columns(i)]
    return lambda i: ref.at[core, :, columns(i)]


class Copies:
    def __init__(self, sems):
        self.sems, self.all = sems, []

    def start(self, source, target, condition=None):
        copy = pltpu.make_async_copy(source, target, self.sems.at[len(self.all)])
        if condition is None:
            copy.start()
        else:
            pl.when(condition)(copy.start)
        self.all.append(copy)
        return copy

    def either(self, condition, first, second, target):
        sem = self.sems.at[len(self.all)]
        pl.when(condition)(lambda: pltpu.make_async_copy(first, target, sem).start())
        pl.when(jnp.logical_not(condition))(lambda: pltpu.make_async_copy(second, target, sem).start())
        self.all.append(pltpu.make_async_copy(first, target, sem))
        return self.all[-1]

    def wait(self):
        for copy in self.all:
            copy.wait()


def halves(ref):
    step = ref.shape[0] // 2
    return [pl.ds(i * step, step) for i in range(2)]


def product_in(rows, weight, waits):
    cuts, cut = rows.shape[0], rows.shape[-1]
    total = None
    for i in range(cuts):
        if i % (cuts // len(waits)) == 0:
            waits[i // (cuts // len(waits))].wait()
        part = jnp.dot(rows[i], weight[i * cut : (i + 1) * cut, :], preferred_element_type=F32)
        total = part if total is None else total + part
    return total


def product_out(rows, weight, waits, stage, part_ref, out):
    cuts, cut = stage.shape[0], stage.shape[-1]
    group = cuts // len(waits)
    for i in range(cuts):
        if i % group == 0:
            waits[i // group].wait()
        part = lax.dot_general(rows, weight[i * cut : (i + 1) * cut, :], NT, preferred_element_type=F32)
        stage[i] = part.astype(BF16)
        if i % group == group - 1:
            cuts_done = pl.ds(i - group + 1, group)
            out.start(stage.at[cuts_done], part_ref.at[cuts_done])


def recompute(chips, with_parts, slot, deps, ids, x_ref, v_ref, *refs):
    o_ref, refs = (refs[0], refs[1:]) if with_parts else (None, refs)
    refs = refs[deps:]
    part_ref, refs = (refs[0], refs[1:]) if with_parts else (None, refs)
    outs, (xbuf, vbuf, act_rows, slope_rows, in_sems, out_sems) = refs[:6], refs[6:12]
    cuts, cut = xbuf.shape[0], xbuf.shape[-1]
    core, side = ids[CORE], ids[SIDE]
    arriving, leaving = Copies(in_sems), Copies(out_sems)
    x = [arriving.start(rows_place(x_ref, cut, core)(i), xbuf.at[i]) for i in range(cuts)]
    v = [arriving.start(v_ref.at[slot, rows], vbuf.at[rows]) for rows in halves(vbuf)]
    if with_parts:
        obuf, stage = refs[12:]
        o = [arriving.start(o_ref.at[slot, rows], obuf.at[rows]) for rows in halves(obuf)]
    for copy in x:
        copy.wait()
    pre = product_in(xbuf, vbuf, v)
    act = jax.nn.silu(pre).astype(BF16)
    if with_parts:
        product_out(act, obuf, o, stage, part_ref, leaving)
    act_rows[...] = act
    slope_rows[...] = silu_slope(pre)
    half = outs[0].shape[0]
    quarter = cut // 4
    for k, which in enumerate((core, 1 - core)):
        rows = pl.ds(pl.multiple_of(which * half, half), half)
        act_out, slope_out, x_out = outs[k], outs[2 + k], outs[4 + k]
        act_out[...] = act_rows[rows, :]
        slope_out[...] = slope_rows[rows, :]
        for to in range(chips):
            for j in range(4):
                columns = pl.ds(pl.multiple_of((j % 2) * 2 * quarter + side * quarter, quarter), quarter)
                x_out[to, :, j * quarter : (j + 1) * quarter] = xbuf[(j // 2) * chips + to, rows, columns]
    leaving.wait()


def step(chips, layer, deps, ids, section_map, g_ref, *refs):
    with_parts = layer > 0
    slopes, refs = refs[:4], refs[4:]
    o_refs, refs = refs[:2], refs[2:]
    v_refs, refs = (refs[:2], refs[2:]) if with_parts else (None, refs)
    refs = refs[deps:]
    part_ref, refs = (refs[0], refs[1:]) if with_parts else (None, refs)
    outs, (gbuf, sbuf, obuf, pay, in_sems, out_sems) = refs[:chips], refs[chips : chips + 6]
    cut, width = gbuf.shape[-1], sbuf.shape[-1]
    span = (pay.shape[-1] - width) // 4
    chip, core, side = ids[CHIP], ids[CORE], ids[SIDE]
    section_core, slot, _ = held_at(ids, section_map, layer)
    own = section_core == core
    arriving, leaving = Copies(in_sems), Copies(out_sems)
    if g_ref.shape == gbuf.shape:
        g = [arriving.start(g_ref, gbuf)]
    else:
        g = [arriving.start(rows_place(g_ref, cut, core)(i), gbuf.at[i]) for i in range(gbuf.shape[0])]
    o = [arriving.either(own, o_refs[0].at[slot, r], o_refs[1].at[slot, r], obuf.at[r]) for r in halves(obuf)]
    which = jnp.where(own, 0, 2) + slot
    for j in range(4):
        pl.when(which == j)(pltpu.make_async_copy(slopes[j], sbuf, in_sems.at[-1 + in_sems.shape[0]]).start)
    slope = pltpu.make_async_copy(slopes[0], sbuf, in_sems.at[-1 + in_sems.shape[0]])
    if with_parts:
        vbuf, stage = refs[chips + 6 :]
        v = [arriving.either(own, v_refs[0].at[slot, r], v_refs[1].at[slot, r], vbuf.at[r]) for r in halves(vbuf)]
    for copy in g:
        copy.wait()
    for far in range(chips):
        to = lax.rem(chip + far, chips)
        for j in range(4):
            start = (j % 2) * (cut // 2) + (0 if span == cut // 2 else side * span)
            columns = pl.ds(start if span == cut // 2 else pl.multiple_of(start, span), span)
            pay[far, :, width + j * span : width + (j + 1) * span] = gbuf[(j // 2) * chips + to, :, columns]
    total = product_in(gbuf, obuf, o)
    slope.wait()
    head = (total * sbuf[...]).astype(BF16)
    for far, out in enumerate(outs):
        pay[far, :, :width] = head
        leaving.start(pay.at[far], out)
    if with_parts:
        product_out(head, vbuf, v, stage, part_ref, leaving)
    leaving.wait()


def reduce_kernel(spread, deps, ids, got_ref, base_ref, *refs):
    out_ref, got, base, stage, sems, out_sems = refs[deps:]
    cuts, cut = got.shape[0], got.shape[-1]
    arriving, leaving = Copies(sems), Copies(out_sems)
    arriving.start(rows_place(base_ref, cut, ids[CORE])(ids[TP]), base)
    for i in range(4):
        some = pl.ds(i * (cuts // 4), cuts // 4)
        arriving.start(got_ref.at[some], got.at[some])
    arriving.wait()
    total = got[0].astype(F32)
    for i in range(1, cuts):
        total += got[i].astype(F32)
    stage[...] = (base[...].astype(F32) + total).astype(BF16)
    for i in range(cuts if spread else 1):
        leaving.start(stage, out_ref.at[i] if spread else out_ref)
    leaving.wait()


def settle_kernel(layer, ids, section_map, kept_ref, came_ref, out_ref, stage, sems, out_sems):
    rep = ids[REP]
    moved = section_map[rep, layer] // 2 > section_map[rep, layer - 1] // 2
    arriving, leaving = Copies(sems), Copies(out_sems)
    arriving.either(moved, came_ref, kept_ref, stage)
    arriving.wait()
    for i in range(out_ref.shape[0]):
        leaving.start(stage, out_ref.at[i])
    leaving.wait()


def carve_kernel(chips, ids, act_mine, act_sib, x_mine, x_sib, *refs):
    outs, sems = refs[:chips], refs[chips]
    chip, core = ids[CHIP], ids[CORE]
    width = act_mine.shape[-1]
    copies = []
    for k, (act, x) in enumerate(((act_mine, x_mine), (act_sib, x_sib))):
        at = core if k == 0 else 1 - core
        for far, out in enumerate(outs):
            to = lax.rem(chip + far, chips)
            for j, source in enumerate((act, x.at[to])):
                target = out.at[at, :, pl.ds(j * width, width)]
                copies.append(pltpu.make_async_copy(source, target, sems.at[k, far, j]))
                copies[-1].start()
    for copy in copies:
        copy.wait()


def pick_kernel(wanted, of_slots, deps, ids, section_map, *refs):
    chips = 4
    count = len(wanted)
    total = (2 if of_slots else count) * chips
    sources, (own_out, sib_out, rep_out, block, in_sems, sems) = refs[:total], refs[total + deps :]
    core, rep = ids[CORE], ids[REP]
    width = 2 * sib_out.shape[-1] - rep_out.shape[-1]
    span = rep_out.shape[-1] - sib_out.shape[-1]
    for n, layer in enumerate(wanted):
        section_core, slot, far = held_at(ids, section_map, layer)
        at = slot * chips + far if of_slots else n * chips + far
        for j in range(total) if of_slots else range(n * chips, (n + 1) * chips):

            def begin(n=n, j=j, section_core=section_core):
                source = sources[j].at[section_core] if of_slots else sources[j]
                pltpu.make_async_copy(source, block.at[n], in_sems.at[n]).start()

            pl.when(at == j)(begin)
    plan = ((own_out, [(rep, core)]), (sib_out, [(rep, 1 - core)]), (rep_out, [(1 - rep, core), (1 - rep, 1 - core)]))
    leaving = Copies(sems)
    for n in range(count):
        pltpu.make_async_copy(block.at[n], block.at[n], in_sems.at[n]).wait()
        for out, pieces in plan:
            leaving.start(block.at[n, :, pl.ds(0, width)], out.at[n, :, pl.ds(0, width)])
            for j, (replica, side) in enumerate(pieces):
                columns = pl.ds(pl.multiple_of(width + (replica * 2 + side) * span, span), span)
                leaving.start(block.at[n, :, columns], out.at[n, :, pl.ds(width + j * span, span)])
    leaving.wait()


def halves_kernel(starts, *refs):
    parts, (out_ref, sems) = refs[:4], refs[4:]
    arriving = Copies(sems)
    for k in range(4):
        arriving.start(parts[k].at[:, :, pl.ds(starts[k], out_ref.shape[-1])], out_ref.at[k])
    arriving.wait()


def gradient_kernel(whole, ids, *refs):
    value_ref, out_ref = refs[-2:]
    width = value_ref.shape[-1]
    first_side = ids[SIDE] == 0

    def factors(parts, mine=None, theirs=None):
        wide = jnp.concatenate([part[0][:, :width] for part in parts], axis=0)
        if mine is None:
            span = parts[0].shape[-1] - width
            starts = (width, width, width, width + span)
            return jnp.concatenate([p[0][:, i : i + span] for p, i in zip(parts, starts)], axis=0), wide
        mine, theirs = (jnp.concatenate([ref[k, 0] for k in range(4)], axis=0) for ref in (mine, theirs))
        left = jnp.where(first_side, mine, theirs)
        right = jnp.where(first_side, theirs, mine)
        return jnp.concatenate([left, right], axis=1), wide

    x, act = factors(refs[0:4], refs[4], refs[5])
    g, head = factors(refs[6:10]) if whole else factors(refs[6:10], refs[10], refs[11])
    value_ref[0] = lax.dot_general(x, head, TN, preferred_element_type=F32).astype(BF16)
    out_ref[0] = lax.dot_general(g, act, TN, preferred_element_type=F32).astype(BF16)


def gradients(ids, layers, first, count, forward, backward, before):
    quarter = forward[4].shape[-1]
    piece, width = 2 * quarter, forward[0].shape[-1] - quarter
    out = jax.ShapeDtypeStruct((layers, piece, width), BF16)
    out_spec = pl.BlockSpec((1, piece, width), lambda l: (first + l, 0, 0))

    def block(array, start):
        if array.ndim == 3:
            return pl.BlockSpec((1,) + array.shape[1:], lambda l: (start + l, 0, 0))
        return pl.BlockSpec((array.shape[0], 1) + array.shape[2:], lambda l: (0, start + l, 0, 0))

    specs = [SMEM] + [block(a, first) for a in forward] + [block(a, 0) for a in backward]
    operands = [ids] + list(forward) + list(backward)
    aliases = {}
    if before is not None:
        aliases = {len(operands): 0, len(operands) + 1: 1}
        operands, specs = operands + list(before), specs + [ANY, ANY]
    return pl.pallas_call(
        functools.partial(gradient_kernel, len(backward) == 4),
        out_shape=(out, out),
        grid=(count,),
        in_specs=specs,
        out_specs=(out_spec, out_spec),
        input_output_aliases=aliases,
        compiler_params=pltpu.CompilerParams(vmem_limit_bytes=VMEM_BYTES),
        cost_estimate=pl.CostEstimate(
            flops=count * 4 * piece * width * 256, bytes_accessed=count * 2400000, transcendentals=0
        ),
    )(*operands)


def per_device(section_map, checkpoint, top_grad, value_weight, out_weight):
    tp_total = lax.axis_size("tp")
    section_total = lax.axis_size("section")
    replica_total = lax.axis_size("rep")
    chips = section_total // 2
    rep, section, tp = (lax.axis_index(name) for name in ("rep", "section", "tp"))
    chip, core, side = section // 2, section % 2, tp % 2
    layers = section_map.shape[1]
    _, _, micro, tokens, model = checkpoint.shape
    slots, width = value_weight.shape[1], value_weight.shape[3]
    rows = micro * tokens
    cut = model // tp_total
    piece = model // (replica_total * section_total)
    v_own, o_own = value_weight[0], out_weight[0]
    x_pair, top_pair = checkpoint[0, 0], top_grad[0]

    ids = jnp.stack([rep, chip, core, side, tp]).astype(jnp.int32)

    chip_of = section_map // 2
    moves = chip_of[:, 1:] - chip_of[:, :-1]
    most_moves = jnp.max(moves, axis=0)

    swap = [(i, i ^ 1) for i in range(section_total)]

    def to_sibling(array):
        return lax.ppermute(array, "section", swap)

    def to_replica(array):
        return lax.ppermute(array, "rep", [(0, 1), (1, 0)])

    o_sib, v_sib = to_sibling(o_own), to_sibling(v_own)

    def shape(*dims, dtype=BF16):
        return jax.ShapeDtypeStruct(dims, dtype)

    def in_hbm(*dims):
        return pltpu.HBM(dims, BF16)

    def dma(*dims):
        return pltpu.SemaphoreType.DMA(dims)

    weight_bytes = model * width * 2
    weight_buffer = pltpu.VMEM((model, width), BF16)

    def reduce_slices(got, base, spread, *deps):
        count = got.shape[1]
        buffer = pltpu.VMEM((count, cut), BF16)
        return run(
            functools.partial(reduce_kernel, spread, len(deps)),
            (ids, got, base, *deps),
            [SMEM] + [ANY] * (2 + len(deps)),
            in_hbm(*got.shape) if spread else in_hbm(count, cut),
            HBM,
            [pltpu.VMEM(got.shape, BF16), buffer, buffer, dma(5), dma(tp_total if spread else 1)],
            got.size * 2,
        )

    def over_tp(parts):
        return lax.all_to_all(parts, "tp", 0, 0, tiled=True)

    def recompute_slot(slot, x, with_parts, deps=()):
        halves = (shape(tokens, width),) * 2 + (shape(tokens, width, dtype=F32),) * 2
        halves += (shape(chips, tokens, cut),) * 2
        outs = ((in_hbm(tp_total, rows, cut),) if with_parts else ()) + halves
        out_specs = ((HBM,) if with_parts else ()) + (VMEM,) * 6
        scratch = [pltpu.VMEM((tp_total, rows, cut), BF16), weight_buffer]
        scratch += [pltpu.VMEM((rows, width), BF16), pltpu.VMEM((rows, width), F32), dma(tp_total + 4), dma(2)]
        if with_parts:
            scratch += [weight_buffer, pltpu.VMEM((tp_total, rows, cut), BF16)]
        operands = (ids, x, v_own) + ((o_own,) if with_parts else ()) + tuple(deps)
        count = 2 if with_parts else 1
        return run(
            functools.partial(recompute, chips, with_parts, slot, len(deps)),
            operands,
            [SMEM] + [ANY] * (len(operands) - 1),
            outs,
            out_specs,
            scratch,
            count * weight_bytes,
            count * 2 * rows * model * width,
        )

    def along_chips(cuts):
        got = [cuts[0]]
        for far in range(1, chips):
            back = chips - far
            route = [(i, (i + 2 * back) % section_total) for i in range(section_total)]
            got.append(lax.ppermute(cuts[back], "section", route))
        return got

    def carve(act_mine, act_sib, x_mine, x_sib):
        block = in_hbm(2, tokens, width + cut)
        return run(
            functools.partial(carve_kernel, chips),
            (ids, act_mine, act_sib, x_mine, x_sib),
            [SMEM] + [VMEM] * 4,
            (block,) * chips,
            (HBM,) * chips,
            [dma(2, chips, 2)],
            2 * chips * tokens * (width + cut) * 4,
        )

    def to_owners(sources, wanted, of_slots, deps=()):
        count = len(wanted)
        columns = sources[0].shape[-1]
        span = (columns - width) // 4
        alone, both = in_hbm(count, tokens, width + span), in_hbm(count, tokens, width + 2 * span)
        own_out, sib_out, rep_out = run(
            functools.partial(pick_kernel, wanted, of_slots, len(deps)),
            (ids, section_map, *sources, *deps),
            [SMEM, SMEM] + [ANY] * (len(sources) + len(deps)),
            (alone, alone, both),
            (HBM,) * 3,
            [pltpu.VMEM((count, tokens, columns), BF16), dma(count), dma(7 * count)],
            count * tokens * columns * 6,
        )
        from_rep = to_replica(rep_out)
        parts = (own_out, to_sibling(sib_out), from_rep, to_sibling(from_rep))
        if span == piece:
            return parts
        mine = run(
            functools.partial(halves_kernel, (width, width, width, width + span)),
            parts,
            [ANY] * 4,
            shape(4, count, tokens, span),
            VMEM,
            [dma(4)],
            16 * count * tokens * span,
        )
        theirs = lax.ppermute(mine, "tp", [(i, i ^ 1) for i in range(tp_total)])
        return parts + (mine, theirs)

    x_rows = x_pair.reshape(rows, model)
    parts, act_mine_0, act_other_0, slope_mine_0, slope_other_0, x_mine_0, x_other_0 = recompute_slot(0, x_rows, True)
    act_sib_0, slope_sib_0, x_sib_0 = to_sibling(act_other_0), to_sibling(slope_other_0), to_sibling(x_other_0)
    first_cuts = carve(act_mine_0, act_sib_0, x_mine_0, x_sib_0)
    first_got = along_chips(first_cuts)
    x_second = over_tp(reduce_slices(over_tp(parts), x_rows, True))
    act_mine_1, act_other_1, slope_mine_1, slope_other_1, x_mine_1, x_other_1 = recompute_slot(
        1, x_second, False, first_cuts
    )
    slope_sib_1, act_sib_1, x_sib_1 = to_sibling(slope_other_1), to_sibling(act_other_1), to_sibling(x_other_1)
    second_cuts = carve(act_mine_1, act_sib_1, x_mine_1, x_sib_1)
    second_got = along_chips(second_cuts)
    slopes = (slope_mine_0, slope_mine_1, slope_sib_0, slope_sib_1)

    down = [(i, i - 2) for i in range(2, section_total)]

    def one_layer(layer, g, deps):
        last = layer == 0
        operands = (ids, section_map, g, *slopes, o_own, o_sib)
        operands += (() if last else (v_own, v_sib)) + tuple(deps)
        columns = width + (2 * cut if last else cut)
        block = in_hbm(tokens, columns)
        outs = (() if last else (in_hbm(tp_total, tokens, cut),)) + (block,) * chips
        scratch = [pltpu.VMEM((tp_total, tokens, cut), BF16), pltpu.VMEM((tokens, width), F32), weight_buffer]
        scratch += [pltpu.VMEM((chips, tokens, columns), BF16), dma(tp_total + 5), dma(chips + 2)]
        if not last:
            scratch += [weight_buffer, pltpu.VMEM((tp_total, tokens, cut), BF16)]
        count = 1 if last else 2
        result = run(
            functools.partial(step, chips, layer, len(deps)),
            operands,
            [SMEM, SMEM] + [ANY] * (len(operands) - 2),
            outs,
            (HBM,) * len(outs),
            scratch,
            count * weight_bytes,
            count * 2 * tokens * model * width,
        )
        return (None if last else result[0]), along_chips(result[-chips:])

    g = top_pair
    got_at = [None] * layers
    deps = {layer: [] for layer in range(layers)}
    upper, middle = [3, 4, 5, 6, 7], [1, 2]

    def collect(wanted, deps=()):
        return to_owners([array for layer in wanted for array in got_at[layer]], wanted, False, deps)

    for layer in reversed(range(layers)):
        if layer < layers - 1:
            deps[layer] += got_at[layer + 1][2:3]
        if layer == 7:
            deps[7] += first_got
        if layer == 6:
            deps[6] += second_cuts
        if layer == 5:
            deps[5] += second_got
        if layer == 4:
            forward = to_owners(first_got + second_got, list(range(layers)), True)
            deps[3] += forward[:4]
        if layer == 2:
            upper_all = collect(upper)
            deps[0] += upper_all[:4]
        parts, got_at[layer] = one_layer(layer, g, deps[layer])
        if layer == 0:
            break
        got = over_tp(parts)
        most = most_moves[layer - 1]

        def stay(*operands):
            return reduce_slices(*operands[:2], True, *operands[2:])

        def settle(kept, came, layer=layer):
            return run(
                functools.partial(settle_kernel, layer),
                (ids, section_map, kept, came),
                [SMEM, SMEM, ANY, ANY],
                in_hbm(tp_total, tokens, cut),
                HBM,
                [pltpu.VMEM((tokens, cut), BF16), dma(1), dma(tp_total)],
                tp_total * tokens * cut * 2,
            )

        def go_one(*operands):
            mine = reduce_slices(*operands[:2], False, *operands[2:])
            return settle(mine, lax.ppermute(mine, "section", down))

        def go_far(*operands, layer=layer, most=most):
            mine = reduce_slices(*operands[:2], False, *operands[2:])
            my_move = lax.dynamic_index_in_dim(moves, rep, 0, keepdims=False)[layer - 1]

            def hop(i, value):
                came = lax.ppermute(value, "section", down)
                return jnp.where(i < my_move, came, value)

            mine = lax.fori_loop(0, most, hop, mine)
            return settle(mine, mine)

        near = got_at[layer][1::2]
        spread = lax.switch(jnp.minimum(most, 2), (stay, go_one, go_far), got, g, *near)
        g = over_tp(spread)
        if layer == 1:
            middle_all = collect(middle, (spread,))

    result = gradients(ids, layers, upper[0], len(upper), forward, upper_all, None)
    result = gradients(ids, layers, middle[0], len(middle), forward, middle_all, result)
    last_all = collect([0], result)
    return gradients(ids, layers, 0, 1, forward, last_all, result)


def solution(mesh):
    placed = (
        P(),
        P("rep", "section", None, None, None),
        P("rep", None, None, None),
        P("rep", "section", None, "tp"),
        P("rep", "section", None, "tp"),
    )
    return jax.shard_map(
        per_device,
        mesh=mesh,
        in_specs=placed,
        out_specs=(P(None, ("rep", "section"), "tp"), P(None, ("rep", "section"), "tp")),
        check_vma=False,
    )
```

```python
import functools

import jax
import jax.numpy as jnp
from jax import lax
from jax.experimental import pallas as pl
from jax.experimental.pallas import tpu as pltpu
from jax.sharding import PartitionSpec as P

BF16 = jnp.bfloat16
F32 = jnp.float32
VMEM_BYTES = 64 * 1024 * 1024
NT = (((1,), (1,)), ((), ()))
TN = (((0,), (0,)), ((), ()))
ANY = pl.BlockSpec(memory_space=pl.ANY)
HBM = pl.BlockSpec(memory_space=pltpu.HBM)
SMEM = pl.BlockSpec(memory_space=pltpu.SMEM)
VMEM = pl.BlockSpec(memory_space=pltpu.VMEM)


REP, CHIP, CORE, SIDE, TP = range(5)


def held_at(ids, section_map, layer):
    section = section_map[ids[REP], layer]
    slot = jnp.int32(0)
    if layer > 0:
        slot = (section_map[ids[REP], layer - 1] == section).astype(jnp.int32)
    chips = 4
    return lax.rem(section, 2), slot, lax.rem(section // 2 - ids[CHIP] + chips, chips)


def silu_slope(preact):
    sigma = jax.nn.sigmoid(preact)
    return sigma * (1.0 + preact * (1.0 - sigma))


def run(kernel, operands, specs, outs, out_specs, scratch, bytes_moved, flops=0):
    return pl.pallas_call(
        kernel,
        out_shape=outs,
        in_specs=specs,
        out_specs=out_specs,
        scratch_shapes=scratch,
        compiler_params=pltpu.CompilerParams(vmem_limit_bytes=VMEM_BYTES),
        cost_estimate=pl.CostEstimate(flops=flops, bytes_accessed=bytes_moved, transcendentals=0),
    )(*operands)


def rows_place(ref, cut, core):
    if len(ref.shape) == 3 and ref.shape[-1] == cut:
        return lambda i: ref.at[i]
    columns = lambda i: pl.ds(pl.multiple_of(i * cut, cut), cut)
    if len(ref.shape) == 2:
        return lambda i: ref.at[:, columns(i)]
    return lambda i: ref.at[core, :, columns(i)]


class Copies:
    def __init__(self, sems):
        self.sems, self.all = sems, []

    def start(self, source, target, condition=None):
        copy = pltpu.make_async_copy(source, target, self.sems.at[len(self.all)])
        if condition is None:
            copy.start()
        else:
            pl.when(condition)(copy.start)
        self.all.append(copy)
        return copy

    def either(self, condition, first, second, target):
        sem = self.sems.at[len(self.all)]
        pl.when(condition)(lambda: pltpu.make_async_copy(first, target, sem).start())
        pl.when(jnp.logical_not(condition))(lambda: pltpu.make_async_copy(second, target, sem).start())
        self.all.append(pltpu.make_async_copy(first, target, sem))
        return self.all[-1]

    def wait(self):
        for copy in self.all:
            copy.wait()


def halves(ref):
    step = ref.shape[0] // 2
    return [pl.ds(i * step, step) for i in range(2)]


def product_in(rows, weight, waits):
    cuts, cut = rows.shape[0], rows.shape[-1]
    total = None
    for i in range(cuts):
        if i % (cuts // len(waits)) == 0:
            waits[i // (cuts // len(waits))].wait()
        part = jnp.dot(rows[i], weight[i * cut : (i + 1) * cut, :], preferred_element_type=F32)
        total = part if total is None else total + part
    return total


def product_out(rows, weight, waits, stage, part_ref, out):
    cuts, cut = stage.shape[0], stage.shape[-1]
    group = cuts // len(waits)
    for i in range(cuts):
        if i % group == 0:
            waits[i // group].wait()
        part = lax.dot_general(rows, weight[i * cut : (i + 1) * cut, :], NT, preferred_element_type=F32)
        stage[i] = part.astype(BF16)
        if i % group == group - 1:
            cuts_done = pl.ds(i - group + 1, group)
            out.start(stage.at[cuts_done], part_ref.at[cuts_done])


def recompute(chips, with_parts, slot, deps, ids, x_ref, v_ref, *refs):
    o_ref, refs = (refs[0], refs[1:]) if with_parts else (None, refs)
    refs = refs[deps:]
    part_ref, refs = (refs[0], refs[1:]) if with_parts else (None, refs)
    outs, (xbuf, vbuf, act_rows, slope_rows, in_sems, out_sems) = refs[:6], refs[6:12]
    cuts, cut = xbuf.shape[0], xbuf.shape[-1]
    core, side = ids[CORE], ids[SIDE]
    arriving, leaving = Copies(in_sems), Copies(out_sems)
    x = [arriving.start(rows_place(x_ref, cut, core)(i), xbuf.at[i]) for i in range(cuts)]
    v = [arriving.start(v_ref.at[slot, rows], vbuf.at[rows]) for rows in halves(vbuf)]
    if with_parts:
        obuf, stage = refs[12:]
        o = [arriving.start(o_ref.at[slot, rows], obuf.at[rows]) for rows in halves(obuf)]
    for copy in x:
        copy.wait()
    pre = product_in(xbuf, vbuf, v)
    act = jax.nn.silu(pre).astype(BF16)
    if with_parts:
        product_out(act, obuf, o, stage, part_ref, leaving)
    act_rows[...] = act
    slope_rows[...] = silu_slope(pre)
    half = outs[0].shape[0]
    quarter = cut // 4
    for k, which in enumerate((core, 1 - core)):
        rows = pl.ds(pl.multiple_of(which * half, half), half)
        act_out, slope_out, x_out = outs[k], outs[2 + k], outs[4 + k]
        act_out[...] = act_rows[rows, :]
        slope_out[...] = slope_rows[rows, :]
        for to in range(chips):
            for j in range(4):
                columns = pl.ds(pl.multiple_of((j % 2) * 2 * quarter + side * quarter, quarter), quarter)
                x_out[to, :, j * quarter : (j + 1) * quarter] = xbuf[(j // 2) * chips + to, rows, columns]
    leaving.wait()


def step(chips, layer, deps, ids, section_map, g_ref, *refs):
    with_parts = layer > 0
    slopes, refs = refs[:4], refs[4:]
    o_refs, refs = refs[:2], refs[2:]
    v_refs, refs = (refs[:2], refs[2:]) if with_parts else (None, refs)
    refs = refs[deps:]
    part_ref, refs = (refs[0], refs[1:]) if with_parts else (None, refs)
    outs, (gbuf, sbuf, obuf, pay, in_sems, out_sems) = refs[:chips], refs[chips : chips + 6]
    cut, width = gbuf.shape[-1], sbuf.shape[-1]
    span = (pay.shape[-1] - width) // 4
    chip, core, side = ids[CHIP], ids[CORE], ids[SIDE]
    section_core, slot, _ = held_at(ids, section_map, layer)
    own = section_core == core
    arriving, leaving = Copies(in_sems), Copies(out_sems)
    if g_ref.shape == gbuf.shape:
        g = [arriving.start(g_ref, gbuf)]
    else:
        g = [arriving.start(rows_place(g_ref, cut, core)(i), gbuf.at[i]) for i in range(gbuf.shape[0])]
    o = [arriving.either(own, o_refs[0].at[slot, r], o_refs[1].at[slot, r], obuf.at[r]) for r in halves(obuf)]
    which = jnp.where(own, 0, 2) + slot
    for j in range(4):
        pl.when(which == j)(pltpu.make_async_copy(slopes[j], sbuf, in_sems.at[-1 + in_sems.shape[0]]).start)
    slope = pltpu.make_async_copy(slopes[0], sbuf, in_sems.at[-1 + in_sems.shape[0]])
    if with_parts:
        vbuf, stage = refs[chips + 6 :]
        v = [arriving.either(own, v_refs[0].at[slot, r], v_refs[1].at[slot, r], vbuf.at[r]) for r in halves(vbuf)]
    for copy in g:
        copy.wait()
    for far in range(chips):
        to = lax.rem(chip + far, chips)
        for j in range(4):
            start = (j % 2) * (cut // 2) + (0 if span == cut // 2 else side * span)
            columns = pl.ds(start if span == cut // 2 else pl.multiple_of(start, span), span)
            pay[far, :, width + j * span : width + (j + 1) * span] = gbuf[(j // 2) * chips + to, :, columns]
    total = product_in(gbuf, obuf, o)
    slope.wait()
    head = (total * sbuf[...]).astype(BF16)
    for far, out in enumerate(outs):
        pay[far, :, :width] = head
        leaving.start(pay.at[far], out)
    if with_parts:
        product_out(head, vbuf, v, stage, part_ref, leaving)
    leaving.wait()


def reduce_kernel(spread, deps, ids, got_ref, base_ref, *refs):
    out_ref, got, base, stage, sems, out_sems = refs[deps:]
    cuts, cut = got.shape[0], got.shape[-1]
    arriving, leaving = Copies(sems), Copies(out_sems)
    arriving.start(rows_place(base_ref, cut, ids[CORE])(ids[TP]), base)
    for i in range(4):
        some = pl.ds(i * (cuts // 4), cuts // 4)
        arriving.start(got_ref.at[some], got.at[some])
    arriving.wait()
    total = got[0].astype(F32)
    for i in range(1, cuts):
        total += got[i].astype(F32)
    stage[...] = (base[...].astype(F32) + total).astype(BF16)
    for i in range(cuts if spread else 1):
        leaving.start(stage, out_ref.at[i] if spread else out_ref)
    leaving.wait()


def settle_kernel(layer, ids, section_map, kept_ref, came_ref, out_ref, stage, sems, out_sems):
    rep = ids[REP]
    moved = section_map[rep, layer] // 2 > section_map[rep, layer - 1] // 2
    arriving, leaving = Copies(sems), Copies(out_sems)
    arriving.either(moved, came_ref, kept_ref, stage)
    arriving.wait()
    for i in range(out_ref.shape[0]):
        leaving.start(stage, out_ref.at[i])
    leaving.wait()


def carve_kernel(chips, ids, act_mine, act_sib, x_mine, x_sib, *refs):
    outs, sems = refs[:chips], refs[chips]
    chip, core = ids[CHIP], ids[CORE]
    width = act_mine.shape[-1]
    copies = []
    for k, (act, x) in enumerate(((act_mine, x_mine), (act_sib, x_sib))):
        at = core if k == 0 else 1 - core
        for far, out in enumerate(outs):
            to = lax.rem(chip + far, chips)
            for j, source in enumerate((act, x.at[to])):
                target = out.at[at, :, pl.ds(j * width, width)]
                copies.append(pltpu.make_async_copy(source, target, sems.at[k, far, j]))
                copies[-1].start()
    for copy in copies:
        copy.wait()


def pick_kernel(wanted, of_slots, deps, ids, section_map, *refs):
    chips = 4
    count = len(wanted)
    total = (2 if of_slots else count) * chips
    sources, (own_out, sib_out, rep_out, block, in_sems, sems) = refs[:total], refs[total + deps :]
    core, rep = ids[CORE], ids[REP]
    width = 2 * sib_out.shape[-1] - rep_out.shape[-1]
    span = rep_out.shape[-1] - sib_out.shape[-1]
    for n, layer in enumerate(wanted):
        section_core, slot, far = held_at(ids, section_map, layer)
        at = slot * chips + far if of_slots else n * chips + far
        for j in range(total) if of_slots else range(n * chips, (n + 1) * chips):

            def begin(n=n, j=j, section_core=section_core):
                source = sources[j].at[section_core] if of_slots else sources[j]
                pltpu.make_async_copy(source, block.at[n], in_sems.at[n]).start()

            pl.when(at == j)(begin)
    plan = ((own_out, [(rep, core)]), (sib_out, [(rep, 1 - core)]), (rep_out, [(1 - rep, core), (1 - rep, 1 - core)]))
    leaving = Copies(sems)
    for n in range(count):
        pltpu.make_async_copy(block.at[n], block.at[n], in_sems.at[n]).wait()
        for out, pieces in plan:
            leaving.start(block.at[n, :, pl.ds(0, width)], out.at[n, :, pl.ds(0, width)])
            for j, (replica, side) in enumerate(pieces):
                columns = pl.ds(pl.multiple_of(width + (replica * 2 + side) * span, span), span)
                leaving.start(block.at[n, :, columns], out.at[n, :, pl.ds(width + j * span, span)])
    leaving.wait()


def halves_kernel(starts, *refs):
    parts, (out_ref, sems) = refs[:4], refs[4:]
    arriving = Copies(sems)
    for k in range(4):
        arriving.start(parts[k].at[:, :, pl.ds(starts[k], out_ref.shape[-1])], out_ref.at[k])
    arriving.wait()


def gradient_kernel(whole, ids, *refs):
    value_ref, out_ref = refs[-2:]
    width = value_ref.shape[-1]
    first_side = ids[SIDE] == 0

    def factors(parts, mine=None, theirs=None):
        wide = jnp.concatenate([part[0][:, :width] for part in parts], axis=0)
        if mine is None:
            span = parts[0].shape[-1] - width
            starts = (width, width, width, width + span)
            return jnp.concatenate([p[0][:, i : i + span] for p, i in zip(parts, starts)], axis=0), wide
        mine, theirs = (jnp.concatenate([ref[k, 0] for k in range(4)], axis=0) for ref in (mine, theirs))
        left = jnp.where(first_side, mine, theirs)
        right = jnp.where(first_side, theirs, mine)
        return jnp.concatenate([left, right], axis=1), wide

    x, act = factors(refs[0:4], refs[4], refs[5])
    g, head = factors(refs[6:10]) if whole else factors(refs[6:10], refs[10], refs[11])
    value_ref[0] = lax.dot_general(x, head, TN, preferred_element_type=F32).astype(BF16)
    out_ref[0] = lax.dot_general(g, act, TN, preferred_element_type=F32).astype(BF16)


def gradients(ids, layers, first, count, forward, backward, before):
    quarter = forward[4].shape[-1]
    piece, width = 2 * quarter, forward[0].shape[-1] - quarter
    out = jax.ShapeDtypeStruct((layers, piece, width), BF16)
    out_spec = pl.BlockSpec((1, piece, width), lambda l: (first + l, 0, 0))

    def block(array, start):
        if array.ndim == 3:
            return pl.BlockSpec((1,) + array.shape[1:], lambda l: (start + l, 0, 0))
        return pl.BlockSpec((array.shape[0], 1) + array.shape[2:], lambda l: (0, start + l, 0, 0))

    specs = [SMEM] + [block(a, first) for a in forward] + [block(a, 0) for a in backward]
    operands = [ids] + list(forward) + list(backward)
    aliases = {}
    if before is not None:
        aliases = {len(operands): 0, len(operands) + 1: 1}
        operands, specs = operands + list(before), specs + [ANY, ANY]
    return pl.pallas_call(
        functools.partial(gradient_kernel, len(backward) == 4),
        out_shape=(out, out),
        grid=(count,),
        in_specs=specs,
        out_specs=(out_spec, out_spec),
        input_output_aliases=aliases,
        compiler_params=pltpu.CompilerParams(vmem_limit_bytes=VMEM_BYTES),
        cost_estimate=pl.CostEstimate(
            flops=count * 4 * piece * width * 256, bytes_accessed=count * 2400000, transcendentals=0
        ),
    )(*operands)


def per_device(section_map, checkpoint, top_grad, value_weight, out_weight):
    tp_total = lax.axis_size("tp")
    section_total = lax.axis_size("section")
    replica_total = lax.axis_size("rep")
    chips = section_total // 2
    rep, section, tp = (lax.axis_index(name) for name in ("rep", "section", "tp"))
    chip, core, side = section // 2, section % 2, tp % 2
    layers = section_map.shape[1]
    _, _, micro, tokens, model = checkpoint.shape
    slots, width = value_weight.shape[1], value_weight.shape[3]
    rows = micro * tokens
    cut = model // tp_total
    piece = model // (replica_total * section_total)
    v_own, o_own = value_weight[0], out_weight[0]
    x_pair, top_pair = checkpoint[0, 0], top_grad[0]

    ids = jnp.stack([rep, chip, core, side, tp]).astype(jnp.int32)

    chip_of = section_map // 2
    moves = chip_of[:, 1:] - chip_of[:, :-1]
    most_moves = jnp.max(moves, axis=0)

    swap = [(i, i ^ 1) for i in range(section_total)]

    def to_sibling(array):
        return lax.ppermute(array, "section", swap)

    def to_replica(array):
        return lax.ppermute(array, "rep", [(0, 1), (1, 0)])

    o_sib, v_sib = to_sibling(o_own), to_sibling(v_own)

    def shape(*dims, dtype=BF16):
        return jax.ShapeDtypeStruct(dims, dtype)

    def in_hbm(*dims):
        return pltpu.HBM(dims, BF16)

    def dma(*dims):
        return pltpu.SemaphoreType.DMA(dims)

    weight_bytes = model * width * 2
    weight_buffer = pltpu.VMEM((model, width), BF16)

    def reduce_slices(got, base, spread, *deps):
        count = got.shape[1]
        buffer = pltpu.VMEM((count, cut), BF16)
        return run(
            functools.partial(reduce_kernel, spread, len(deps)),
            (ids, got, base, *deps),
            [SMEM] + [ANY] * (2 + len(deps)),
            in_hbm(*got.shape) if spread else in_hbm(count, cut),
            HBM,
            [pltpu.VMEM(got.shape, BF16), buffer, buffer, dma(5), dma(tp_total if spread else 1)],
            got.size * 2,
        )

    def over_tp(parts):
        return lax.all_to_all(parts, "tp", 0, 0, tiled=True)

    def recompute_slot(slot, x, with_parts, deps=()):
        halves = (shape(tokens, width),) * 2 + (shape(tokens, width, dtype=F32),) * 2
        halves += (shape(chips, tokens, cut),) * 2
        outs = ((in_hbm(tp_total, rows, cut),) if with_parts else ()) + halves
        out_specs = ((HBM,) if with_parts else ()) + (VMEM,) * 6
        scratch = [pltpu.VMEM((tp_total, rows, cut), BF16), weight_buffer]
        scratch += [pltpu.VMEM((rows, width), BF16), pltpu.VMEM((rows, width), F32), dma(tp_total + 4), dma(2)]
        if with_parts:
            scratch += [weight_buffer, pltpu.VMEM((tp_total, rows, cut), BF16)]
        operands = (ids, x, v_own) + ((o_own,) if with_parts else ()) + tuple(deps)
        count = 2 if with_parts else 1
        return run(
            functools.partial(recompute, chips, with_parts, slot, len(deps)),
            operands,
            [SMEM] + [ANY] * (len(operands) - 1),
            outs,
            out_specs,
            scratch,
            count * weight_bytes,
            count * 2 * rows * model * width,
        )

    def along_chips(cuts):
        got = [cuts[0]]
        for far in range(1, chips):
            back = chips - far
            route = [(i, (i + 2 * back) % section_total) for i in range(section_total)]
            got.append(lax.ppermute(cuts[back], "section", route))
        return got

    def carve(act_mine, act_sib, x_mine, x_sib):
        block = in_hbm(2, tokens, width + cut)
        return run(
            functools.partial(carve_kernel, chips),
            (ids, act_mine, act_sib, x_mine, x_sib),
            [SMEM] + [VMEM] * 4,
            (block,) * chips,
            (HBM,) * chips,
            [dma(2, chips, 2)],
            2 * chips * tokens * (width + cut) * 4,
        )

    def to_owners(sources, wanted, of_slots, deps=()):
        count = len(wanted)
        columns = sources[0].shape[-1]
        span = (columns - width) // 4
        alone, both = in_hbm(count, tokens, width + span), in_hbm(count, tokens, width + 2 * span)
        own_out, sib_out, rep_out = run(
            functools.partial(pick_kernel, wanted, of_slots, len(deps)),
            (ids, section_map, *sources, *deps),
            [SMEM, SMEM] + [ANY] * (len(sources) + len(deps)),
            (alone, alone, both),
            (HBM,) * 3,
            [pltpu.VMEM((count, tokens, columns), BF16), dma(count), dma(7 * count)],
            count * tokens * columns * 6,
        )
        from_rep = to_replica(rep_out)
        parts = (own_out, to_sibling(sib_out), from_rep, to_sibling(from_rep))
        if span == piece:
            return parts
        mine = run(
            functools.partial(halves_kernel, (width, width, width, width + span)),
            parts,
            [ANY] * 4,
            shape(4, count, tokens, span),
            VMEM,
            [dma(4)],
            16 * count * tokens * span,
        )
        theirs = lax.ppermute(mine, "tp", [(i, i ^ 1) for i in range(tp_total)])
        return parts + (mine, theirs)

    x_rows = x_pair.reshape(rows, model)
    parts, act_mine_0, act_other_0, slope_mine_0, slope_other_0, x_mine_0, x_other_0 = recompute_slot(0, x_rows, True)
    act_sib_0, slope_sib_0, x_sib_0 = to_sibling(act_other_0), to_sibling(slope_other_0), to_sibling(x_other_0)
    first_cuts = carve(act_mine_0, act_sib_0, x_mine_0, x_sib_0)
    first_got = along_chips(first_cuts)
    x_second = over_tp(reduce_slices(over_tp(parts), x_rows, True))
    act_mine_1, act_other_1, slope_mine_1, slope_other_1, x_mine_1, x_other_1 = recompute_slot(
        1, x_second, False, first_cuts
    )
    slope_sib_1, act_sib_1, x_sib_1 = to_sibling(slope_other_1), to_sibling(act_other_1), to_sibling(x_other_1)
    second_cuts = carve(act_mine_1, act_sib_1, x_mine_1, x_sib_1)
    second_got = along_chips(second_cuts)
    slopes = (slope_mine_0, slope_mine_1, slope_sib_0, slope_sib_1)

    down = [(i, i - 2) for i in range(2, section_total)]
    earlier, latest = [2, 3, 4, 5, 6, 7], [0, 1]

    def one_layer(layer, g, deps):
        last = layer == 0
        operands = (ids, section_map, g, *slopes, o_own, o_sib)
        operands += (() if last else (v_own, v_sib)) + tuple(deps)
        columns = width + (2 * cut if layer in latest else cut)
        block = in_hbm(tokens, columns)
        outs = (() if last else (in_hbm(tp_total, tokens, cut),)) + (block,) * chips
        scratch = [pltpu.VMEM((tp_total, tokens, cut), BF16), pltpu.VMEM((tokens, width), F32), weight_buffer]
        scratch += [pltpu.VMEM((chips, tokens, columns), BF16), dma(tp_total + 5), dma(chips + 2)]
        if not last:
            scratch += [weight_buffer, pltpu.VMEM((tp_total, tokens, cut), BF16)]
        count = 1 if last else 2
        result = run(
            functools.partial(step, chips, layer, len(deps)),
            operands,
            [SMEM, SMEM] + [ANY] * (len(operands) - 2),
            outs,
            (HBM,) * len(outs),
            scratch,
            count * weight_bytes,
            count * 2 * tokens * model * width,
        )
        return (None if last else result[0]), along_chips(result[-chips:])

    g = top_pair
    got_at = [None] * layers
    deps = {layer: [] for layer in range(layers)}

    def collect(wanted, deps=()):
        return to_owners([array for layer in wanted for array in got_at[layer]], wanted, False, deps)

    for layer in reversed(range(layers)):
        if layer == 7:
            deps[7] += first_got
        if layer == 6:
            deps[6] += list(second_cuts) + got_at[7][2:3]
        if layer == 5:
            deps[5] += second_got[1::2]
        if layer == 4:
            deps[4] += second_got[2:3] + got_at[6][2:3]
            forward = to_owners(first_got + second_got, list(range(layers)), True)
        if layer == 3:
            deps[3] += got_at[5][2:3] + got_at[4][2:3]
        if layer == 2:
            deps[2] += got_at[3][2:3] + list(forward[:4])
        if layer == 1:
            deps[1] += got_at[2][2:3]
            earlier_all = collect(earlier)
        if layer == 0:
            deps[0] += got_at[1][2:3] + list(earlier_all[:4])
        parts, got_at[layer] = one_layer(layer, g, deps[layer])
        if layer == 0:
            break
        got = over_tp(parts)
        most = most_moves[layer - 1]

        def stay(*operands):
            return reduce_slices(*operands[:2], True, *operands[2:])

        def settle(kept, came, layer=layer):
            return run(
                functools.partial(settle_kernel, layer),
                (ids, section_map, kept, came),
                [SMEM, SMEM, ANY, ANY],
                in_hbm(tp_total, tokens, cut),
                HBM,
                [pltpu.VMEM((tokens, cut), BF16), dma(1), dma(tp_total)],
                tp_total * tokens * cut * 2,
            )

        def go_one(*operands):
            mine = reduce_slices(*operands[:2], False, *operands[2:])
            return settle(mine, lax.ppermute(mine, "section", down))

        def go_far(*operands, layer=layer, most=most):
            mine = reduce_slices(*operands[:2], False, *operands[2:])
            my_move = lax.dynamic_index_in_dim(moves, rep, 0, keepdims=False)[layer - 1]

            def hop(i, value):
                came = lax.ppermute(value, "section", down)
                return jnp.where(i < my_move, came, value)

            mine = lax.fori_loop(0, most, hop, mine)
            return settle(mine, mine)

        near = got_at[layer][1::2]
        spread = lax.switch(jnp.minimum(most, 2), (stay, go_one, go_far), got, g, *near)
        g = over_tp(spread)

    result = gradients(ids, layers, earlier[0], len(earlier), forward, earlier_all, None)
    latest_all = collect(latest, result)
    return gradients(ids, layers, latest[0], len(latest), forward, latest_all, result)


def solution(mesh):
    placed = (
        P(),
        P("rep", "section", None, None, None),
        P("rep", None, None, None),
        P("rep", "section", None, "tp"),
        P("rep", "section", None, "tp"),
    )
    return jax.shard_map(
        per_device,
        mesh=mesh,
        in_specs=placed,
        out_specs=(P(None, ("rep", "section"), "tp"), P(None, ("rep", "section"), "tp")),
        check_vma=False,
    )
```

```python
import functools

import jax
import jax.numpy as jnp
from jax import lax
from jax.experimental import pallas as pl
from jax.experimental.pallas import tpu as pltpu
from jax.sharding import PartitionSpec as P

BF16 = jnp.bfloat16
F32 = jnp.float32
VMEM_BYTES = 64 * 1024 * 1024
NT = (((1,), (1,)), ((), ()))
TN = (((0,), (0,)), ((), ()))
ANY = pl.BlockSpec(memory_space=pl.ANY)
HBM = pl.BlockSpec(memory_space=pltpu.HBM)
SMEM = pl.BlockSpec(memory_space=pltpu.SMEM)
VMEM = pl.BlockSpec(memory_space=pltpu.VMEM)


REP, CHIP, CORE, SIDE, TP = range(5)


def held_at(ids, section_map, layer):
    section = section_map[ids[REP], layer]
    slot = jnp.int32(0)
    if layer > 0:
        slot = (section_map[ids[REP], layer - 1] == section).astype(jnp.int32)
    chips = 4
    return lax.rem(section, 2), slot, lax.rem(section // 2 - ids[CHIP] + chips, chips)


def silu_slope(preact):
    sigma = jax.nn.sigmoid(preact)
    return sigma * (1.0 + preact * (1.0 - sigma))


def run(kernel, operands, specs, outs, out_specs, scratch, bytes_moved, flops=0):
    return pl.pallas_call(
        kernel,
        out_shape=outs,
        in_specs=specs,
        out_specs=out_specs,
        scratch_shapes=scratch,
        compiler_params=pltpu.CompilerParams(vmem_limit_bytes=VMEM_BYTES),
        cost_estimate=pl.CostEstimate(flops=flops, bytes_accessed=bytes_moved, transcendentals=0),
    )(*operands)


def rows_place(ref, cut, core):
    if len(ref.shape) == 3 and ref.shape[-1] == cut:
        return lambda i: ref.at[i]
    columns = lambda i: pl.ds(pl.multiple_of(i * cut, cut), cut)
    if len(ref.shape) == 2:
        return lambda i: ref.at[:, columns(i)]
    return lambda i: ref.at[core, :, columns(i)]


class Copies:
    def __init__(self, sems):
        self.sems, self.all = sems, []

    def start(self, source, target, condition=None):
        copy = pltpu.make_async_copy(source, target, self.sems.at[len(self.all)])
        if condition is None:
            copy.start()
        else:
            pl.when(condition)(copy.start)
        self.all.append(copy)
        return copy

    def either(self, condition, first, second, target):
        sem = self.sems.at[len(self.all)]
        pl.when(condition)(lambda: pltpu.make_async_copy(first, target, sem).start())
        pl.when(jnp.logical_not(condition))(lambda: pltpu.make_async_copy(second, target, sem).start())
        self.all.append(pltpu.make_async_copy(first, target, sem))
        return self.all[-1]

    def wait(self):
        for copy in self.all:
            copy.wait()


def halves(ref):
    step = ref.shape[0] // 2
    return [pl.ds(i * step, step) for i in range(2)]


def product_in(rows, weight, waits):
    cuts, cut = rows.shape[0], rows.shape[-1]
    total = None
    for i in range(cuts):
        if i % (cuts // len(waits)) == 0:
            waits[i // (cuts // len(waits))].wait()
        part = jnp.dot(rows[i], weight[i * cut : (i + 1) * cut, :], preferred_element_type=F32)
        total = part if total is None else total + part
    return total


def product_out(rows, weight, waits, stage, part_ref, out):
    cuts, cut = stage.shape[0], stage.shape[-1]
    group = cuts // len(waits)
    for i in range(cuts):
        if i % group == 0:
            waits[i // group].wait()
        part = lax.dot_general(rows, weight[i * cut : (i + 1) * cut, :], NT, preferred_element_type=F32)
        stage[i] = part.astype(BF16)
        if i % group == group - 1:
            cuts_done = pl.ds(i - group + 1, group)
            out.start(stage.at[cuts_done], part_ref.at[cuts_done])


def recompute(chips, with_parts, slot, deps, ids, x_ref, v_ref, *refs):
    o_ref, refs = (refs[0], refs[1:]) if with_parts else (None, refs)
    refs = refs[deps:]
    part_ref, refs = (refs[0], refs[1:]) if with_parts else (None, refs)
    outs, (xbuf, vbuf, act_rows, slope_rows, in_sems, out_sems) = refs[:6], refs[6:12]
    cuts, cut = xbuf.shape[0], xbuf.shape[-1]
    core, side = ids[CORE], ids[SIDE]
    arriving, leaving = Copies(in_sems), Copies(out_sems)
    x = [arriving.start(rows_place(x_ref, cut, core)(i), xbuf.at[i]) for i in range(cuts)]
    v = [arriving.start(v_ref.at[slot, rows], vbuf.at[rows]) for rows in halves(vbuf)]
    if with_parts:
        obuf, stage = refs[12:]
        o = [arriving.start(o_ref.at[slot, rows], obuf.at[rows]) for rows in halves(obuf)]
    for copy in x:
        copy.wait()
    pre = product_in(xbuf, vbuf, v)
    act = jax.nn.silu(pre).astype(BF16)
    if with_parts:
        product_out(act, obuf, o, stage, part_ref, leaving)
    act_rows[...] = act
    slope_rows[...] = silu_slope(pre)
    half = outs[0].shape[0]
    quarter = cut // 4
    for k, which in enumerate((core, 1 - core)):
        rows = pl.ds(pl.multiple_of(which * half, half), half)
        act_out, slope_out, x_out = outs[k], outs[2 + k], outs[4 + k]
        act_out[...] = act_rows[rows, :]
        slope_out[...] = slope_rows[rows, :]
        for to in range(chips):
            for j in range(4):
                columns = pl.ds(pl.multiple_of((j % 2) * 2 * quarter + side * quarter, quarter), quarter)
                x_out[to, :, j * quarter : (j + 1) * quarter] = xbuf[(j // 2) * chips + to, rows, columns]
    leaving.wait()


def step(chips, layer, deps, ids, section_map, g_ref, *refs):
    with_parts = layer > 0
    slopes, refs = refs[:4], refs[4:]
    o_refs, refs = refs[:2], refs[2:]
    v_refs, refs = (refs[:2], refs[2:]) if with_parts else (None, refs)
    refs = refs[deps:]
    part_ref, refs = (refs[0], refs[1:]) if with_parts else (None, refs)
    outs, (gbuf, sbuf, obuf, pay, in_sems, out_sems) = refs[:chips], refs[chips : chips + 6]
    cut, width = gbuf.shape[-1], sbuf.shape[-1]
    span = (pay.shape[-1] - width) // 4
    chip, core, side = ids[CHIP], ids[CORE], ids[SIDE]
    section_core, slot, _ = held_at(ids, section_map, layer)
    own = section_core == core
    arriving, leaving = Copies(in_sems), Copies(out_sems)
    if g_ref.shape == gbuf.shape:
        g = [arriving.start(g_ref, gbuf)]
    else:
        g = [arriving.start(rows_place(g_ref, cut, core)(i), gbuf.at[i]) for i in range(gbuf.shape[0])]
    o = [arriving.either(own, o_refs[0].at[slot, r], o_refs[1].at[slot, r], obuf.at[r]) for r in halves(obuf)]
    which = jnp.where(own, 0, 2) + slot
    for j in range(4):
        pl.when(which == j)(pltpu.make_async_copy(slopes[j], sbuf, in_sems.at[-1 + in_sems.shape[0]]).start)
    slope = pltpu.make_async_copy(slopes[0], sbuf, in_sems.at[-1 + in_sems.shape[0]])
    if with_parts:
        vbuf, stage = refs[chips + 6 :]
        v = [arriving.either(own, v_refs[0].at[slot, r], v_refs[1].at[slot, r], vbuf.at[r]) for r in halves(vbuf)]
    for copy in g:
        copy.wait()
    for far in range(chips):
        to = lax.rem(chip + far, chips)
        for j in range(4):
            start = (j % 2) * (cut // 2) + (0 if span == cut // 2 else side * span)
            columns = pl.ds(start if span == cut // 2 else pl.multiple_of(start, span), span)
            pay[far, :, width + j * span : width + (j + 1) * span] = gbuf[(j // 2) * chips + to, :, columns]
    total = product_in(gbuf, obuf, o)
    slope.wait()
    head = (total * sbuf[...]).astype(BF16)
    for far, out in enumerate(outs):
        pay[far, :, :width] = head
        leaving.start(pay.at[far], out)
    if with_parts:
        product_out(head, vbuf, v, stage, part_ref, leaving)
    leaving.wait()


def reduce_kernel(spread, deps, ids, got_ref, base_ref, *refs):
    out_ref, got, base, stage, sems, out_sems = refs[deps:]
    cuts, cut = got.shape[0], got.shape[-1]
    arriving, leaving = Copies(sems), Copies(out_sems)
    arriving.start(rows_place(base_ref, cut, ids[CORE])(ids[TP]), base)
    for i in range(4):
        some = pl.ds(i * (cuts // 4), cuts // 4)
        arriving.start(got_ref.at[some], got.at[some])
    arriving.wait()
    total = got[0].astype(F32)
    for i in range(1, cuts):
        total += got[i].astype(F32)
    stage[...] = (base[...].astype(F32) + total).astype(BF16)
    for i in range(cuts if spread else 1):
        leaving.start(stage, out_ref.at[i] if spread else out_ref)
    leaving.wait()


def settle_kernel(layer, ids, section_map, kept_ref, came_ref, out_ref, stage, sems, out_sems):
    rep = ids[REP]
    moved = section_map[rep, layer] // 2 > section_map[rep, layer - 1] // 2
    arriving, leaving = Copies(sems), Copies(out_sems)
    arriving.either(moved, came_ref, kept_ref, stage)
    arriving.wait()
    for i in range(out_ref.shape[0]):
        leaving.start(stage, out_ref.at[i])
    leaving.wait()


def carve_kernel(chips, ids, act_mine, act_sib, x_mine, x_sib, *refs):
    outs, sems = refs[:chips], refs[chips]
    chip, core = ids[CHIP], ids[CORE]
    width = act_mine.shape[-1]
    copies = []
    for k, (act, x) in enumerate(((act_mine, x_mine), (act_sib, x_sib))):
        at = core if k == 0 else 1 - core
        for far, out in enumerate(outs):
            to = lax.rem(chip + far, chips)
            for j, source in enumerate((act, x.at[to])):
                target = out.at[at, :, pl.ds(j * width, width)]
                copies.append(pltpu.make_async_copy(source, target, sems.at[k, far, j]))
                copies[-1].start()
    for copy in copies:
        copy.wait()


def pick_kernel(wanted, of_slots, deps, ids, section_map, *refs):
    chips = 4
    count = len(wanted)
    total = (2 if of_slots else count) * chips
    sources, (own_out, sib_out, rep_out, block, in_sems, sems) = refs[:total], refs[total + deps :]
    core, rep = ids[CORE], ids[REP]
    width = 2 * sib_out.shape[-1] - rep_out.shape[-1]
    span = rep_out.shape[-1] - sib_out.shape[-1]
    for n, layer in enumerate(wanted):
        section_core, slot, far = held_at(ids, section_map, layer)
        at = slot * chips + far if of_slots else n * chips + far
        for j in range(total) if of_slots else range(n * chips, (n + 1) * chips):

            def begin(n=n, j=j, section_core=section_core):
                source = sources[j].at[section_core] if of_slots else sources[j]
                pltpu.make_async_copy(source, block.at[n], in_sems.at[n]).start()

            pl.when(at == j)(begin)
    plan = ((own_out, [(rep, core)]), (sib_out, [(rep, 1 - core)]), (rep_out, [(1 - rep, core), (1 - rep, 1 - core)]))
    leaving = Copies(sems)
    for n in range(count):
        pltpu.make_async_copy(block.at[n], block.at[n], in_sems.at[n]).wait()
        for out, pieces in plan:
            leaving.start(block.at[n, :, pl.ds(0, width)], out.at[n, :, pl.ds(0, width)])
            for j, (replica, side) in enumerate(pieces):
                columns = pl.ds(pl.multiple_of(width + (replica * 2 + side) * span, span), span)
                leaving.start(block.at[n, :, columns], out.at[n, :, pl.ds(width + j * span, span)])
    leaving.wait()


def halves_kernel(starts, *refs):
    parts, (out_ref, sems) = refs[:4], refs[4:]
    arriving = Copies(sems)
    for k in range(4):
        arriving.start(parts[k].at[:, :, pl.ds(starts[k], out_ref.shape[-1])], out_ref.at[k])
    arriving.wait()


def gradient_kernel(whole, ids, *refs):
    value_ref, out_ref = refs[-2:]
    width = value_ref.shape[-1]
    first_side = ids[SIDE] == 0

    def factors(parts, mine=None, theirs=None):
        wide = jnp.concatenate([part[0][:, :width] for part in parts], axis=0)
        if mine is None:
            span = parts[0].shape[-1] - width
            starts = (width, width, width, width + span)
            return jnp.concatenate([p[0][:, i : i + span] for p, i in zip(parts, starts)], axis=0), wide
        mine, theirs = (jnp.concatenate([ref[k, 0] for k in range(4)], axis=0) for ref in (mine, theirs))
        left = jnp.where(first_side, mine, theirs)
        right = jnp.where(first_side, theirs, mine)
        return jnp.concatenate([left, right], axis=1), wide

    x, act = factors(refs[0:4], refs[4], refs[5])
    g, head = factors(refs[6:10]) if whole else factors(refs[6:10], refs[10], refs[11])
    value_ref[0] = lax.dot_general(x, head, TN, preferred_element_type=F32).astype(BF16)
    out_ref[0] = lax.dot_general(g, act, TN, preferred_element_type=F32).astype(BF16)


def gradients(ids, layers, first, count, forward, backward, before):
    quarter = forward[4].shape[-1]
    piece, width = 2 * quarter, forward[0].shape[-1] - quarter
    out = jax.ShapeDtypeStruct((layers, piece, width), BF16)
    out_spec = pl.BlockSpec((1, piece, width), lambda l: (first + l, 0, 0))

    def block(array, start):
        if array.ndim == 3:
            return pl.BlockSpec((1,) + array.shape[1:], lambda l: (start + l, 0, 0))
        return pl.BlockSpec((array.shape[0], 1) + array.shape[2:], lambda l: (0, start + l, 0, 0))

    specs = [SMEM] + [block(a, first) for a in forward] + [block(a, 0) for a in backward]
    operands = [ids] + list(forward) + list(backward)
    aliases = {}
    if before is not None:
        aliases = {len(operands): 0, len(operands) + 1: 1}
        operands, specs = operands + list(before), specs + [ANY, ANY]
    return pl.pallas_call(
        functools.partial(gradient_kernel, len(backward) == 4),
        out_shape=(out, out),
        grid=(count,),
        in_specs=specs,
        out_specs=(out_spec, out_spec),
        input_output_aliases=aliases,
        compiler_params=pltpu.CompilerParams(vmem_limit_bytes=VMEM_BYTES),
        cost_estimate=pl.CostEstimate(
            flops=count * 4 * piece * width * 256, bytes_accessed=count * 2400000, transcendentals=0
        ),
    )(*operands)


def per_device(section_map, checkpoint, top_grad, value_weight, out_weight):
    tp_total = lax.axis_size("tp")
    section_total = lax.axis_size("section")
    replica_total = lax.axis_size("rep")
    chips = section_total // 2
    rep, section, tp = (lax.axis_index(name) for name in ("rep", "section", "tp"))
    chip, core, side = section // 2, section % 2, tp % 2
    layers = section_map.shape[1]
    _, _, micro, tokens, model = checkpoint.shape
    slots, width = value_weight.shape[1], value_weight.shape[3]
    rows = micro * tokens
    cut = model // tp_total
    piece = model // (replica_total * section_total)
    v_own, o_own = value_weight[0], out_weight[0]
    x_pair, top_pair = checkpoint[0, 0], top_grad[0]

    ids = jnp.stack([rep, chip, core, side, tp]).astype(jnp.int32)

    chip_of = section_map // 2
    moves = chip_of[:, 1:] - chip_of[:, :-1]
    most_moves = jnp.max(moves, axis=0)

    swap = [(i, i ^ 1) for i in range(section_total)]

    def to_sibling(array):
        return lax.ppermute(array, "section", swap)

    def to_replica(array):
        return lax.ppermute(array, "rep", [(0, 1), (1, 0)])

    o_sib, v_sib = to_sibling(o_own), to_sibling(v_own)

    def shape(*dims, dtype=BF16):
        return jax.ShapeDtypeStruct(dims, dtype)

    def in_hbm(*dims):
        return pltpu.HBM(dims, BF16)

    def dma(*dims):
        return pltpu.SemaphoreType.DMA(dims)

    weight_bytes = model * width * 2
    weight_buffer = pltpu.VMEM((model, width), BF16)

    def reduce_slices(got, base, spread, *deps):
        count = got.shape[1]
        buffer = pltpu.VMEM((count, cut), BF16)
        return run(
            functools.partial(reduce_kernel, spread, len(deps)),
            (ids, got, base, *deps),
            [SMEM] + [ANY] * (2 + len(deps)),
            in_hbm(*got.shape) if spread else in_hbm(count, cut),
            HBM,
            [pltpu.VMEM(got.shape, BF16), buffer, buffer, dma(5), dma(tp_total if spread else 1)],
            got.size * 2,
        )

    def over_tp(parts):
        return lax.all_to_all(parts, "tp", 0, 0, tiled=True)

    def recompute_slot(slot, x, with_parts, deps=()):
        halves = (shape(tokens, width),) * 2 + (shape(tokens, width, dtype=F32),) * 2
        halves += (shape(chips, tokens, cut),) * 2
        outs = ((in_hbm(tp_total, rows, cut),) if with_parts else ()) + halves
        out_specs = ((HBM,) if with_parts else ()) + (VMEM,) * 6
        scratch = [pltpu.VMEM((tp_total, rows, cut), BF16), weight_buffer]
        scratch += [pltpu.VMEM((rows, width), BF16), pltpu.VMEM((rows, width), F32), dma(tp_total + 4), dma(2)]
        if with_parts:
            scratch += [weight_buffer, pltpu.VMEM((tp_total, rows, cut), BF16)]
        operands = (ids, x, v_own) + ((o_own,) if with_parts else ()) + tuple(deps)
        count = 2 if with_parts else 1
        return run(
            functools.partial(recompute, chips, with_parts, slot, len(deps)),
            operands,
            [SMEM] + [ANY] * (len(operands) - 1),
            outs,
            out_specs,
            scratch,
            count * weight_bytes,
            count * 2 * rows * model * width,
        )

    def along_chips(cuts):
        got = [cuts[0]]
        for far in range(1, chips):
            back = chips - far
            route = [(i, (i + 2 * back) % section_total) for i in range(section_total)]
            got.append(lax.ppermute(cuts[back], "section", route))
        return got

    def carve(act_mine, act_sib, x_mine, x_sib):
        block = in_hbm(2, tokens, width + cut)
        return run(
            functools.partial(carve_kernel, chips),
            (ids, act_mine, act_sib, x_mine, x_sib),
            [SMEM] + [VMEM] * 4,
            (block,) * chips,
            (HBM,) * chips,
            [dma(2, chips, 2)],
            2 * chips * tokens * (width + cut) * 4,
        )

    def to_owners(sources, wanted, of_slots, deps=()):
        count = len(wanted)
        columns = sources[0].shape[-1]
        span = (columns - width) // 4
        alone, both = in_hbm(count, tokens, width + span), in_hbm(count, tokens, width + 2 * span)
        own_out, sib_out, rep_out = run(
            functools.partial(pick_kernel, wanted, of_slots, len(deps)),
            (ids, section_map, *sources, *deps),
            [SMEM, SMEM] + [ANY] * (len(sources) + len(deps)),
            (alone, alone, both),
            (HBM,) * 3,
            [pltpu.VMEM((count, tokens, columns), BF16), dma(count), dma(7 * count)],
            count * tokens * columns * 6,
        )
        from_rep = to_replica(rep_out)
        parts = (own_out, to_sibling(sib_out), from_rep, to_sibling(from_rep))
        if span == piece:
            return parts
        mine = run(
            functools.partial(halves_kernel, (width, width, width, width + span)),
            parts,
            [ANY] * 4,
            shape(4, count, tokens, span),
            VMEM,
            [dma(4)],
            16 * count * tokens * span,
        )
        theirs = lax.ppermute(mine, "tp", [(i, i ^ 1) for i in range(tp_total)])
        return parts + (mine, theirs)

    x_rows = x_pair.reshape(rows, model)
    parts, act_mine_0, act_other_0, slope_mine_0, slope_other_0, x_mine_0, x_other_0 = recompute_slot(0, x_rows, True)
    act_sib_0, slope_sib_0, x_sib_0 = to_sibling(act_other_0), to_sibling(slope_other_0), to_sibling(x_other_0)
    first_cuts = carve(act_mine_0, act_sib_0, x_mine_0, x_sib_0)
    first_got = along_chips(first_cuts)
    x_second = over_tp(reduce_slices(over_tp(parts), x_rows, True))
    act_mine_1, act_other_1, slope_mine_1, slope_other_1, x_mine_1, x_other_1 = recompute_slot(
        1, x_second, False, first_cuts
    )
    slope_sib_1, act_sib_1, x_sib_1 = to_sibling(slope_other_1), to_sibling(act_other_1), to_sibling(x_other_1)
    second_cuts = carve(act_mine_1, act_sib_1, x_mine_1, x_sib_1)
    second_got = along_chips(second_cuts)
    slopes = (slope_mine_0, slope_mine_1, slope_sib_0, slope_sib_1)

    down = [(i, i - 2) for i in range(2, section_total)]
    earlier, middle = [3, 4, 5, 6, 7], [1, 2]

    def one_layer(layer, g, deps):
        last = layer == 0
        operands = (ids, section_map, g, *slopes, o_own, o_sib)
        operands += (() if last else (v_own, v_sib)) + tuple(deps)
        columns = width + (cut if layer in earlier else 2 * cut)
        block = in_hbm(tokens, columns)
        outs = (() if last else (in_hbm(tp_total, tokens, cut),)) + (block,) * chips
        scratch = [pltpu.VMEM((tp_total, tokens, cut), BF16), pltpu.VMEM((tokens, width), F32), weight_buffer]
        scratch += [pltpu.VMEM((chips, tokens, columns), BF16), dma(tp_total + 5), dma(chips + 2)]
        if not last:
            scratch += [weight_buffer, pltpu.VMEM((tp_total, tokens, cut), BF16)]
        count = 1 if last else 2
        result = run(
            functools.partial(step, chips, layer, len(deps)),
            operands,
            [SMEM, SMEM] + [ANY] * (len(operands) - 2),
            outs,
            (HBM,) * len(outs),
            scratch,
            count * weight_bytes,
            count * 2 * tokens * model * width,
        )
        return (None if last else result[0]), along_chips(result[-chips:])

    g = top_pair
    got_at = [None] * layers
    deps = {layer: [] for layer in range(layers)}

    def collect(wanted, deps=()):
        return to_owners([array for layer in wanted for array in got_at[layer]], wanted, False, deps)

    for layer in reversed(range(layers)):
        if layer == 7:
            deps[7] += first_got
        if layer == 6:
            deps[6] += list(second_cuts) + got_at[7][2:3]
        if layer == 5:
            deps[5] += second_got[1::2]
        if layer == 4:
            deps[4] += second_got[2:3] + got_at[6][2:3]
        if layer == 3:
            deps[3] += got_at[5][2:3] + got_at[4][2:3]
        if layer == 2:
            deps[2] += got_at[3][2:3] + list(forward[:4])
            earlier_all = collect(earlier)
        if layer == 1:
            deps[1] += got_at[2][2:3] + list(earlier_all[2:3])
        if layer == 0:
            result = gradients(ids, layers, earlier[0], len(earlier), forward, earlier_all, None)
            deps[0] += got_at[1][2:3] + list(result)
        parts, got_at[layer] = one_layer(layer, g, deps[layer])
        if layer == 0:
            break
        got = over_tp(parts)
        most = most_moves[layer - 1]

        def stay(*operands):
            return reduce_slices(*operands[:2], True, *operands[2:])

        def settle(kept, came, layer=layer):
            return run(
                functools.partial(settle_kernel, layer),
                (ids, section_map, kept, came),
                [SMEM, SMEM, ANY, ANY],
                in_hbm(tp_total, tokens, cut),
                HBM,
                [pltpu.VMEM((tokens, cut), BF16), dma(1), dma(tp_total)],
                tp_total * tokens * cut * 2,
            )

        def go_one(*operands):
            mine = reduce_slices(*operands[:2], False, *operands[2:])
            return settle(mine, lax.ppermute(mine, "section", down))

        def go_far(*operands, layer=layer, most=most):
            mine = reduce_slices(*operands[:2], False, *operands[2:])
            my_move = lax.dynamic_index_in_dim(moves, rep, 0, keepdims=False)[layer - 1]

            def hop(i, value):
                came = lax.ppermute(value, "section", down)
                return jnp.where(i < my_move, came, value)

            mine = lax.fori_loop(0, most, hop, mine)
            return settle(mine, mine)

        near = got_at[layer][1::2]
        spread = lax.switch(jnp.minimum(most, 2), (stay, go_one, go_far), got, g, *near)
        g = over_tp(spread)
        if layer == 4:
            forward = to_owners(first_got + second_got, list(range(layers)), True, (spread,))

    middle_all = collect(middle, got_at[0][:1])
    last_all = collect([0])
    result = gradients(ids, layers, middle[0], len(middle), forward, middle_all, result)
    return gradients(ids, layers, 0, 1, forward, last_all, result)


def solution(mesh):
    placed = (
        P(),
        P("rep", "section", None, None, None),
        P("rep", None, None, None),
        P("rep", "section", None, "tp"),
        P("rep", "section", None, "tp"),
    )
    return jax.shard_map(
        per_device,
        mesh=mesh,
        in_specs=placed,
        out_specs=(P(None, ("rep", "section"), "tp"), P(None, ("rep", "section"), "tp")),
        check_vma=False,
    )
```

```python
import functools

import jax
import jax.numpy as jnp
from jax import lax
from jax.experimental import pallas as pl
from jax.experimental.pallas import tpu as pltpu
from jax.sharding import PartitionSpec as P

BF16 = jnp.bfloat16
F32 = jnp.float32
VMEM_BYTES = 64 * 1024 * 1024
NT = (((1,), (1,)), ((), ()))
TN = (((0,), (0,)), ((), ()))
ANY = pl.BlockSpec(memory_space=pl.ANY)
HBM = pl.BlockSpec(memory_space=pltpu.HBM)
SMEM = pl.BlockSpec(memory_space=pltpu.SMEM)
VMEM = pl.BlockSpec(memory_space=pltpu.VMEM)


REP, CHIP, CORE, SIDE, TP = range(5)


def held_at(ids, section_map, layer):
    section = section_map[ids[REP], layer]
    slot = jnp.int32(0)
    if layer > 0:
        slot = (section_map[ids[REP], layer - 1] == section).astype(jnp.int32)
    chips = 4
    return lax.rem(section, 2), slot, lax.rem(section // 2 - ids[CHIP] + chips, chips)


def silu_slope(preact):
    sigma = jax.nn.sigmoid(preact)
    return sigma * (1.0 + preact * (1.0 - sigma))


def run(kernel, operands, specs, outs, out_specs, scratch, bytes_moved, flops=0):
    return pl.pallas_call(
        kernel,
        out_shape=outs,
        in_specs=specs,
        out_specs=out_specs,
        scratch_shapes=scratch,
        compiler_params=pltpu.CompilerParams(vmem_limit_bytes=VMEM_BYTES),
        cost_estimate=pl.CostEstimate(flops=flops, bytes_accessed=bytes_moved, transcendentals=0),
    )(*operands)


def rows_place(ref, cut, core):
    if len(ref.shape) == 3 and ref.shape[-1] == cut:
        return lambda i: ref.at[i]
    columns = lambda i: pl.ds(pl.multiple_of(i * cut, cut), cut)
    if len(ref.shape) == 2:
        return lambda i: ref.at[:, columns(i)]
    return lambda i: ref.at[core, :, columns(i)]


class Copies:
    def __init__(self, sems):
        self.sems, self.all = sems, []

    def start(self, source, target, condition=None):
        copy = pltpu.make_async_copy(source, target, self.sems.at[len(self.all)])
        if condition is None:
            copy.start()
        else:
            pl.when(condition)(copy.start)
        self.all.append(copy)
        return copy

    def either(self, condition, first, second, target):
        sem = self.sems.at[len(self.all)]
        pl.when(condition)(lambda: pltpu.make_async_copy(first, target, sem).start())
        pl.when(jnp.logical_not(condition))(lambda: pltpu.make_async_copy(second, target, sem).start())
        self.all.append(pltpu.make_async_copy(first, target, sem))
        return self.all[-1]

    def wait(self):
        for copy in self.all:
            copy.wait()


def halves(ref):
    step = ref.shape[0] // 2
    return [pl.ds(i * step, step) for i in range(2)]


def product_in(rows, weight, waits):
    cuts, cut = rows.shape[0], rows.shape[-1]
    total = None
    for i in range(cuts):
        if i % (cuts // len(waits)) == 0:
            waits[i // (cuts // len(waits))].wait()
        part = jnp.dot(rows[i], weight[i * cut : (i + 1) * cut, :], preferred_element_type=F32)
        total = part if total is None else total + part
    return total


def product_out(rows, weight, waits, stage, part_ref, out):
    cuts, cut = stage.shape[0], stage.shape[-1]
    group = cuts // len(waits)
    for i in range(cuts):
        if i % group == 0:
            waits[i // group].wait()
        part = lax.dot_general(rows, weight[i * cut : (i + 1) * cut, :], NT, preferred_element_type=F32)
        stage[i] = part.astype(BF16)
        if i % group == group - 1:
            cuts_done = pl.ds(i - group + 1, group)
            out.start(stage.at[cuts_done], part_ref.at[cuts_done])


def recompute(chips, with_parts, slot, deps, ids, x_ref, v_ref, *refs):
    o_ref, refs = (refs[0], refs[1:]) if with_parts else (None, refs)
    refs = refs[deps:]
    part_ref, refs = (refs[0], refs[1:]) if with_parts else (None, refs)
    outs, (xbuf, vbuf, act_rows, slope_rows, in_sems, out_sems) = refs[:6], refs[6:12]
    cuts, cut = xbuf.shape[0], xbuf.shape[-1]
    core, side = ids[CORE], ids[SIDE]
    arriving, leaving = Copies(in_sems), Copies(out_sems)
    x = [arriving.start(rows_place(x_ref, cut, core)(i), xbuf.at[i]) for i in range(cuts)]
    v = [arriving.start(v_ref.at[slot, rows], vbuf.at[rows]) for rows in halves(vbuf)]
    if with_parts:
        obuf, stage = refs[12:]
        o = [arriving.start(o_ref.at[slot, rows], obuf.at[rows]) for rows in halves(obuf)]
    for copy in x:
        copy.wait()
    pre = product_in(xbuf, vbuf, v)
    act = jax.nn.silu(pre).astype(BF16)
    if with_parts:
        product_out(act, obuf, o, stage, part_ref, leaving)
    act_rows[...] = act
    slope_rows[...] = silu_slope(pre)
    half = outs[0].shape[0]
    quarter = cut // 4
    for k, which in enumerate((core, 1 - core)):
        rows = pl.ds(pl.multiple_of(which * half, half), half)
        act_out, slope_out, x_out = outs[k], outs[2 + k], outs[4 + k]
        act_out[...] = act_rows[rows, :]
        slope_out[...] = slope_rows[rows, :]
        for to in range(chips):
            for j in range(4):
                columns = pl.ds(pl.multiple_of((j % 2) * 2 * quarter + side * quarter, quarter), quarter)
                x_out[to, :, j * quarter : (j + 1) * quarter] = xbuf[(j // 2) * chips + to, rows, columns]
    leaving.wait()


def step(chips, layer, deps, ids, section_map, g_ref, *refs):
    with_parts = layer > 0
    slopes, refs = refs[:4], refs[4:]
    o_refs, refs = refs[:2], refs[2:]
    v_refs, refs = (refs[:2], refs[2:]) if with_parts else (None, refs)
    refs = refs[deps:]
    part_ref, refs = (refs[0], refs[1:]) if with_parts else (None, refs)
    outs, (gbuf, sbuf, obuf, pay, in_sems, out_sems) = refs[:chips], refs[chips : chips + 6]
    cut, width = gbuf.shape[-1], sbuf.shape[-1]
    span = (pay.shape[-1] - width) // 4
    chip, core, side = ids[CHIP], ids[CORE], ids[SIDE]
    section_core, slot, _ = held_at(ids, section_map, layer)
    own = section_core == core
    arriving, leaving = Copies(in_sems), Copies(out_sems)
    if g_ref.shape == gbuf.shape:
        g = [arriving.start(g_ref, gbuf)]
    else:
        g = [arriving.start(rows_place(g_ref, cut, core)(i), gbuf.at[i]) for i in range(gbuf.shape[0])]
    o = [arriving.either(own, o_refs[0].at[slot, r], o_refs[1].at[slot, r], obuf.at[r]) for r in halves(obuf)]
    which = jnp.where(own, 0, 2) + slot
    for j in range(4):
        pl.when(which == j)(pltpu.make_async_copy(slopes[j], sbuf, in_sems.at[-1 + in_sems.shape[0]]).start)
    slope = pltpu.make_async_copy(slopes[0], sbuf, in_sems.at[-1 + in_sems.shape[0]])
    if with_parts:
        vbuf, stage = refs[chips + 6 :]
        v = [arriving.either(own, v_refs[0].at[slot, r], v_refs[1].at[slot, r], vbuf.at[r]) for r in halves(vbuf)]
    for copy in g:
        copy.wait()
    for far in range(chips):
        to = lax.rem(chip + far, chips)
        for j in range(4):
            start = (j % 2) * (cut // 2) + (0 if span == cut // 2 else side * span)
            columns = pl.ds(start if span == cut // 2 else pl.multiple_of(start, span), span)
            pay[far, :, width + j * span : width + (j + 1) * span] = gbuf[(j // 2) * chips + to, :, columns]
    total = product_in(gbuf, obuf, o)
    slope.wait()
    head = (total * sbuf[...]).astype(BF16)
    for far, out in enumerate(outs):
        pay[far, :, :width] = head
        leaving.start(pay.at[far], out)
    if with_parts:
        product_out(head, vbuf, v, stage, part_ref, leaving)
    leaving.wait()


def reduce_kernel(spread, deps, ids, got_ref, base_ref, *refs):
    out_ref, got, base, stage, sems, out_sems = refs[deps:]
    cuts, cut = got.shape[0], got.shape[-1]
    arriving, leaving = Copies(sems), Copies(out_sems)
    arriving.start(rows_place(base_ref, cut, ids[CORE])(ids[TP]), base)
    for i in range(4):
        some = pl.ds(i * (cuts // 4), cuts // 4)
        arriving.start(got_ref.at[some], got.at[some])
    arriving.wait()
    total = got[0].astype(F32)
    for i in range(1, cuts):
        total += got[i].astype(F32)
    stage[...] = (base[...].astype(F32) + total).astype(BF16)
    for i in range(cuts if spread else 1):
        leaving.start(stage, out_ref.at[i] if spread else out_ref)
    leaving.wait()


def settle_kernel(layer, ids, section_map, kept_ref, came_ref, out_ref, stage, sems, out_sems):
    rep = ids[REP]
    moved = section_map[rep, layer] // 2 > section_map[rep, layer - 1] // 2
    arriving, leaving = Copies(sems), Copies(out_sems)
    arriving.either(moved, came_ref, kept_ref, stage)
    arriving.wait()
    for i in range(out_ref.shape[0]):
        leaving.start(stage, out_ref.at[i])
    leaving.wait()


def carve_kernel(chips, ids, act_mine, act_sib, x_mine, x_sib, *refs):
    outs, sems = refs[:chips], refs[chips]
    chip, core = ids[CHIP], ids[CORE]
    width = act_mine.shape[-1]
    copies = []
    for k, (act, x) in enumerate(((act_mine, x_mine), (act_sib, x_sib))):
        at = core if k == 0 else 1 - core
        for far, out in enumerate(outs):
            to = lax.rem(chip + far, chips)
            for j, source in enumerate((act, x.at[to])):
                target = out.at[at, :, pl.ds(j * width, width)]
                copies.append(pltpu.make_async_copy(source, target, sems.at[k, far, j]))
                copies[-1].start()
    for copy in copies:
        copy.wait()


def pick_kernel(wanted, of_slots, deps, ids, section_map, *refs):
    chips = 4
    count = len(wanted)
    total = (2 if of_slots else count) * chips
    sources, (own_out, sib_out, rep_out, block, in_sems, sems) = refs[:total], refs[total + deps :]
    core, rep = ids[CORE], ids[REP]
    width = 2 * sib_out.shape[-1] - rep_out.shape[-1]
    span = rep_out.shape[-1] - sib_out.shape[-1]
    for n, layer in enumerate(wanted):
        section_core, slot, far = held_at(ids, section_map, layer)
        at = slot * chips + far if of_slots else n * chips + far
        for j in range(total) if of_slots else range(n * chips, (n + 1) * chips):

            def begin(n=n, j=j, section_core=section_core):
                source = sources[j].at[section_core] if of_slots else sources[j]
                pltpu.make_async_copy(source, block.at[n], in_sems.at[n]).start()

            pl.when(at == j)(begin)
    plan = ((own_out, [(rep, core)]), (sib_out, [(rep, 1 - core)]), (rep_out, [(1 - rep, core), (1 - rep, 1 - core)]))
    leaving = Copies(sems)
    for n in range(count):
        pltpu.make_async_copy(block.at[n], block.at[n], in_sems.at[n]).wait()
        for out, pieces in plan:
            leaving.start(block.at[n, :, pl.ds(0, width)], out.at[n, :, pl.ds(0, width)])
            for j, (replica, side) in enumerate(pieces):
                columns = pl.ds(pl.multiple_of(width + (replica * 2 + side) * span, span), span)
                leaving.start(block.at[n, :, columns], out.at[n, :, pl.ds(width + j * span, span)])
    leaving.wait()


def halves_kernel(starts, *refs):
    parts, (out_ref, sems) = refs[:4], refs[4:]
    arriving = Copies(sems)
    for k in range(4):
        arriving.start(parts[k].at[:, :, pl.ds(starts[k], out_ref.shape[-1])], out_ref.at[k])
    arriving.wait()


def gradient_kernel(whole, ids, *refs):
    value_ref, out_ref = refs[-2:]
    width = value_ref.shape[-1]
    first_side = ids[SIDE] == 0

    def factors(parts, mine=None, theirs=None):
        wide = jnp.concatenate([part[0][:, :width] for part in parts], axis=0)
        if mine is None:
            span = parts[0].shape[-1] - width
            starts = (width, width, width, width + span)
            return jnp.concatenate([p[0][:, i : i + span] for p, i in zip(parts, starts)], axis=0), wide
        mine, theirs = (jnp.concatenate([ref[k, 0] for k in range(4)], axis=0) for ref in (mine, theirs))
        left = jnp.where(first_side, mine, theirs)
        right = jnp.where(first_side, theirs, mine)
        return jnp.concatenate([left, right], axis=1), wide

    x, act = factors(refs[0:4], refs[4], refs[5])
    g, head = factors(refs[6:10]) if whole else factors(refs[6:10], refs[10], refs[11])
    value_ref[0] = lax.dot_general(x, head, TN, preferred_element_type=F32).astype(BF16)
    out_ref[0] = lax.dot_general(g, act, TN, preferred_element_type=F32).astype(BF16)


def gradients(ids, layers, first, count, forward, backward, before):
    quarter = forward[4].shape[-1]
    piece, width = 2 * quarter, forward[0].shape[-1] - quarter
    out = jax.ShapeDtypeStruct((layers, piece, width), BF16)
    out_spec = pl.BlockSpec((1, piece, width), lambda l: (first + l, 0, 0))

    def block(array, start):
        if array.ndim == 3:
            return pl.BlockSpec((1,) + array.shape[1:], lambda l: (start + l, 0, 0))
        return pl.BlockSpec((array.shape[0], 1) + array.shape[2:], lambda l: (0, start + l, 0, 0))

    specs = [SMEM] + [block(a, first) for a in forward] + [block(a, 0) for a in backward]
    operands = [ids] + list(forward) + list(backward)
    aliases = {}
    if before is not None:
        aliases = {len(operands): 0, len(operands) + 1: 1}
        operands, specs = operands + list(before), specs + [ANY, ANY]
    return pl.pallas_call(
        functools.partial(gradient_kernel, len(backward) == 4),
        out_shape=(out, out),
        grid=(count,),
        in_specs=specs,
        out_specs=(out_spec, out_spec),
        input_output_aliases=aliases,
        compiler_params=pltpu.CompilerParams(vmem_limit_bytes=VMEM_BYTES),
        cost_estimate=pl.CostEstimate(
            flops=count * 4 * piece * width * 256, bytes_accessed=count * 2400000, transcendentals=0
        ),
    )(*operands)


def per_device(section_map, checkpoint, top_grad, value_weight, out_weight):
    tp_total = lax.axis_size("tp")
    section_total = lax.axis_size("section")
    replica_total = lax.axis_size("rep")
    chips = section_total // 2
    rep, section, tp = (lax.axis_index(name) for name in ("rep", "section", "tp"))
    chip, core, side = section // 2, section % 2, tp % 2
    layers = section_map.shape[1]
    _, _, micro, tokens, model = checkpoint.shape
    slots, width = value_weight.shape[1], value_weight.shape[3]
    rows = micro * tokens
    cut = model // tp_total
    piece = model // (replica_total * section_total)
    v_own, o_own = value_weight[0], out_weight[0]
    x_pair, top_pair = checkpoint[0, 0], top_grad[0]

    ids = jnp.stack([rep, chip, core, side, tp]).astype(jnp.int32)

    chip_of = section_map // 2
    moves = chip_of[:, 1:] - chip_of[:, :-1]
    most_moves = jnp.max(moves, axis=0)

    swap = [(i, i ^ 1) for i in range(section_total)]

    def to_sibling(array):
        return lax.ppermute(array, "section", swap)

    def to_replica(array):
        return lax.ppermute(array, "rep", [(0, 1), (1, 0)])

    o_sib, v_sib = to_sibling(o_own), to_sibling(v_own)

    def shape(*dims, dtype=BF16):
        return jax.ShapeDtypeStruct(dims, dtype)

    def in_hbm(*dims):
        return pltpu.HBM(dims, BF16)

    def dma(*dims):
        return pltpu.SemaphoreType.DMA(dims)

    weight_bytes = model * width * 2
    weight_buffer = pltpu.VMEM((model, width), BF16)

    def reduce_slices(got, base, spread, *deps):
        count = got.shape[1]
        buffer = pltpu.VMEM((count, cut), BF16)
        return run(
            functools.partial(reduce_kernel, spread, len(deps)),
            (ids, got, base, *deps),
            [SMEM] + [ANY] * (2 + len(deps)),
            in_hbm(*got.shape) if spread else in_hbm(count, cut),
            HBM,
            [pltpu.VMEM(got.shape, BF16), buffer, buffer, dma(5), dma(tp_total if spread else 1)],
            got.size * 2,
        )

    def over_tp(parts):
        return lax.all_to_all(parts, "tp", 0, 0, tiled=True)

    def recompute_slot(slot, x, with_parts, deps=()):
        halves = (shape(tokens, width),) * 2 + (shape(tokens, width, dtype=F32),) * 2
        halves += (shape(chips, tokens, cut),) * 2
        outs = ((in_hbm(tp_total, rows, cut),) if with_parts else ()) + halves
        out_specs = ((HBM,) if with_parts else ()) + (VMEM,) * 6
        scratch = [pltpu.VMEM((tp_total, rows, cut), BF16), weight_buffer]
        scratch += [pltpu.VMEM((rows, width), BF16), pltpu.VMEM((rows, width), F32), dma(tp_total + 4), dma(2)]
        if with_parts:
            scratch += [weight_buffer, pltpu.VMEM((tp_total, rows, cut), BF16)]
        operands = (ids, x, v_own) + ((o_own,) if with_parts else ()) + tuple(deps)
        count = 2 if with_parts else 1
        return run(
            functools.partial(recompute, chips, with_parts, slot, len(deps)),
            operands,
            [SMEM] + [ANY] * (len(operands) - 1),
            outs,
            out_specs,
            scratch,
            count * weight_bytes,
            count * 2 * rows * model * width,
        )

    def along_chips(cuts):
        got = [cuts[0]]
        for far in range(1, chips):
            back = chips - far
            route = [(i, (i + 2 * back) % section_total) for i in range(section_total)]
            got.append(lax.ppermute(cuts[back], "section", route))
        return got

    def carve(act_mine, act_sib, x_mine, x_sib):
        block = in_hbm(2, tokens, width + cut)
        return run(
            functools.partial(carve_kernel, chips),
            (ids, act_mine, act_sib, x_mine, x_sib),
            [SMEM] + [VMEM] * 4,
            (block,) * chips,
            (HBM,) * chips,
            [dma(2, chips, 2)],
            2 * chips * tokens * (width + cut) * 4,
        )

    def to_owners(sources, wanted, of_slots, deps=(), later=None):
        count = len(wanted)
        columns = sources[0].shape[-1]
        span = (columns - width) // 4
        alone, both = in_hbm(count, tokens, width + span), in_hbm(count, tokens, width + 2 * span)
        own_out, sib_out, rep_out = run(
            functools.partial(pick_kernel, wanted, of_slots, len(deps)),
            (ids, section_map, *sources, *deps),
            [SMEM, SMEM] + [ANY] * (len(sources) + len(deps)),
            (alone, alone, both),
            (HBM,) * 3,
            [pltpu.VMEM((count, tokens, columns), BF16), dma(count), dma(7 * count)],
            count * tokens * columns * 6,
        )
        from_rep = to_replica(rep_out)
        if later is not None:
            from_rep, later = lax.optimization_barrier((from_rep, later))
        parts = (own_out, to_sibling(sib_out), from_rep, to_sibling(from_rep))
        if span == piece:
            return parts, later
        mine = run(
            functools.partial(halves_kernel, (width, width, width, width + span)),
            parts,
            [ANY] * 4,
            shape(4, count, tokens, span),
            VMEM,
            [dma(4)],
            16 * count * tokens * span,
        )
        theirs = lax.ppermute(mine, "tp", [(i, i ^ 1) for i in range(tp_total)])
        return parts + (mine, theirs)

    x_rows = x_pair.reshape(rows, model)
    parts, act_mine_0, act_other_0, slope_mine_0, slope_other_0, x_mine_0, x_other_0 = recompute_slot(0, x_rows, True)
    act_sib_0, slope_sib_0, x_sib_0 = to_sibling(act_other_0), to_sibling(slope_other_0), to_sibling(x_other_0)
    first_cuts = carve(act_mine_0, act_sib_0, x_mine_0, x_sib_0)
    first_got = along_chips(first_cuts)
    x_second = over_tp(reduce_slices(over_tp(parts), x_rows, True))
    act_mine_1, act_other_1, slope_mine_1, slope_other_1, x_mine_1, x_other_1 = recompute_slot(
        1, x_second, False, first_cuts
    )
    slope_sib_1, act_sib_1, x_sib_1 = to_sibling(slope_other_1), to_sibling(act_other_1), to_sibling(x_other_1)
    second_cuts = carve(act_mine_1, act_sib_1, x_mine_1, x_sib_1)
    second_got = along_chips(second_cuts)
    slopes = (slope_mine_0, slope_mine_1, slope_sib_0, slope_sib_1)

    down = [(i, i - 2) for i in range(2, section_total)]
    earlier, latest = [2, 3, 4, 5, 6, 7], [0, 1]

    def one_layer(layer, g, deps):
        last = layer == 0
        operands = (ids, section_map, g, *slopes, o_own, o_sib)
        operands += (() if last else (v_own, v_sib)) + tuple(deps)
        columns = width + (2 * cut if layer in latest else cut)
        block = in_hbm(tokens, columns)
        outs = (() if last else (in_hbm(tp_total, tokens, cut),)) + (block,) * chips
        scratch = [pltpu.VMEM((tp_total, tokens, cut), BF16), pltpu.VMEM((tokens, width), F32), weight_buffer]
        scratch += [pltpu.VMEM((chips, tokens, columns), BF16), dma(tp_total + 5), dma(chips + 2)]
        if not last:
            scratch += [weight_buffer, pltpu.VMEM((tp_total, tokens, cut), BF16)]
        count = 1 if last else 2
        result = run(
            functools.partial(step, chips, layer, len(deps)),
            operands,
            [SMEM, SMEM] + [ANY] * (len(operands) - 2),
            outs,
            (HBM,) * len(outs),
            scratch,
            count * weight_bytes,
            count * 2 * tokens * model * width,
        )
        return (None if last else result[0]), along_chips(result[-chips:])

    g = top_pair
    got_at = [None] * layers
    deps = {layer: [] for layer in range(layers)}

    def collect(wanted, deps=(), later=None):
        return to_owners([array for layer in wanted for array in got_at[layer]], wanted, False, deps, later)

    for layer in reversed(range(layers)):
        if layer == 7:
            deps[7] += first_got
        if layer == 6:
            deps[6] += list(second_cuts) + got_at[7][2:3]
        if layer == 5:
            deps[5] += second_got[1::2]
        if layer == 4:
            deps[4] += second_got[2:3] + got_at[6][2:3]
            forward = to_owners(first_got + second_got, list(range(layers)), True)
        if layer == 3:
            deps[3] += got_at[5][2:3] + got_at[4][2:3]
        if layer == 2:
            deps[2] += got_at[3][2:3] + list(forward[:4])
        if layer == 1:
            deps[1] += got_at[2][2:3]
            earlier_all = collect(earlier)
        if layer == 0:
            deps[0] += got_at[1][2:3] + list(earlier_all[:4])
        parts, got_at[layer] = one_layer(layer, g, deps[layer])
        if layer == 0:
            break
        got = over_tp(parts)
        most = most_moves[layer - 1]

        def stay(*operands):
            return reduce_slices(*operands[:2], True, *operands[2:])

        def settle(kept, came, layer=layer):
            return run(
                functools.partial(settle_kernel, layer),
                (ids, section_map, kept, came),
                [SMEM, SMEM, ANY, ANY],
                in_hbm(tp_total, tokens, cut),
                HBM,
                [pltpu.VMEM((tokens, cut), BF16), dma(1), dma(tp_total)],
                tp_total * tokens * cut * 2,
            )

        def go_one(*operands):
            mine = reduce_slices(*operands[:2], False, *operands[2:])
            return settle(mine, lax.ppermute(mine, "section", down))

        def go_far(*operands, layer=layer, most=most):
            mine = reduce_slices(*operands[:2], False, *operands[2:])
            my_move = lax.dynamic_index_in_dim(moves, rep, 0, keepdims=False)[layer - 1]

            def hop(i, value):
                came = lax.ppermute(value, "section", down)
                return jnp.where(i < my_move, came, value)

            mine = lax.fori_loop(0, most, hop, mine)
            return settle(mine, mine)

        near = got_at[layer][1::2]
        spread = lax.switch(jnp.minimum(most, 2), (stay, go_one, go_far), got, g, *near)
        g = over_tp(spread)

    result = gradients(ids, layers, earlier[0], len(earlier), forward, earlier_all, None)
    latest_all, result = collect(latest, (), result)
    return gradients(ids, layers, latest[0], len(latest), forward, latest_all, result)


def solution(mesh):
    placed = (
        P(),
        P("rep", "section", None, None, None),
        P("rep", None, None, None),
        P("rep", "section", None, "tp"),
        P("rep", "section", None, "tp"),
    )
    return jax.shard_map(
        per_device,
        mesh=mesh,
        in_specs=placed,
        out_specs=(P(None, ("rep", "section"), "tp"), P(None, ("rep", "section"), "tp")),
        check_vma=False,
    )
```

```python
import functools

import jax
import jax.numpy as jnp
from jax import lax
from jax.experimental import pallas as pl
from jax.experimental.pallas import tpu as pltpu
from jax.sharding import PartitionSpec as P

BF16 = jnp.bfloat16
F32 = jnp.float32
VMEM_BYTES = 64 * 1024 * 1024
NT = (((1,), (1,)), ((), ()))
TN = (((0,), (0,)), ((), ()))
ANY = pl.BlockSpec(memory_space=pl.ANY)
HBM = pl.BlockSpec(memory_space=pltpu.HBM)
SMEM = pl.BlockSpec(memory_space=pltpu.SMEM)
VMEM = pl.BlockSpec(memory_space=pltpu.VMEM)


REP, CHIP, CORE, SIDE, TP = range(5)


def held_at(ids, section_map, layer):
    section = section_map[ids[REP], layer]
    slot = jnp.int32(0)
    if layer > 0:
        slot = (section_map[ids[REP], layer - 1] == section).astype(jnp.int32)
    chips = 4
    return lax.rem(section, 2), slot, lax.rem(section // 2 - ids[CHIP] + chips, chips)


def silu_slope(preact):
    sigma = jax.nn.sigmoid(preact)
    return sigma * (1.0 + preact * (1.0 - sigma))


def run(kernel, operands, specs, outs, out_specs, scratch, bytes_moved, flops=0):
    return pl.pallas_call(
        kernel,
        out_shape=outs,
        in_specs=specs,
        out_specs=out_specs,
        scratch_shapes=scratch,
        compiler_params=pltpu.CompilerParams(vmem_limit_bytes=VMEM_BYTES),
        cost_estimate=pl.CostEstimate(flops=flops, bytes_accessed=bytes_moved, transcendentals=0),
    )(*operands)


def rows_place(ref, cut, core):
    if len(ref.shape) == 3 and ref.shape[-1] == cut:
        return lambda i: ref.at[i]
    columns = lambda i: pl.ds(pl.multiple_of(i * cut, cut), cut)
    if len(ref.shape) == 2:
        return lambda i: ref.at[:, columns(i)]
    return lambda i: ref.at[core, :, columns(i)]


class Copies:
    def __init__(self, sems):
        self.sems, self.all = sems, []

    def start(self, source, target, condition=None):
        copy = pltpu.make_async_copy(source, target, self.sems.at[len(self.all)])
        if condition is None:
            copy.start()
        else:
            pl.when(condition)(copy.start)
        self.all.append(copy)
        return copy

    def either(self, condition, first, second, target):
        sem = self.sems.at[len(self.all)]
        pl.when(condition)(lambda: pltpu.make_async_copy(first, target, sem).start())
        pl.when(jnp.logical_not(condition))(lambda: pltpu.make_async_copy(second, target, sem).start())
        self.all.append(pltpu.make_async_copy(first, target, sem))
        return self.all[-1]

    def wait(self):
        for copy in self.all:
            copy.wait()


def halves(ref):
    step = ref.shape[0] // 2
    return [pl.ds(i * step, step) for i in range(2)]


def product_in(rows, weight, waits):
    cuts, cut = rows.shape[0], rows.shape[-1]
    total = None
    for i in range(cuts):
        if i % (cuts // len(waits)) == 0:
            waits[i // (cuts // len(waits))].wait()
        part = jnp.dot(rows[i], weight[i * cut : (i + 1) * cut, :], preferred_element_type=F32)
        total = part if total is None else total + part
    return total


def product_out(rows, weight, waits, stage, part_ref, out):
    cuts, cut = stage.shape[0], stage.shape[-1]
    group = cuts // len(waits)
    for i in range(cuts):
        if i % group == 0:
            waits[i // group].wait()
        part = lax.dot_general(rows, weight[i * cut : (i + 1) * cut, :], NT, preferred_element_type=F32)
        stage[i] = part.astype(BF16)
        if i % group == group - 1:
            cuts_done = pl.ds(i - group + 1, group)
            out.start(stage.at[cuts_done], part_ref.at[cuts_done])


def recompute(chips, with_parts, slot, deps, ids, x_ref, v_ref, *refs):
    o_ref, refs = (refs[0], refs[1:]) if with_parts else (None, refs)
    refs = refs[deps:]
    part_ref, refs = (refs[0], refs[1:]) if with_parts else (None, refs)
    outs, (xbuf, vbuf, act_rows, slope_rows, in_sems, out_sems) = refs[:6], refs[6:12]
    cuts, cut = xbuf.shape[0], xbuf.shape[-1]
    core, side = ids[CORE], ids[SIDE]
    arriving, leaving = Copies(in_sems), Copies(out_sems)
    x = [arriving.start(rows_place(x_ref, cut, core)(i), xbuf.at[i]) for i in range(cuts)]
    v = [arriving.start(v_ref.at[slot, rows], vbuf.at[rows]) for rows in halves(vbuf)]
    if with_parts:
        obuf, stage = refs[12:]
        o = [arriving.start(o_ref.at[slot, rows], obuf.at[rows]) for rows in halves(obuf)]
    for copy in x:
        copy.wait()
    pre = product_in(xbuf, vbuf, v)
    act = jax.nn.silu(pre).astype(BF16)
    if with_parts:
        product_out(act, obuf, o, stage, part_ref, leaving)
    act_rows[...] = act
    slope_rows[...] = silu_slope(pre)
    half = outs[0].shape[0]
    quarter = cut // 4
    for k, which in enumerate((core, 1 - core)):
        rows = pl.ds(pl.multiple_of(which * half, half), half)
        act_out, slope_out, x_out = outs[k], outs[2 + k], outs[4 + k]
        act_out[...] = act_rows[rows, :]
        slope_out[...] = slope_rows[rows, :]
        for to in range(chips):
            for j in range(4):
                columns = pl.ds(pl.multiple_of((j % 2) * 2 * quarter + side * quarter, quarter), quarter)
                x_out[to, :, j * quarter : (j + 1) * quarter] = xbuf[(j // 2) * chips + to, rows, columns]
    leaving.wait()


def step(chips, layer, deps, ids, section_map, g_ref, *refs):
    with_parts = layer > 0
    slopes, refs = refs[:4], refs[4:]
    o_refs, refs = refs[:2], refs[2:]
    v_refs, refs = (refs[:2], refs[2:]) if with_parts else (None, refs)
    refs = refs[deps:]
    part_ref, refs = (refs[0], refs[1:]) if with_parts else (None, refs)
    outs, (gbuf, sbuf, obuf, pay, in_sems, out_sems) = refs[:chips], refs[chips : chips + 6]
    cut, width = gbuf.shape[-1], sbuf.shape[-1]
    span = (pay.shape[-1] - width) // 4
    chip, core, side = ids[CHIP], ids[CORE], ids[SIDE]
    section_core, slot, _ = held_at(ids, section_map, layer)
    own = section_core == core
    arriving, leaving = Copies(in_sems), Copies(out_sems)
    if g_ref.shape == gbuf.shape:
        g = [arriving.start(g_ref, gbuf)]
    else:
        g = [arriving.start(rows_place(g_ref, cut, core)(i), gbuf.at[i]) for i in range(gbuf.shape[0])]
    o = [arriving.either(own, o_refs[0].at[slot, r], o_refs[1].at[slot, r], obuf.at[r]) for r in halves(obuf)]
    which = jnp.where(own, 0, 2) + slot
    for j in range(4):
        pl.when(which == j)(pltpu.make_async_copy(slopes[j], sbuf, in_sems.at[-1 + in_sems.shape[0]]).start)
    slope = pltpu.make_async_copy(slopes[0], sbuf, in_sems.at[-1 + in_sems.shape[0]])
    if with_parts:
        vbuf, stage = refs[chips + 6 :]
        v = [arriving.either(own, v_refs[0].at[slot, r], v_refs[1].at[slot, r], vbuf.at[r]) for r in halves(vbuf)]
    for copy in g:
        copy.wait()
    for far in range(chips):
        to = lax.rem(chip + far, chips)
        for j in range(4):
            start = (j % 2) * (cut // 2) + (0 if span == cut // 2 else side * span)
            columns = pl.ds(start if span == cut // 2 else pl.multiple_of(start, span), span)
            pay[far, :, width + j * span : width + (j + 1) * span] = gbuf[(j // 2) * chips + to, :, columns]
    total = product_in(gbuf, obuf, o)
    slope.wait()
    head = (total * sbuf[...]).astype(BF16)
    for far, out in enumerate(outs):
        pay[far, :, :width] = head
        leaving.start(pay.at[far], out)
    if with_parts:
        product_out(head, vbuf, v, stage, part_ref, leaving)
    leaving.wait()


def reduce_kernel(spread, deps, ids, got_ref, base_ref, *refs):
    out_ref, got, base, stage, sems, out_sems = refs[deps:]
    cuts, cut = got.shape[0], got.shape[-1]
    arriving, leaving = Copies(sems), Copies(out_sems)
    arriving.start(rows_place(base_ref, cut, ids[CORE])(ids[TP]), base)
    for i in range(4):
        some = pl.ds(i * (cuts // 4), cuts // 4)
        arriving.start(got_ref.at[some], got.at[some])
    arriving.wait()
    total = got[0].astype(F32)
    for i in range(1, cuts):
        total += got[i].astype(F32)
    stage[...] = (base[...].astype(F32) + total).astype(BF16)
    for i in range(cuts if spread else 1):
        leaving.start(stage, out_ref.at[i] if spread else out_ref)
    leaving.wait()


def settle_kernel(layer, ids, section_map, kept_ref, came_ref, out_ref, stage, sems, out_sems):
    rep = ids[REP]
    moved = section_map[rep, layer] // 2 > section_map[rep, layer - 1] // 2
    arriving, leaving = Copies(sems), Copies(out_sems)
    arriving.either(moved, came_ref, kept_ref, stage)
    arriving.wait()
    for i in range(out_ref.shape[0]):
        leaving.start(stage, out_ref.at[i])
    leaving.wait()


def carve_kernel(chips, ids, act_mine, act_sib, x_mine, x_sib, *refs):
    outs, sems = refs[:chips], refs[chips]
    chip, core = ids[CHIP], ids[CORE]
    width = act_mine.shape[-1]
    copies = []
    for k, (act, x) in enumerate(((act_mine, x_mine), (act_sib, x_sib))):
        at = core if k == 0 else 1 - core
        for far, out in enumerate(outs):
            to = lax.rem(chip + far, chips)
            for j, source in enumerate((act, x.at[to])):
                target = out.at[at, :, pl.ds(j * width, width)]
                copies.append(pltpu.make_async_copy(source, target, sems.at[k, far, j]))
                copies[-1].start()
    for copy in copies:
        copy.wait()


def pick_kernel(wanted, of_slots, deps, ids, section_map, *refs):
    chips = 4
    count = len(wanted)
    total = (2 if of_slots else count) * chips
    sources, (own_out, sib_out, rep_out, block, in_sems, sems) = refs[:total], refs[total + deps :]
    core, rep = ids[CORE], ids[REP]
    width = 2 * sib_out.shape[-1] - rep_out.shape[-1]
    span = rep_out.shape[-1] - sib_out.shape[-1]
    for n, layer in enumerate(wanted):
        section_core, slot, far = held_at(ids, section_map, layer)
        at = slot * chips + far if of_slots else n * chips + far
        for j in range(total) if of_slots else range(n * chips, (n + 1) * chips):

            def begin(n=n, j=j, section_core=section_core):
                source = sources[j].at[section_core] if of_slots else sources[j]
                pltpu.make_async_copy(source, block.at[n], in_sems.at[n]).start()

            pl.when(at == j)(begin)
    plan = ((own_out, [(rep, core)]), (sib_out, [(rep, 1 - core)]), (rep_out, [(1 - rep, core), (1 - rep, 1 - core)]))
    leaving = Copies(sems)
    for n in range(count):
        pltpu.make_async_copy(block.at[n], block.at[n], in_sems.at[n]).wait()
        for out, pieces in plan:
            leaving.start(block.at[n, :, pl.ds(0, width)], out.at[n, :, pl.ds(0, width)])
            for j, (replica, side) in enumerate(pieces):
                columns = pl.ds(pl.multiple_of(width + (replica * 2 + side) * span, span), span)
                leaving.start(block.at[n, :, columns], out.at[n, :, pl.ds(width + j * span, span)])
    leaving.wait()


def halves_kernel(starts, *refs):
    parts, (out_ref, sems) = refs[:4], refs[4:]
    arriving = Copies(sems)
    for k in range(4):
        arriving.start(parts[k].at[:, :, pl.ds(starts[k], out_ref.shape[-1])], out_ref.at[k])
    arriving.wait()


def gradient_kernel(whole, ids, *refs):
    value_ref, out_ref = refs[-2:]
    width = value_ref.shape[-1]
    first_side = ids[SIDE] == 0

    def factors(parts, mine=None, theirs=None):
        wide = jnp.concatenate([part[0][:, :width] for part in parts], axis=0)
        if mine is None:
            span = parts[0].shape[-1] - width
            starts = (width, width, width, width + span)
            return jnp.concatenate([p[0][:, i : i + span] for p, i in zip(parts, starts)], axis=0), wide
        mine, theirs = (jnp.concatenate([ref[k, 0] for k in range(4)], axis=0) for ref in (mine, theirs))
        left = jnp.where(first_side, mine, theirs)
        right = jnp.where(first_side, theirs, mine)
        return jnp.concatenate([left, right], axis=1), wide

    x, act = factors(refs[0:4], refs[4], refs[5])
    g, head = factors(refs[6:10]) if whole else factors(refs[6:10], refs[10], refs[11])
    value_ref[0] = lax.dot_general(x, head, TN, preferred_element_type=F32).astype(BF16)
    out_ref[0] = lax.dot_general(g, act, TN, preferred_element_type=F32).astype(BF16)


def gradients(ids, layers, first, count, forward, backward, before):
    quarter = forward[4].shape[-1]
    piece, width = 2 * quarter, forward[0].shape[-1] - quarter
    out = jax.ShapeDtypeStruct((layers, piece, width), BF16)
    out_spec = pl.BlockSpec((1, piece, width), lambda l: (first + l, 0, 0))

    def block(array, start):
        if array.ndim == 3:
            return pl.BlockSpec((1,) + array.shape[1:], lambda l: (start + l, 0, 0))
        return pl.BlockSpec((array.shape[0], 1) + array.shape[2:], lambda l: (0, start + l, 0, 0))

    specs = [SMEM] + [block(a, first) for a in forward] + [block(a, 0) for a in backward]
    operands = [ids] + list(forward) + list(backward)
    aliases = {}
    if before is not None:
        aliases = {len(operands): 0, len(operands) + 1: 1}
        operands, specs = operands + list(before), specs + [ANY, ANY]
    return pl.pallas_call(
        functools.partial(gradient_kernel, len(backward) == 4),
        out_shape=(out, out),
        grid=(count,),
        in_specs=specs,
        out_specs=(out_spec, out_spec),
        input_output_aliases=aliases,
        compiler_params=pltpu.CompilerParams(vmem_limit_bytes=VMEM_BYTES),
        cost_estimate=pl.CostEstimate(
            flops=count * 4 * piece * width * 256, bytes_accessed=count * 2400000, transcendentals=0
        ),
    )(*operands)


def per_device(section_map, checkpoint, top_grad, value_weight, out_weight):
    tp_total = lax.axis_size("tp")
    section_total = lax.axis_size("section")
    replica_total = lax.axis_size("rep")
    chips = section_total // 2
    rep, section, tp = (lax.axis_index(name) for name in ("rep", "section", "tp"))
    chip, core, side = section // 2, section % 2, tp % 2
    layers = section_map.shape[1]
    _, _, micro, tokens, model = checkpoint.shape
    slots, width = value_weight.shape[1], value_weight.shape[3]
    rows = micro * tokens
    cut = model // tp_total
    piece = model // (replica_total * section_total)
    v_own, o_own = value_weight[0], out_weight[0]
    x_pair, top_pair = checkpoint[0, 0], top_grad[0]

    ids = jnp.stack([rep, chip, core, side, tp]).astype(jnp.int32)

    chip_of = section_map // 2
    moves = chip_of[:, 1:] - chip_of[:, :-1]
    most_moves = jnp.max(moves, axis=0)

    swap = [(i, i ^ 1) for i in range(section_total)]

    def to_sibling(array):
        return lax.ppermute(array, "section", swap)

    def to_replica(array):
        return lax.ppermute(array, "rep", [(0, 1), (1, 0)])

    o_sib, v_sib = to_sibling(o_own), to_sibling(v_own)

    def shape(*dims, dtype=BF16):
        return jax.ShapeDtypeStruct(dims, dtype)

    def in_hbm(*dims):
        return pltpu.HBM(dims, BF16)

    def dma(*dims):
        return pltpu.SemaphoreType.DMA(dims)

    weight_bytes = model * width * 2
    weight_buffer = pltpu.VMEM((model, width), BF16)

    def reduce_slices(got, base, spread, *deps):
        count = got.shape[1]
        buffer = pltpu.VMEM((count, cut), BF16)
        return run(
            functools.partial(reduce_kernel, spread, len(deps)),
            (ids, got, base, *deps),
            [SMEM] + [ANY] * (2 + len(deps)),
            in_hbm(*got.shape) if spread else in_hbm(count, cut),
            HBM,
            [pltpu.VMEM(got.shape, BF16), buffer, buffer, dma(5), dma(tp_total if spread else 1)],
            got.size * 2,
        )

    def over_tp(parts):
        return lax.all_to_all(parts, "tp", 0, 0, tiled=True)

    def recompute_slot(slot, x, with_parts, deps=()):
        halves = (shape(tokens, width),) * 2 + (shape(tokens, width, dtype=F32),) * 2
        halves += (shape(chips, tokens, cut),) * 2
        outs = ((in_hbm(tp_total, rows, cut),) if with_parts else ()) + halves
        out_specs = ((HBM,) if with_parts else ()) + (VMEM,) * 6
        scratch = [pltpu.VMEM((tp_total, rows, cut), BF16), weight_buffer]
        scratch += [pltpu.VMEM((rows, width), BF16), pltpu.VMEM((rows, width), F32), dma(tp_total + 4), dma(2)]
        if with_parts:
            scratch += [weight_buffer, pltpu.VMEM((tp_total, rows, cut), BF16)]
        operands = (ids, x, v_own) + ((o_own,) if with_parts else ()) + tuple(deps)
        count = 2 if with_parts else 1
        return run(
            functools.partial(recompute, chips, with_parts, slot, len(deps)),
            operands,
            [SMEM] + [ANY] * (len(operands) - 1),
            outs,
            out_specs,
            scratch,
            count * weight_bytes,
            count * 2 * rows * model * width,
        )

    def along_chips(cuts):
        got = [cuts[0]]
        for far in range(1, chips):
            back = chips - far
            route = [(i, (i + 2 * back) % section_total) for i in range(section_total)]
            got.append(lax.ppermute(cuts[back], "section", route))
        return got

    def carve(act_mine, act_sib, x_mine, x_sib):
        block = in_hbm(2, tokens, width + cut)
        return run(
            functools.partial(carve_kernel, chips),
            (ids, act_mine, act_sib, x_mine, x_sib),
            [SMEM] + [VMEM] * 4,
            (block,) * chips,
            (HBM,) * chips,
            [dma(2, chips, 2)],
            2 * chips * tokens * (width + cut) * 4,
        )

    def to_owners(sources, wanted, of_slots, deps=(), later=None):
        count = len(wanted)
        columns = sources[0].shape[-1]
        span = (columns - width) // 4
        alone, both = in_hbm(count, tokens, width + span), in_hbm(count, tokens, width + 2 * span)
        own_out, sib_out, rep_out = run(
            functools.partial(pick_kernel, wanted, of_slots, len(deps)),
            (ids, section_map, *sources, *deps),
            [SMEM, SMEM] + [ANY] * (len(sources) + len(deps)),
            (alone, alone, both),
            (HBM,) * 3,
            [pltpu.VMEM((count, tokens, columns), BF16), dma(count), dma(7 * count)],
            count * tokens * columns * 6,
        )
        from_rep = to_replica(rep_out)
        if later is not None:
            from_rep, later = lax.optimization_barrier((from_rep, later))
        parts = (own_out, to_sibling(sib_out), from_rep, to_sibling(from_rep))
        if span == piece:
            return parts, later
        mine = run(
            functools.partial(halves_kernel, (width, width, width, width + span)),
            parts,
            [ANY] * 4,
            shape(4, count, tokens, span),
            VMEM,
            [dma(4)],
            16 * count * tokens * span,
        )
        theirs = lax.ppermute(mine, "tp", [(i, i ^ 1) for i in range(tp_total)])
        return parts + (mine, theirs)

    x_rows = x_pair.reshape(rows, model)
    parts, act_mine_0, act_other_0, slope_mine_0, slope_other_0, x_mine_0, x_other_0 = recompute_slot(0, x_rows, True)
    act_sib_0, slope_sib_0, x_sib_0 = to_sibling(act_other_0), to_sibling(slope_other_0), to_sibling(x_other_0)
    first_cuts = carve(act_mine_0, act_sib_0, x_mine_0, x_sib_0)
    first_got = along_chips(first_cuts)
    x_second = over_tp(reduce_slices(over_tp(parts), x_rows, True))
    act_mine_1, act_other_1, slope_mine_1, slope_other_1, x_mine_1, x_other_1 = recompute_slot(
        1, x_second, False, first_cuts
    )
    slope_sib_1, act_sib_1, x_sib_1 = to_sibling(slope_other_1), to_sibling(act_other_1), to_sibling(x_other_1)
    second_cuts = carve(act_mine_1, act_sib_1, x_mine_1, x_sib_1)
    second_got = along_chips(second_cuts)
    slopes = (slope_mine_0, slope_mine_1, slope_sib_0, slope_sib_1)

    down = [(i, i - 2) for i in range(2, section_total)]
    earlier, latest = [2, 3, 4, 5, 6, 7], [0, 1]

    def one_layer(layer, g, deps):
        last = layer == 0
        operands = (ids, section_map, g, *slopes, o_own, o_sib)
        operands += (() if last else (v_own, v_sib)) + tuple(deps)
        columns = width + (2 * cut if layer in latest else cut)
        block = in_hbm(tokens, columns)
        outs = (() if last else (in_hbm(tp_total, tokens, cut),)) + (block,) * chips
        scratch = [pltpu.VMEM((tp_total, tokens, cut), BF16), pltpu.VMEM((tokens, width), F32), weight_buffer]
        scratch += [pltpu.VMEM((chips, tokens, columns), BF16), dma(tp_total + 5), dma(chips + 2)]
        if not last:
            scratch += [weight_buffer, pltpu.VMEM((tp_total, tokens, cut), BF16)]
        count = 1 if last else 2
        result = run(
            functools.partial(step, chips, layer, len(deps)),
            operands,
            [SMEM, SMEM] + [ANY] * (len(operands) - 2),
            outs,
            (HBM,) * len(outs),
            scratch,
            count * weight_bytes,
            count * 2 * tokens * model * width,
        )
        return (None if last else result[0]), along_chips(result[-chips:])

    g = top_pair
    got_at = [None] * layers
    deps = {layer: [] for layer in range(layers)}

    def collect(wanted, deps=(), later=None):
        return to_owners([array for layer in wanted for array in got_at[layer]], wanted, False, deps, later)

    for layer in reversed(range(layers)):
        if layer == 7:
            deps[7] += first_got
        if layer == 6:
            deps[6] += list(second_cuts) + got_at[7][2:3]
        if layer == 5:
            deps[5] += second_got[1::2]
        if layer == 4:
            deps[4] += second_got[2:3] + got_at[6][2:3]
        if layer == 3:
            deps[3] += list(forward[:1])
        if layer == 2:
            deps[2] += got_at[3][2:3]
        if layer == 1:
            deps[1] += list(forward[:4])
        if layer == 0:
            deps[0] += got_at[1][2:3] + list(earlier_all[:4])
        parts, got_at[layer] = one_layer(layer, g, deps[layer])
        if layer == 0:
            break
        got = over_tp(parts)
        most = most_moves[layer - 1]

        def stay(*operands):
            return reduce_slices(*operands[:2], True, *operands[2:])

        def settle(kept, came, layer=layer):
            return run(
                functools.partial(settle_kernel, layer),
                (ids, section_map, kept, came),
                [SMEM, SMEM, ANY, ANY],
                in_hbm(tp_total, tokens, cut),
                HBM,
                [pltpu.VMEM((tokens, cut), BF16), dma(1), dma(tp_total)],
                tp_total * tokens * cut * 2,
            )

        def go_one(*operands):
            mine = reduce_slices(*operands[:2], False, *operands[2:])
            return settle(mine, lax.ppermute(mine, "section", down))

        def go_far(*operands, layer=layer, most=most):
            mine = reduce_slices(*operands[:2], False, *operands[2:])
            my_move = lax.dynamic_index_in_dim(moves, rep, 0, keepdims=False)[layer - 1]

            def hop(i, value):
                came = lax.ppermute(value, "section", down)
                return jnp.where(i < my_move, came, value)

            mine = lax.fori_loop(0, most, hop, mine)
            return settle(mine, mine)

        near = got_at[layer][1:] if layer in (5, 4, 2) else got_at[layer][1::2]
        spread = lax.switch(jnp.minimum(most, 2), (stay, go_one, go_far), got, g, *near)
        g = over_tp(spread)
        if layer == 4:
            forward = to_owners(first_got + second_got, list(range(layers)), True, (spread,))
        if layer == 2:
            earlier_all = collect(earlier, (spread,))

    result = gradients(ids, layers, earlier[0], len(earlier), forward, earlier_all, None)
    latest_all, result = collect(latest, (), result)
    return gradients(ids, layers, latest[0], len(latest), forward, latest_all, result)


def solution(mesh):
    placed = (
        P(),
        P("rep", "section", None, None, None),
        P("rep", None, None, None),
        P("rep", "section", None, "tp"),
        P("rep", "section", None, "tp"),
    )
    return jax.shard_map(
        per_device,
        mesh=mesh,
        in_specs=placed,
        out_specs=(P(None, ("rep", "section"), "tp"), P(None, ("rep", "section"), "tp")),
        check_vma=False,
    )
```

```python
import functools

import jax
import jax.numpy as jnp
from jax import lax
from jax.experimental import pallas as pl
from jax.experimental.pallas import tpu as pltpu
from jax.sharding import PartitionSpec as P

BF16 = jnp.bfloat16
F32 = jnp.float32
VMEM_BYTES = 64 * 1024 * 1024
NT = (((1,), (1,)), ((), ()))
TN = (((0,), (0,)), ((), ()))
ANY = pl.BlockSpec(memory_space=pl.ANY)
HBM = pl.BlockSpec(memory_space=pltpu.HBM)
SMEM = pl.BlockSpec(memory_space=pltpu.SMEM)
VMEM = pl.BlockSpec(memory_space=pltpu.VMEM)


REP, CHIP, CORE, SIDE, TP = range(5)


def held_at(ids, section_map, layer):
    section = section_map[ids[REP], layer]
    slot = jnp.int32(0)
    if layer > 0:
        slot = (section_map[ids[REP], layer - 1] == section).astype(jnp.int32)
    chips = 4
    return lax.rem(section, 2), slot, lax.rem(section // 2 - ids[CHIP] + chips, chips)


def silu_slope(preact):
    sigma = jax.nn.sigmoid(preact)
    return sigma * (1.0 + preact * (1.0 - sigma))


def run(kernel, operands, specs, outs, out_specs, scratch, bytes_moved, flops=0):
    return pl.pallas_call(
        kernel,
        out_shape=outs,
        in_specs=specs,
        out_specs=out_specs,
        scratch_shapes=scratch,
        compiler_params=pltpu.CompilerParams(vmem_limit_bytes=VMEM_BYTES),
        cost_estimate=pl.CostEstimate(flops=flops, bytes_accessed=bytes_moved, transcendentals=0),
    )(*operands)


def rows_place(ref, cut, core):
    if len(ref.shape) == 3 and ref.shape[-1] == cut:
        return lambda i: ref.at[i]
    columns = lambda i: pl.ds(pl.multiple_of(i * cut, cut), cut)
    if len(ref.shape) == 2:
        return lambda i: ref.at[:, columns(i)]
    return lambda i: ref.at[core, :, columns(i)]


class Copies:
    def __init__(self, sems):
        self.sems, self.all = sems, []

    def start(self, source, target, condition=None):
        copy = pltpu.make_async_copy(source, target, self.sems.at[len(self.all)])
        if condition is None:
            copy.start()
        else:
            pl.when(condition)(copy.start)
        self.all.append(copy)
        return copy

    def either(self, condition, first, second, target):
        sem = self.sems.at[len(self.all)]
        pl.when(condition)(lambda: pltpu.make_async_copy(first, target, sem).start())
        pl.when(jnp.logical_not(condition))(lambda: pltpu.make_async_copy(second, target, sem).start())
        self.all.append(pltpu.make_async_copy(first, target, sem))
        return self.all[-1]

    def wait(self):
        for copy in self.all:
            copy.wait()


def halves(ref):
    step = ref.shape[0] // 2
    return [pl.ds(i * step, step) for i in range(2)]


def product_in(rows, weight, waits):
    cuts, cut = rows.shape[0], rows.shape[-1]
    total = None
    for i in range(cuts):
        if i % (cuts // len(waits)) == 0:
            waits[i // (cuts // len(waits))].wait()
        part = jnp.dot(rows[i], weight[i * cut : (i + 1) * cut, :], preferred_element_type=F32)
        total = part if total is None else total + part
    return total


def product_out(rows, weight, waits, stage, part_ref, out):
    cuts, cut = stage.shape[0], stage.shape[-1]
    group = cuts // len(waits)
    for i in range(cuts):
        if i % group == 0:
            waits[i // group].wait()
        part = lax.dot_general(rows, weight[i * cut : (i + 1) * cut, :], NT, preferred_element_type=F32)
        stage[i] = part.astype(BF16)
        if i % group == group - 1:
            cuts_done = pl.ds(i - group + 1, group)
            out.start(stage.at[cuts_done], part_ref.at[cuts_done])


def recompute(chips, with_parts, slot, deps, ids, x_ref, v_ref, *refs):
    o_ref, refs = (refs[0], refs[1:]) if with_parts else (None, refs)
    refs = refs[deps:]
    part_ref, refs = (refs[0], refs[1:]) if with_parts else (None, refs)
    outs, (xbuf, vbuf, act_rows, slope_rows, in_sems, out_sems) = refs[:6], refs[6:12]
    cuts, cut = xbuf.shape[0], xbuf.shape[-1]
    core, side = ids[CORE], ids[SIDE]
    arriving, leaving = Copies(in_sems), Copies(out_sems)
    x = [arriving.start(rows_place(x_ref, cut, core)(i), xbuf.at[i]) for i in range(cuts)]
    v = [arriving.start(v_ref.at[slot, rows], vbuf.at[rows]) for rows in halves(vbuf)]
    if with_parts:
        obuf, stage = refs[12:]
        o = [arriving.start(o_ref.at[slot, rows], obuf.at[rows]) for rows in halves(obuf)]
    for copy in x:
        copy.wait()
    pre = product_in(xbuf, vbuf, v)
    act = jax.nn.silu(pre).astype(BF16)
    if with_parts:
        product_out(act, obuf, o, stage, part_ref, leaving)
    act_rows[...] = act
    slope_rows[...] = silu_slope(pre)
    half = outs[0].shape[0]
    quarter = cut // 4
    for k, which in enumerate((core, 1 - core)):
        rows = pl.ds(pl.multiple_of(which * half, half), half)
        act_out, slope_out, x_out = outs[k], outs[2 + k], outs[4 + k]
        act_out[...] = act_rows[rows, :]
        slope_out[...] = slope_rows[rows, :]
        for to in range(chips):
            for j in range(4):
                columns = pl.ds(pl.multiple_of((j % 2) * 2 * quarter + side * quarter, quarter), quarter)
                x_out[to, :, j * quarter : (j + 1) * quarter] = xbuf[(j // 2) * chips + to, rows, columns]
    leaving.wait()


def step(chips, layer, deps, ids, section_map, g_ref, *refs):
    with_parts = layer > 0
    slopes, refs = refs[:4], refs[4:]
    o_refs, refs = refs[:2], refs[2:]
    v_refs, refs = (refs[:2], refs[2:]) if with_parts else (None, refs)
    refs = refs[deps:]
    part_ref, refs = (refs[0], refs[1:]) if with_parts else (None, refs)
    outs, (gbuf, sbuf, obuf, pay, in_sems, out_sems) = refs[:chips], refs[chips : chips + 6]
    cut, width = gbuf.shape[-1], sbuf.shape[-1]
    span = (pay.shape[-1] - width) // 4
    chip, core, side = ids[CHIP], ids[CORE], ids[SIDE]
    section_core, slot, _ = held_at(ids, section_map, layer)
    own = section_core == core
    arriving, leaving = Copies(in_sems), Copies(out_sems)
    if g_ref.shape == gbuf.shape:
        g = [arriving.start(g_ref, gbuf)]
    else:
        g = [arriving.start(rows_place(g_ref, cut, core)(i), gbuf.at[i]) for i in range(gbuf.shape[0])]
    o = [arriving.either(own, o_refs[0].at[slot, r], o_refs[1].at[slot, r], obuf.at[r]) for r in halves(obuf)]
    which = jnp.where(own, 0, 2) + slot
    for j in range(4):
        pl.when(which == j)(pltpu.make_async_copy(slopes[j], sbuf, in_sems.at[-1 + in_sems.shape[0]]).start)
    slope = pltpu.make_async_copy(slopes[0], sbuf, in_sems.at[-1 + in_sems.shape[0]])
    if with_parts:
        vbuf, stage = refs[chips + 6 :]
        v = [arriving.either(own, v_refs[0].at[slot, r], v_refs[1].at[slot, r], vbuf.at[r]) for r in halves(vbuf)]
    for copy in g:
        copy.wait()
    for far in range(chips):
        to = lax.rem(chip + far, chips)
        for j in range(4):
            start = (j % 2) * (cut // 2) + (0 if span == cut // 2 else side * span)
            columns = pl.ds(start if span == cut // 2 else pl.multiple_of(start, span), span)
            pay[far, :, width + j * span : width + (j + 1) * span] = gbuf[(j // 2) * chips + to, :, columns]
    total = product_in(gbuf, obuf, o)
    slope.wait()
    head = (total * sbuf[...]).astype(BF16)
    for far, out in enumerate(outs):
        pay[far, :, :width] = head
        leaving.start(pay.at[far], out)
    if with_parts:
        product_out(head, vbuf, v, stage, part_ref, leaving)
    leaving.wait()


def reduce_kernel(spread, deps, ids, got_ref, base_ref, *refs):
    out_ref, got, base, stage, sems, out_sems = refs[deps:]
    cuts, cut = got.shape[0], got.shape[-1]
    arriving, leaving = Copies(sems), Copies(out_sems)
    arriving.start(rows_place(base_ref, cut, ids[CORE])(ids[TP]), base)
    for i in range(4):
        some = pl.ds(i * (cuts // 4), cuts // 4)
        arriving.start(got_ref.at[some], got.at[some])
    arriving.wait()
    total = got[0].astype(F32)
    for i in range(1, cuts):
        total += got[i].astype(F32)
    stage[...] = (base[...].astype(F32) + total).astype(BF16)
    for i in range(cuts if spread else 1):
        leaving.start(stage, out_ref.at[i] if spread else out_ref)
    leaving.wait()


def settle_kernel(layer, ids, section_map, kept_ref, came_ref, out_ref, stage, sems, out_sems):
    rep = ids[REP]
    moved = section_map[rep, layer] // 2 > section_map[rep, layer - 1] // 2
    arriving, leaving = Copies(sems), Copies(out_sems)
    arriving.either(moved, came_ref, kept_ref, stage)
    arriving.wait()
    for i in range(out_ref.shape[0]):
        leaving.start(stage, out_ref.at[i])
    leaving.wait()


def carve_kernel(chips, ids, act_mine, act_sib, x_mine, x_sib, *refs):
    outs, sems = refs[:chips], refs[chips]
    chip, core = ids[CHIP], ids[CORE]
    width = act_mine.shape[-1]
    copies = []
    for k, (act, x) in enumerate(((act_mine, x_mine), (act_sib, x_sib))):
        at = core if k == 0 else 1 - core
        for far, out in enumerate(outs):
            to = lax.rem(chip + far, chips)
            for j, source in enumerate((act, x.at[to])):
                target = out.at[at, :, pl.ds(j * width, width)]
                copies.append(pltpu.make_async_copy(source, target, sems.at[k, far, j]))
                copies[-1].start()
    for copy in copies:
        copy.wait()


def pick_kernel(wanted, of_slots, deps, ids, section_map, *refs):
    chips = 4
    count = len(wanted)
    total = (2 if of_slots else count) * chips
    sources, (own_out, sib_out, rep_out, block, in_sems, sems) = refs[:total], refs[total + deps :]
    core, rep = ids[CORE], ids[REP]
    width = 2 * sib_out.shape[-1] - rep_out.shape[-1]
    span = rep_out.shape[-1] - sib_out.shape[-1]
    for n, layer in enumerate(wanted):
        section_core, slot, far = held_at(ids, section_map, layer)
        at = slot * chips + far if of_slots else n * chips + far
        for j in range(total) if of_slots else range(n * chips, (n + 1) * chips):

            def begin(n=n, j=j, section_core=section_core):
                source = sources[j].at[section_core] if of_slots else sources[j]
                pltpu.make_async_copy(source, block.at[n], in_sems.at[n]).start()

            pl.when(at == j)(begin)
    plan = ((own_out, [(rep, core)]), (sib_out, [(rep, 1 - core)]), (rep_out, [(1 - rep, core), (1 - rep, 1 - core)]))
    leaving = Copies(sems)
    for n in range(count):
        pltpu.make_async_copy(block.at[n], block.at[n], in_sems.at[n]).wait()
        for out, pieces in plan:
            leaving.start(block.at[n, :, pl.ds(0, width)], out.at[n, :, pl.ds(0, width)])
            for j, (replica, side) in enumerate(pieces):
                columns = pl.ds(pl.multiple_of(width + (replica * 2 + side) * span, span), span)
                leaving.start(block.at[n, :, columns], out.at[n, :, pl.ds(width + j * span, span)])
    leaving.wait()


def halves_kernel(starts, *refs):
    parts, (out_ref, sems) = refs[:4], refs[4:]
    arriving = Copies(sems)
    for k in range(4):
        arriving.start(parts[k].at[:, :, pl.ds(starts[k], out_ref.shape[-1])], out_ref.at[k])
    arriving.wait()


def gradient_kernel(whole, ids, *refs):
    value_ref, out_ref = refs[-2:]
    width = value_ref.shape[-1]
    first_side = ids[SIDE] == 0

    def factors(parts, mine=None, theirs=None):
        wide = jnp.concatenate([part[0][:, :width] for part in parts], axis=0)
        if mine is None:
            span = parts[0].shape[-1] - width
            starts = (width, width, width, width + span)
            return jnp.concatenate([p[0][:, i : i + span] for p, i in zip(parts, starts)], axis=0), wide
        mine, theirs = (jnp.concatenate([ref[k, 0] for k in range(4)], axis=0) for ref in (mine, theirs))
        left = jnp.where(first_side, mine, theirs)
        right = jnp.where(first_side, theirs, mine)
        return jnp.concatenate([left, right], axis=1), wide

    x, act = factors(refs[0:4], refs[4], refs[5])
    g, head = factors(refs[6:10]) if whole else factors(refs[6:10], refs[10], refs[11])
    value_ref[0] = lax.dot_general(x, head, TN, preferred_element_type=F32).astype(BF16)
    out_ref[0] = lax.dot_general(g, act, TN, preferred_element_type=F32).astype(BF16)


def gradients(ids, layers, first, count, forward, backward, before, after=None):
    quarter = forward[4].shape[-1]
    piece, width = 2 * quarter, forward[0].shape[-1] - quarter
    out = jax.ShapeDtypeStruct((layers, piece, width), BF16)
    out_spec = pl.BlockSpec((1, piece, width), lambda l: (first + l, 0, 0))

    def block(array, start):
        if array.ndim == 3:
            return pl.BlockSpec((1,) + array.shape[1:], lambda l: (start + l, 0, 0))
        return pl.BlockSpec((array.shape[0], 1) + array.shape[2:], lambda l: (0, start + l, 0, 0))

    specs = [SMEM] + [block(a, first) for a in forward] + [block(a, 0) for a in backward]
    operands = [ids] + list(forward) + list(backward)
    aliases = {}
    if before is not None:
        aliases = {len(operands): 0, len(operands) + 1: 1}
        operands, specs = operands + list(before), specs + [ANY, ANY]
    if after is not None:
        operands, specs = operands + [after], specs + [ANY]
    return pl.pallas_call(
        functools.partial(gradient_kernel, len(backward) == 4),
        out_shape=(out, out),
        grid=(count,),
        in_specs=specs,
        out_specs=(out_spec, out_spec),
        input_output_aliases=aliases,
        compiler_params=pltpu.CompilerParams(vmem_limit_bytes=VMEM_BYTES),
        cost_estimate=pl.CostEstimate(
            flops=count * 4 * piece * width * 256, bytes_accessed=count * 2400000, transcendentals=0
        ),
    )(*operands)


def per_device(section_map, checkpoint, top_grad, value_weight, out_weight):
    tp_total = lax.axis_size("tp")
    section_total = lax.axis_size("section")
    replica_total = lax.axis_size("rep")
    chips = section_total // 2
    rep, section, tp = (lax.axis_index(name) for name in ("rep", "section", "tp"))
    chip, core, side = section // 2, section % 2, tp % 2
    layers = section_map.shape[1]
    _, _, micro, tokens, model = checkpoint.shape
    slots, width = value_weight.shape[1], value_weight.shape[3]
    rows = micro * tokens
    cut = model // tp_total
    piece = model // (replica_total * section_total)
    v_own, o_own = value_weight[0], out_weight[0]
    x_pair, top_pair = checkpoint[0, 0], top_grad[0]

    ids = jnp.stack([rep, chip, core, side, tp]).astype(jnp.int32)

    chip_of = section_map // 2
    moves = chip_of[:, 1:] - chip_of[:, :-1]
    most_moves = jnp.max(moves, axis=0)

    swap = [(i, i ^ 1) for i in range(section_total)]

    def to_sibling(array):
        return lax.ppermute(array, "section", swap)

    def to_replica(array):
        return lax.ppermute(array, "rep", [(0, 1), (1, 0)])

    o_sib, v_sib = to_sibling(o_own), to_sibling(v_own)

    def shape(*dims, dtype=BF16):
        return jax.ShapeDtypeStruct(dims, dtype)

    def in_hbm(*dims):
        return pltpu.HBM(dims, BF16)

    def dma(*dims):
        return pltpu.SemaphoreType.DMA(dims)

    weight_bytes = model * width * 2
    weight_buffer = pltpu.VMEM((model, width), BF16)

    def reduce_slices(got, base, spread, *deps):
        count = got.shape[1]
        buffer = pltpu.VMEM((count, cut), BF16)
        return run(
            functools.partial(reduce_kernel, spread, len(deps)),
            (ids, got, base, *deps),
            [SMEM] + [ANY] * (2 + len(deps)),
            in_hbm(*got.shape) if spread else in_hbm(count, cut),
            HBM,
            [pltpu.VMEM(got.shape, BF16), buffer, buffer, dma(5), dma(tp_total if spread else 1)],
            got.size * 2,
        )

    def over_tp(parts):
        return lax.all_to_all(parts, "tp", 0, 0, tiled=True)

    def recompute_slot(slot, x, with_parts, deps=()):
        halves = (shape(tokens, width),) * 2 + (shape(tokens, width, dtype=F32),) * 2
        halves += (shape(chips, tokens, cut),) * 2
        outs = ((in_hbm(tp_total, rows, cut),) if with_parts else ()) + halves
        out_specs = ((HBM,) if with_parts else ()) + (VMEM,) * 6
        scratch = [pltpu.VMEM((tp_total, rows, cut), BF16), weight_buffer]
        scratch += [pltpu.VMEM((rows, width), BF16), pltpu.VMEM((rows, width), F32), dma(tp_total + 4), dma(2)]
        if with_parts:
            scratch += [weight_buffer, pltpu.VMEM((tp_total, rows, cut), BF16)]
        operands = (ids, x, v_own) + ((o_own,) if with_parts else ()) + tuple(deps)
        count = 2 if with_parts else 1
        return run(
            functools.partial(recompute, chips, with_parts, slot, len(deps)),
            operands,
            [SMEM] + [ANY] * (len(operands) - 1),
            outs,
            out_specs,
            scratch,
            count * weight_bytes,
            count * 2 * rows * model * width,
        )

    def along_chips(cuts):
        got = [cuts[0]]
        for far in range(1, chips):
            back = chips - far
            route = [(i, (i + 2 * back) % section_total) for i in range(section_total)]
            got.append(lax.ppermute(cuts[back], "section", route))
        return got

    def carve(act_mine, act_sib, x_mine, x_sib):
        block = in_hbm(2, tokens, width + cut)
        return run(
            functools.partial(carve_kernel, chips),
            (ids, act_mine, act_sib, x_mine, x_sib),
            [SMEM] + [VMEM] * 4,
            (block,) * chips,
            (HBM,) * chips,
            [dma(2, chips, 2)],
            2 * chips * tokens * (width + cut) * 4,
        )

    def to_owners(sources, wanted, of_slots, deps=(), later=None):
        count = len(wanted)
        columns = sources[0].shape[-1]
        span = (columns - width) // 4
        alone, both = in_hbm(count, tokens, width + span), in_hbm(count, tokens, width + 2 * span)
        own_out, sib_out, rep_out = run(
            functools.partial(pick_kernel, wanted, of_slots, len(deps)),
            (ids, section_map, *sources, *deps),
            [SMEM, SMEM] + [ANY] * (len(sources) + len(deps)),
            (alone, alone, both),
            (HBM,) * 3,
            [pltpu.VMEM((count, tokens, columns), BF16), dma(count), dma(7 * count)],
            count * tokens * columns * 6,
        )
        from_rep, from_sib = to_replica(rep_out), to_sibling(sib_out)
        if later is not None:
            from_rep, later = lax.optimization_barrier((from_rep, later(from_sib)))
        parts = (own_out, from_sib, from_rep, to_sibling(from_rep))
        if span == piece:
            return parts, later
        mine = run(
            functools.partial(halves_kernel, (width, width, width, width + span)),
            parts,
            [ANY] * 4,
            shape(4, count, tokens, span),
            VMEM,
            [dma(4)],
            16 * count * tokens * span,
        )
        theirs = lax.ppermute(mine, "tp", [(i, i ^ 1) for i in range(tp_total)])
        return parts + (mine, theirs)

    x_rows = x_pair.reshape(rows, model)
    parts, act_mine_0, act_other_0, slope_mine_0, slope_other_0, x_mine_0, x_other_0 = recompute_slot(0, x_rows, True)
    act_sib_0, slope_sib_0, x_sib_0 = to_sibling(act_other_0), to_sibling(slope_other_0), to_sibling(x_other_0)
    first_cuts = carve(act_mine_0, act_sib_0, x_mine_0, x_sib_0)
    first_got = along_chips(first_cuts)
    x_second = over_tp(reduce_slices(over_tp(parts), x_rows, True))
    act_mine_1, act_other_1, slope_mine_1, slope_other_1, x_mine_1, x_other_1 = recompute_slot(
        1, x_second, False, first_cuts
    )
    slope_sib_1, act_sib_1, x_sib_1 = to_sibling(slope_other_1), to_sibling(act_other_1), to_sibling(x_other_1)
    second_cuts = carve(act_mine_1, act_sib_1, x_mine_1, x_sib_1)
    second_got = along_chips(second_cuts)
    slopes = (slope_mine_0, slope_mine_1, slope_sib_0, slope_sib_1)

    down = [(i, i - 2) for i in range(2, section_total)]
    earlier, latest = [2, 3, 4, 5, 6, 7], [0, 1]

    def one_layer(layer, g, deps):
        last = layer == 0
        operands = (ids, section_map, g, *slopes, o_own, o_sib)
        operands += (() if last else (v_own, v_sib)) + tuple(deps)
        columns = width + (2 * cut if layer in latest else cut)
        block = in_hbm(tokens, columns)
        outs = (() if last else (in_hbm(tp_total, tokens, cut),)) + (block,) * chips
        scratch = [pltpu.VMEM((tp_total, tokens, cut), BF16), pltpu.VMEM((tokens, width), F32), weight_buffer]
        scratch += [pltpu.VMEM((chips, tokens, columns), BF16), dma(tp_total + 5), dma(chips + 2)]
        if not last:
            scratch += [weight_buffer, pltpu.VMEM((tp_total, tokens, cut), BF16)]
        count = 1 if last else 2
        result = run(
            functools.partial(step, chips, layer, len(deps)),
            operands,
            [SMEM, SMEM] + [ANY] * (len(operands) - 2),
            outs,
            (HBM,) * len(outs),
            scratch,
            count * weight_bytes,
            count * 2 * tokens * model * width,
        )
        return (None if last else result[0]), along_chips(result[-chips:])

    g = top_pair
    got_at = [None] * layers
    deps = {layer: [] for layer in range(layers)}

    def collect(wanted, deps=(), later=None):
        return to_owners([array for layer in wanted for array in got_at[layer]], wanted, False, deps, later)

    for layer in reversed(range(layers)):
        if layer == 7:
            deps[7] += first_got
        if layer == 6:
            deps[6] += list(second_cuts) + got_at[7][2:3]
        if layer == 5:
            deps[5] += second_got[1::2]
        if layer == 4:
            deps[4] += second_got[2:3] + got_at[6][2:3]
        if layer == 3:
            deps[3] += list(forward[:1])
        if layer == 2:
            deps[2] += got_at[3][2:3]
        if layer == 1:
            deps[1] += list(forward[:4])
        if layer == 0:
            deps[0] += got_at[1][2:3] + list(earlier_all[:4])
        parts, got_at[layer] = one_layer(layer, g, deps[layer])
        if layer == 0:
            break
        got = over_tp(parts)
        most = most_moves[layer - 1]

        def stay(*operands):
            return reduce_slices(*operands[:2], True, *operands[2:])

        def settle(kept, came, layer=layer):
            return run(
                functools.partial(settle_kernel, layer),
                (ids, section_map, kept, came),
                [SMEM, SMEM, ANY, ANY],
                in_hbm(tp_total, tokens, cut),
                HBM,
                [pltpu.VMEM((tokens, cut), BF16), dma(1), dma(tp_total)],
                tp_total * tokens * cut * 2,
            )

        def go_one(*operands):
            mine = reduce_slices(*operands[:2], False, *operands[2:])
            return settle(mine, lax.ppermute(mine, "section", down))

        def go_far(*operands, layer=layer, most=most):
            mine = reduce_slices(*operands[:2], False, *operands[2:])
            my_move = lax.dynamic_index_in_dim(moves, rep, 0, keepdims=False)[layer - 1]

            def hop(i, value):
                came = lax.ppermute(value, "section", down)
                return jnp.where(i < my_move, came, value)

            mine = lax.fori_loop(0, most, hop, mine)
            return settle(mine, mine)

        near = got_at[layer][1:] if layer in (5, 4, 2) else got_at[layer][1::2]
        spread = lax.switch(jnp.minimum(most, 2), (stay, go_one, go_far), got, g, *near)
        g = over_tp(spread)
        if layer == 4:
            forward = to_owners(first_got + second_got, list(range(layers)), True, (spread,))
        if layer == 2:
            earlier_all = collect(earlier, (spread,))

    def earlier_gradients(after):
        return gradients(ids, layers, earlier[0], len(earlier), forward, earlier_all, None, after)

    latest_all, result = collect(latest, (), earlier_gradients)
    return gradients(ids, layers, latest[0], len(latest), forward, latest_all, result)


def solution(mesh):
    placed = (
        P(),
        P("rep", "section", None, None, None),
        P("rep", None, None, None),
        P("rep", "section", None, "tp"),
        P("rep", "section", None, "tp"),
    )
    return jax.shard_map(
        per_device,
        mesh=mesh,
        in_specs=placed,
        out_specs=(P(None, ("rep", "section"), "tp"), P(None, ("rep", "section"), "tp")),
        check_vma=False,
    )
```

```python
import functools

import jax
import jax.numpy as jnp
from jax import lax
from jax.experimental import pallas as pl
from jax.experimental.pallas import tpu as pltpu
from jax.sharding import PartitionSpec as P

BF16 = jnp.bfloat16
F32 = jnp.float32
VMEM_BYTES = 64 * 1024 * 1024
NT = (((1,), (1,)), ((), ()))
TN = (((0,), (0,)), ((), ()))
ANY = pl.BlockSpec(memory_space=pl.ANY)
HBM = pl.BlockSpec(memory_space=pltpu.HBM)
SMEM = pl.BlockSpec(memory_space=pltpu.SMEM)
VMEM = pl.BlockSpec(memory_space=pltpu.VMEM)


REP, CHIP, CORE, SIDE, TP = range(5)


def held_at(ids, section_map, layer):
    section = section_map[ids[REP], layer]
    slot = jnp.int32(0)
    if layer > 0:
        slot = (section_map[ids[REP], layer - 1] == section).astype(jnp.int32)
    chips = 4
    return lax.rem(section, 2), slot, lax.rem(section // 2 - ids[CHIP] + chips, chips)


def silu_slope(preact):
    sigma = jax.nn.sigmoid(preact)
    return sigma * (1.0 + preact * (1.0 - sigma))


def run(kernel, operands, specs, outs, out_specs, scratch, bytes_moved, flops=0):
    return pl.pallas_call(
        kernel,
        out_shape=outs,
        in_specs=specs,
        out_specs=out_specs,
        scratch_shapes=scratch,
        compiler_params=pltpu.CompilerParams(vmem_limit_bytes=VMEM_BYTES),
        cost_estimate=pl.CostEstimate(flops=flops, bytes_accessed=bytes_moved, transcendentals=0),
    )(*operands)


def rows_place(ref, cut, core):
    if len(ref.shape) == 3 and ref.shape[-1] == cut:
        return lambda i: ref.at[i]
    columns = lambda i: pl.ds(pl.multiple_of(i * cut, cut), cut)
    if len(ref.shape) == 2:
        return lambda i: ref.at[:, columns(i)]
    return lambda i: ref.at[core, :, columns(i)]


class Copies:
    def __init__(self, sems):
        self.sems, self.all = sems, []

    def start(self, source, target, condition=None):
        copy = pltpu.make_async_copy(source, target, self.sems.at[len(self.all)])
        if condition is None:
            copy.start()
        else:
            pl.when(condition)(copy.start)
        self.all.append(copy)
        return copy

    def either(self, condition, first, second, target):
        sem = self.sems.at[len(self.all)]
        pl.when(condition)(lambda: pltpu.make_async_copy(first, target, sem).start())
        pl.when(jnp.logical_not(condition))(lambda: pltpu.make_async_copy(second, target, sem).start())
        self.all.append(pltpu.make_async_copy(first, target, sem))
        return self.all[-1]

    def wait(self):
        for copy in self.all:
            copy.wait()


def halves(ref):
    step = ref.shape[0] // 2
    return [pl.ds(i * step, step) for i in range(2)]


def product_in(rows, weight, waits):
    cuts, cut = rows.shape[0], rows.shape[-1]
    total = None
    for i in range(cuts):
        if i % (cuts // len(waits)) == 0:
            waits[i // (cuts // len(waits))].wait()
        part = jnp.dot(rows[i], weight[i * cut : (i + 1) * cut, :], preferred_element_type=F32)
        total = part if total is None else total + part
    return total


def product_out(rows, weight, waits, stage, part_ref, out):
    cuts, cut = stage.shape[0], stage.shape[-1]
    group = cuts // len(waits)
    for i in range(cuts):
        if i % group == 0:
            waits[i // group].wait()
        part = lax.dot_general(rows, weight[i * cut : (i + 1) * cut, :], NT, preferred_element_type=F32)
        stage[i] = part.astype(BF16)
        if i % group == group - 1:
            cuts_done = pl.ds(i - group + 1, group)
            out.start(stage.at[cuts_done], part_ref.at[cuts_done])


def recompute(chips, with_parts, slot, deps, ids, x_ref, v_ref, *refs):
    o_ref, refs = (refs[0], refs[1:]) if with_parts else (None, refs)
    refs = refs[deps:]
    part_ref, refs = (refs[0], refs[1:]) if with_parts else (None, refs)
    outs, (xbuf, vbuf, act_rows, slope_rows, in_sems, out_sems) = refs[:6], refs[6:12]
    cuts, cut = xbuf.shape[0], xbuf.shape[-1]
    core, side = ids[CORE], ids[SIDE]
    arriving, leaving = Copies(in_sems), Copies(out_sems)
    x = [arriving.start(rows_place(x_ref, cut, core)(i), xbuf.at[i]) for i in range(cuts)]
    v = [arriving.start(v_ref.at[slot, rows], vbuf.at[rows]) for rows in halves(vbuf)]
    if with_parts:
        obuf, stage = refs[12:]
        o = [arriving.start(o_ref.at[slot, rows], obuf.at[rows]) for rows in halves(obuf)]
    for copy in x:
        copy.wait()
    pre = product_in(xbuf, vbuf, v)
    act = jax.nn.silu(pre).astype(BF16)
    if with_parts:
        product_out(act, obuf, o, stage, part_ref, leaving)
    act_rows[...] = act
    slope_rows[...] = silu_slope(pre)
    half = outs[0].shape[0]
    quarter = cut // 4
    for k, which in enumerate((core, 1 - core)):
        rows = pl.ds(pl.multiple_of(which * half, half), half)
        act_out, slope_out, x_out = outs[k], outs[2 + k], outs[4 + k]
        act_out[...] = act_rows[rows, :]
        slope_out[...] = slope_rows[rows, :]
        for to in range(chips):
            for j in range(4):
                columns = pl.ds(pl.multiple_of((j % 2) * 2 * quarter + side * quarter, quarter), quarter)
                x_out[to, :, j * quarter : (j + 1) * quarter] = xbuf[(j // 2) * chips + to, rows, columns]
    leaving.wait()


def step(chips, layer, deps, ids, section_map, g_ref, *refs):
    with_parts = layer > 0
    slopes, refs = refs[:4], refs[4:]
    o_refs, refs = refs[:2], refs[2:]
    v_refs, refs = (refs[:2], refs[2:]) if with_parts else (None, refs)
    refs = refs[deps:]
    part_ref, refs = (refs[0], refs[1:]) if with_parts else (None, refs)
    outs, (gbuf, sbuf, obuf, pay, in_sems, out_sems) = refs[:chips], refs[chips : chips + 6]
    cut, width = gbuf.shape[-1], sbuf.shape[-1]
    span = (pay.shape[-1] - width) // 4
    chip, core, side = ids[CHIP], ids[CORE], ids[SIDE]
    section_core, slot, _ = held_at(ids, section_map, layer)
    own = section_core == core
    arriving, leaving = Copies(in_sems), Copies(out_sems)
    if g_ref.shape == gbuf.shape:
        g = [arriving.start(g_ref, gbuf)]
    else:
        g = [arriving.start(rows_place(g_ref, cut, core)(i), gbuf.at[i]) for i in range(gbuf.shape[0])]
    o = [arriving.either(own, o_refs[0].at[slot, r], o_refs[1].at[slot, r], obuf.at[r]) for r in halves(obuf)]
    which = jnp.where(own, 0, 2) + slot
    for j in range(4):
        pl.when(which == j)(pltpu.make_async_copy(slopes[j], sbuf, in_sems.at[-1 + in_sems.shape[0]]).start)
    slope = pltpu.make_async_copy(slopes[0], sbuf, in_sems.at[-1 + in_sems.shape[0]])
    if with_parts:
        vbuf, stage = refs[chips + 6 :]
        v = [arriving.either(own, v_refs[0].at[slot, r], v_refs[1].at[slot, r], vbuf.at[r]) for r in halves(vbuf)]
    for copy in g:
        copy.wait()
    for far in range(chips):
        to = lax.rem(chip + far, chips)
        for j in range(4):
            start = (j % 2) * (cut // 2) + (0 if span == cut // 2 else side * span)
            columns = pl.ds(start if span == cut // 2 else pl.multiple_of(start, span), span)
            pay[far, :, width + j * span : width + (j + 1) * span] = gbuf[(j // 2) * chips + to, :, columns]
    total = product_in(gbuf, obuf, o)
    slope.wait()
    head = (total * sbuf[...]).astype(BF16)
    for far, out in enumerate(outs):
        pay[far, :, :width] = head
        leaving.start(pay.at[far], out)
    if with_parts:
        product_out(head, vbuf, v, stage, part_ref, leaving)
    leaving.wait()


def reduce_kernel(spread, deps, ids, got_ref, base_ref, *refs):
    out_ref, got, base, stage, sems, out_sems = refs[deps:]
    cuts, cut = got.shape[0], got.shape[-1]
    arriving, leaving = Copies(sems), Copies(out_sems)
    arriving.start(rows_place(base_ref, cut, ids[CORE])(ids[TP]), base)
    for i in range(4):
        some = pl.ds(i * (cuts // 4), cuts // 4)
        arriving.start(got_ref.at[some], got.at[some])
    arriving.wait()
    total = got[0].astype(F32)
    for i in range(1, cuts):
        total += got[i].astype(F32)
    stage[...] = (base[...].astype(F32) + total).astype(BF16)
    for i in range(cuts if spread else 1):
        leaving.start(stage, out_ref.at[i] if spread else out_ref)
    leaving.wait()


def settle_kernel(layer, ids, section_map, kept_ref, came_ref, out_ref, stage, sems, out_sems):
    rep = ids[REP]
    moved = section_map[rep, layer] // 2 > section_map[rep, layer - 1] // 2
    arriving, leaving = Copies(sems), Copies(out_sems)
    arriving.either(moved, came_ref, kept_ref, stage)
    arriving.wait()
    for i in range(out_ref.shape[0]):
        leaving.start(stage, out_ref.at[i])
    leaving.wait()


def carve_kernel(chips, ids, act_mine, act_sib, x_mine, x_sib, *refs):
    outs, sems = refs[:chips], refs[chips]
    chip, core = ids[CHIP], ids[CORE]
    width = act_mine.shape[-1]
    copies = []
    for k, (act, x) in enumerate(((act_mine, x_mine), (act_sib, x_sib))):
        at = core if k == 0 else 1 - core
        for far, out in enumerate(outs):
            to = lax.rem(chip + far, chips)
            for j, source in enumerate((act, x.at[to])):
                target = out.at[at, :, pl.ds(j * width, width)]
                copies.append(pltpu.make_async_copy(source, target, sems.at[k, far, j]))
                copies[-1].start()
    for copy in copies:
        copy.wait()


def pick_kernel(wanted, of_slots, deps, ids, section_map, *refs):
    chips = 4
    count = len(wanted)
    total = (2 if of_slots else count) * chips
    sources, (own_out, sib_out, rep_out, block, in_sems, sems) = refs[:total], refs[total + deps :]
    core, rep = ids[CORE], ids[REP]
    width = 2 * sib_out.shape[-1] - rep_out.shape[-1]
    span = rep_out.shape[-1] - sib_out.shape[-1]
    for n, layer in enumerate(wanted):
        section_core, slot, far = held_at(ids, section_map, layer)
        at = slot * chips + far if of_slots else n * chips + far
        for j in range(total) if of_slots else range(n * chips, (n + 1) * chips):

            def begin(n=n, j=j, section_core=section_core):
                source = sources[j].at[section_core] if of_slots else sources[j]
                pltpu.make_async_copy(source, block.at[n], in_sems.at[n]).start()

            pl.when(at == j)(begin)
    plan = ((own_out, [(rep, core)]), (sib_out, [(rep, 1 - core)]), (rep_out, [(1 - rep, core), (1 - rep, 1 - core)]))
    leaving = Copies(sems)
    for n in range(count):
        pltpu.make_async_copy(block.at[n], block.at[n], in_sems.at[n]).wait()
        for out, pieces in plan:
            leaving.start(block.at[n, :, pl.ds(0, width)], out.at[n, :, pl.ds(0, width)])
            for j, (replica, side) in enumerate(pieces):
                columns = pl.ds(pl.multiple_of(width + (replica * 2 + side) * span, span), span)
                leaving.start(block.at[n, :, columns], out.at[n, :, pl.ds(width + j * span, span)])
    leaving.wait()


def halves_kernel(starts, *refs):
    parts, (out_ref, sems) = refs[:4], refs[4:]
    arriving = Copies(sems)
    for k in range(4):
        arriving.start(parts[k].at[:, :, pl.ds(starts[k], out_ref.shape[-1])], out_ref.at[k])
    arriving.wait()


def gradient_kernel(whole, ids, *refs):
    value_ref, out_ref = refs[-2:]
    width = value_ref.shape[-1]
    first_side = ids[SIDE] == 0

    def factors(parts, mine=None, theirs=None):
        wide = jnp.concatenate([part[0][:, :width] for part in parts], axis=0)
        if mine is None:
            span = parts[0].shape[-1] - width
            starts = (width, width, width, width + span)
            return jnp.concatenate([p[0][:, i : i + span] for p, i in zip(parts, starts)], axis=0), wide
        mine, theirs = (jnp.concatenate([ref[k, 0] for k in range(4)], axis=0) for ref in (mine, theirs))
        left = jnp.where(first_side, mine, theirs)
        right = jnp.where(first_side, theirs, mine)
        return jnp.concatenate([left, right], axis=1), wide

    x, act = factors(refs[0:4], refs[4], refs[5])
    g, head = factors(refs[6:10]) if whole else factors(refs[6:10], refs[10], refs[11])
    value_ref[0] = lax.dot_general(x, head, TN, preferred_element_type=F32).astype(BF16)
    out_ref[0] = lax.dot_general(g, act, TN, preferred_element_type=F32).astype(BF16)


def gradients(ids, layers, first, count, forward, backward, before, after=None):
    quarter = forward[4].shape[-1]
    piece, width = 2 * quarter, forward[0].shape[-1] - quarter
    out = jax.ShapeDtypeStruct((layers, piece, width), BF16)
    out_spec = pl.BlockSpec((1, piece, width), lambda l: (first + l, 0, 0))

    def block(array, start):
        if array.ndim == 3:
            return pl.BlockSpec((1,) + array.shape[1:], lambda l: (start + l, 0, 0))
        return pl.BlockSpec((array.shape[0], 1) + array.shape[2:], lambda l: (0, start + l, 0, 0))

    specs = [SMEM] + [block(a, first) for a in forward] + [block(a, 0) for a in backward]
    operands = [ids] + list(forward) + list(backward)
    aliases = {}
    if before is not None:
        aliases = {len(operands): 0, len(operands) + 1: 1}
        operands, specs = operands + list(before), specs + [ANY, ANY]
    if after is not None:
        operands, specs = operands + [after], specs + [ANY]
    return pl.pallas_call(
        functools.partial(gradient_kernel, len(backward) == 4),
        out_shape=(out, out),
        grid=(count,),
        in_specs=specs,
        out_specs=(out_spec, out_spec),
        input_output_aliases=aliases,
        compiler_params=pltpu.CompilerParams(vmem_limit_bytes=VMEM_BYTES),
        cost_estimate=pl.CostEstimate(
            flops=count * 4 * piece * width * 256, bytes_accessed=count * 2400000, transcendentals=0
        ),
    )(*operands)


def per_device(section_map, checkpoint, top_grad, value_weight, out_weight):
    tp_total = lax.axis_size("tp")
    section_total = lax.axis_size("section")
    replica_total = lax.axis_size("rep")
    chips = section_total // 2
    rep, section, tp = (lax.axis_index(name) for name in ("rep", "section", "tp"))
    chip, core, side = section // 2, section % 2, tp % 2
    layers = section_map.shape[1]
    _, _, micro, tokens, model = checkpoint.shape
    slots, width = value_weight.shape[1], value_weight.shape[3]
    rows = micro * tokens
    cut = model // tp_total
    piece = model // (replica_total * section_total)
    v_own, o_own = value_weight[0], out_weight[0]
    x_pair, top_pair = checkpoint[0, 0], top_grad[0]

    ids = jnp.stack([rep, chip, core, side, tp]).astype(jnp.int32)

    chip_of = section_map // 2
    moves = chip_of[:, 1:] - chip_of[:, :-1]
    most_moves = jnp.max(moves, axis=0)

    swap = [(i, i ^ 1) for i in range(section_total)]

    def to_sibling(array):
        return lax.ppermute(array, "section", swap)

    def to_replica(array):
        return lax.ppermute(array, "rep", [(0, 1), (1, 0)])

    o_sib, v_sib = to_sibling(o_own), to_sibling(v_own)

    def shape(*dims, dtype=BF16):
        return jax.ShapeDtypeStruct(dims, dtype)

    def in_hbm(*dims):
        return pltpu.HBM(dims, BF16)

    def dma(*dims):
        return pltpu.SemaphoreType.DMA(dims)

    weight_bytes = model * width * 2
    weight_buffer = pltpu.VMEM((model, width), BF16)

    def reduce_slices(got, base, spread, *deps):
        count = got.shape[1]
        buffer = pltpu.VMEM((count, cut), BF16)
        return run(
            functools.partial(reduce_kernel, spread, len(deps)),
            (ids, got, base, *deps),
            [SMEM] + [ANY] * (2 + len(deps)),
            in_hbm(*got.shape) if spread else in_hbm(count, cut),
            HBM,
            [pltpu.VMEM(got.shape, BF16), buffer, buffer, dma(5), dma(tp_total if spread else 1)],
            got.size * 2,
        )

    def over_tp(parts):
        return lax.all_to_all(parts, "tp", 0, 0, tiled=True)

    def recompute_slot(slot, x, with_parts, deps=()):
        halves = (shape(tokens, width),) * 2 + (shape(tokens, width, dtype=F32),) * 2
        halves += (shape(chips, tokens, cut),) * 2
        outs = ((in_hbm(tp_total, rows, cut),) if with_parts else ()) + halves
        out_specs = ((HBM,) if with_parts else ()) + (VMEM,) * 6
        scratch = [pltpu.VMEM((tp_total, rows, cut), BF16), weight_buffer]
        scratch += [pltpu.VMEM((rows, width), BF16), pltpu.VMEM((rows, width), F32), dma(tp_total + 4), dma(2)]
        if with_parts:
            scratch += [weight_buffer, pltpu.VMEM((tp_total, rows, cut), BF16)]
        operands = (ids, x, v_own) + ((o_own,) if with_parts else ()) + tuple(deps)
        count = 2 if with_parts else 1
        return run(
            functools.partial(recompute, chips, with_parts, slot, len(deps)),
            operands,
            [SMEM] + [ANY] * (len(operands) - 1),
            outs,
            out_specs,
            scratch,
            count * weight_bytes,
            count * 2 * rows * model * width,
        )

    def along_chips(cuts):
        got = [cuts[0]]
        for far in range(1, chips):
            back = chips - far
            route = [(i, (i + 2 * back) % section_total) for i in range(section_total)]
            got.append(lax.ppermute(cuts[back], "section", route))
        return got

    def carve(act_mine, act_sib, x_mine, x_sib):
        block = in_hbm(2, tokens, width + cut)
        return run(
            functools.partial(carve_kernel, chips),
            (ids, act_mine, act_sib, x_mine, x_sib),
            [SMEM] + [VMEM] * 4,
            (block,) * chips,
            (HBM,) * chips,
            [dma(2, chips, 2)],
            2 * chips * tokens * (width + cut) * 4,
        )

    def to_owners(sources, wanted, of_slots, deps=(), later=None):
        count = len(wanted)
        columns = sources[0].shape[-1]
        span = (columns - width) // 4
        alone, both = in_hbm(count, tokens, width + span), in_hbm(count, tokens, width + 2 * span)
        own_out, sib_out, rep_out = run(
            functools.partial(pick_kernel, wanted, of_slots, len(deps)),
            (ids, section_map, *sources, *deps),
            [SMEM, SMEM] + [ANY] * (len(sources) + len(deps)),
            (alone, alone, both),
            (HBM,) * 3,
            [pltpu.VMEM((count, tokens, columns), BF16), dma(count), dma(7 * count)],
            count * tokens * columns * 6,
        )
        from_rep, from_sib = to_replica(rep_out), to_sibling(sib_out)
        if later is not None:
            from_rep, later = lax.optimization_barrier((from_rep, later(from_sib)))
        parts = (own_out, from_sib, from_rep, to_sibling(from_rep))
        if span == piece:
            return parts, later
        mine = run(
            functools.partial(halves_kernel, (width, width, width, width + span)),
            parts,
            [ANY] * 4,
            shape(4, count, tokens, span),
            VMEM,
            [dma(4)],
            16 * count * tokens * span,
        )
        theirs = lax.ppermute(mine, "tp", [(i, i ^ 1) for i in range(tp_total)])
        return parts + (mine, theirs)

    x_rows = x_pair.reshape(rows, model)
    parts, act_mine_0, act_other_0, slope_mine_0, slope_other_0, x_mine_0, x_other_0 = recompute_slot(0, x_rows, True)
    act_sib_0, slope_sib_0, x_sib_0 = to_sibling(act_other_0), to_sibling(slope_other_0), to_sibling(x_other_0)
    first_cuts = carve(act_mine_0, act_sib_0, x_mine_0, x_sib_0)
    first_got = along_chips(first_cuts)
    x_second = over_tp(reduce_slices(over_tp(parts), x_rows, True))
    act_mine_1, act_other_1, slope_mine_1, slope_other_1, x_mine_1, x_other_1 = recompute_slot(
        1, x_second, False, first_cuts
    )
    slope_sib_1, act_sib_1, x_sib_1 = to_sibling(slope_other_1), to_sibling(act_other_1), to_sibling(x_other_1)
    second_cuts = carve(act_mine_1, act_sib_1, x_mine_1, x_sib_1)
    second_got = along_chips(second_cuts)
    slopes = (slope_mine_0, slope_mine_1, slope_sib_0, slope_sib_1)

    down = [(i, i - 2) for i in range(2, section_total)]
    earlier, latest = [2, 3, 4, 5, 6, 7], [0, 1]

    def one_layer(layer, g, deps):
        last = layer == 0
        operands = (ids, section_map, g, *slopes, o_own, o_sib)
        operands += (() if last else (v_own, v_sib)) + tuple(deps)
        columns = width + (2 * cut if layer in latest else cut)
        block = in_hbm(tokens, columns)
        outs = (() if last else (in_hbm(tp_total, tokens, cut),)) + (block,) * chips
        scratch = [pltpu.VMEM((tp_total, tokens, cut), BF16), pltpu.VMEM((tokens, width), F32), weight_buffer]
        scratch += [pltpu.VMEM((chips, tokens, columns), BF16), dma(tp_total + 5), dma(chips + 2)]
        if not last:
            scratch += [weight_buffer, pltpu.VMEM((tp_total, tokens, cut), BF16)]
        count = 1 if last else 2
        result = run(
            functools.partial(step, chips, layer, len(deps)),
            operands,
            [SMEM, SMEM] + [ANY] * (len(operands) - 2),
            outs,
            (HBM,) * len(outs),
            scratch,
            count * weight_bytes,
            count * 2 * tokens * model * width,
        )
        return (None if last else result[0]), along_chips(result[-chips:])

    g = top_pair
    got_at = [None] * layers
    deps = {layer: [] for layer in range(layers)}

    def collect(wanted, deps=(), later=None):
        return to_owners([array for layer in wanted for array in got_at[layer]], wanted, False, deps, later)

    for layer in reversed(range(layers)):
        if layer == 7:
            deps[7] += first_got
        if layer == 6:
            deps[6] += list(second_cuts) + got_at[7][2:3]
        if layer == 5:
            deps[5] += second_got[1::2]
        if layer == 4:
            deps[4] += second_got[2:3] + got_at[6][2:3]
        if layer == 3:
            deps[3] += list(forward[:1])
        if layer == 2:
            deps[2] += got_at[3][2:3]
        if layer == 1:
            deps[1] += list(forward[:4])
        if layer == 0:
            deps[0] += got_at[1][2:3] + list(earlier_all[:4])
        parts, got_at[layer] = one_layer(layer, g, deps[layer])
        if layer == 0:
            break
        got = over_tp(parts)
        most = most_moves[layer - 1]

        def stay(*operands):
            return reduce_slices(*operands[:2], True, *operands[2:])

        def settle(kept, came, layer=layer):
            return run(
                functools.partial(settle_kernel, layer),
                (ids, section_map, kept, came),
                [SMEM, SMEM, ANY, ANY],
                in_hbm(tp_total, tokens, cut),
                HBM,
                [pltpu.VMEM((tokens, cut), BF16), dma(1), dma(tp_total)],
                tp_total * tokens * cut * 2,
            )

        def go_one(*operands):
            mine = reduce_slices(*operands[:2], False, *operands[2:])
            return settle(mine, lax.ppermute(mine, "section", down))

        def go_far(*operands, layer=layer, most=most):
            mine = reduce_slices(*operands[:2], False, *operands[2:])
            my_move = lax.dynamic_index_in_dim(moves, rep, 0, keepdims=False)[layer - 1]

            def hop(i, value):
                came = lax.ppermute(value, "section", down)
                return jnp.where(i < my_move, came, value)

            mine = lax.fori_loop(0, most, hop, mine)
            return settle(mine, mine)

        near = got_at[layer][1:]
        spread = lax.switch(jnp.minimum(most, 2), (stay, go_one, go_far), got, g, *near)
        g = over_tp(spread)
        if layer == 4:
            forward = to_owners(first_got + second_got, list(range(layers)), True, (spread,))
        if layer == 2:
            earlier_all = collect(earlier, (spread,))

    def earlier_gradients(after):
        return gradients(ids, layers, earlier[0], len(earlier), forward, earlier_all, None, after)

    latest_all, result = collect(latest, (), earlier_gradients)
    return gradients(ids, layers, latest[0], len(latest), forward, latest_all, result)


def solution(mesh):
    placed = (
        P(),
        P("rep", "section", None, None, None),
        P("rep", None, None, None),
        P("rep", "section", None, "tp"),
        P("rep", "section", None, "tp"),
    )
    return jax.shard_map(
        per_device,
        mesh=mesh,
        in_specs=placed,
        out_specs=(P(None, ("rep", "section"), "tp"), P(None, ("rep", "section"), "tp")),
        check_vma=False,
    )
```
